32 devices in a mesh: gx: 2 (over y), gy: 4 (over z), gz: 4 (over x, core).
Axes of the slice: x: 2, y: 2, z: 4, core: 2. Of those that a mesh axis runs over, the one named last changes fastest.
Arguments:
- adjoint: float32 [1024, 1715], P(('gx', 'gy', 'gz')), may hold values from -6 to 6
- order: int32 [1024], P(('gx', 'gy', 'gz')), may hold values from 2 to 6
- mortar_trace: float32 [3072, 245], P(('gx', 'gy', 'gz')), may hold values from -6 to 6
- mortar_sub: int32 [3072], P(('gx', 'gy', 'gz')), may hold values from 0 to 3
- mortar_dest: int32 [3072, 1], P(('gx', 'gy', 'gz')), may hold values from 0 to 7; in each aligned block of 96 rows (0 to 95, 96 to 191, ...) at most 24 rows name the same one
- mortar_elem: int32 [3072], P(('gx', 'gy', 'gz')), may hold values from 0 to 31
- mortar_face: int32 [3072], P(('gx', 'gy', 'gz')), may hold values from 0 to 5
- conf_trace: float32 [2048, 245], P(('gx', 'gy', 'gz')), may hold values from -6 to 6
- conf_elem: int32 [2048], P(('gx', 'gy', 'gz')), may hold values from 0 to 31
- conf_face: int32 [2048], P(('gx', 'gy', 'gz')), may hold values from 0 to 5
- coarse_row: int32 [1024], P(('gx', 'gy', 'gz')), may hold values from 0 to 255, as said below
Outputs:
- coarse_rows: float32 [1024, 1080], P(('gx', 'gy', 'gz'))
The draws below stay inside these ranges and needn't reach their ends.
Inputs may be any that keep to these rules, and one draw needn't show every extreme that they name: `mortar_dest`: in each aligned block of 96 rows (one device) no value appears more than 24 times. `coarse_row`: within each gz layer the values of all its devices form a permutation; each device sends either exactly 4 or no rows to each device of its layer.
All inputs are finite; a program needn't handle non-finite values.
Results may differ from the reference program's by a relative error of at most 0.0003.
Values sent between devices are 32-bit elements; how exact they have to be, the bound alone decides.
No kernel may reach another device: no remote copies, remote signals or barrier semaphores. Data moves between devices by JAX's collectives and lax.ppermute only.
A program may use at most 192 MiB of HBM per device.

```python
import math
import jax
import jax.numpy as jnp
import numpy as np
from jax import lax

VARS = 5
NODES = 343
FACE = 49
EL_DEV = 32
MORT_DEV = 96
CONF_DEV = 64
MCAP = 24
RCAP = 4
ELEMS = 1024
MORTARS = 3072
CONFS = 2048
N_GX = 2
N_GY = 4
N_GZ = 4


def draw_coarse_row(key, part):
    key = jax.random.fold_in(key, 11)
    layer_count = N_GX * N_GY
    bins = EL_DEV // RCAP
    layer_keys = jax.random.split(jax.random.fold_in(key, 1), N_GZ)
    orders = jax.vmap(lambda single: jax.random.permutation(single, layer_count))(layer_keys).astype(jnp.int32)
    shifts = (orders[:, :bins] - orders[:, :1] + layer_count // 2) % layer_count
    device_keys = jax.random.split(jax.random.fold_in(key, 2), layer_count * N_GZ)
    shuffled = jax.vmap(lambda single: jax.random.permutation(single, EL_DEV))(device_keys)
    shuffled = shuffled.reshape(layer_count, N_GZ, EL_DEV).astype(jnp.int32)
    within = jnp.arange(layer_count, dtype=jnp.int32)[:, None, None]
    layers = jnp.broadcast_to(jnp.arange(N_GZ, dtype=jnp.int32)[None, :, None], shuffled.shape)
    bin_index = shuffled // RCAP
    position = shuffled % RCAP
    offset = shifts.astype(jnp.int32)[layers, bin_index]
    target = (within + offset) % layer_count
    return (target * EL_DEV + bin_index * RCAP + position).reshape(-1).astype(jnp.int32)


def touch_ends(array, rng, smallest, top_value):
    longest = array.shape.index(max(array.shape))
    spots = []
    for shift in (0, 1):
        where = [jax.random.randint(jax.random.fold_in(rng, axis), (), 0, length) for axis, length in enumerate(array.shape)]
        where[longest] = (where[longest] + shift) % array.shape[longest]
        spots.append(tuple(where))
    return array.at[spots[0]].set(smallest).at[spots[1]].set(top_value)


def levels(own_key, shape, cuts, least, largest):
    level, own = 1.0, jax.random.fold_in(own_key, 6)
    for dim, shards_of in cuts:
        heights = jnp.exp(jax.random.uniform(jax.random.fold_in(own, dim), (shards_of,), jnp.float32, least / len(cuts), largest / len(cuts)))
        level = level * jnp.repeat(heights, shape[dim] // shards_of).reshape([-1 if axis == dim else 1 for axis in range(len(shape))])
    return level


def assign_block(rng, own, number, rows, amount, top, most, skew):
    order = jax.random.permutation(rng, amount)
    packed, ordinary = portions_of(amount, rows * top, most, skew, True), portions_of(amount, rows * top, most, skew, False)
    places = jnp.arange(amount)

    def named(sizes, rotation):
        used = int((sizes > 0).sum())
        fixed = max(1, used // 4)
        passed = fixed + (places - fixed + rotation * (used - fixed)) % max(1, amount - fixed)
        return jnp.zeros((amount,), jnp.int32).at[order[jnp.where(places < fixed, places, passed)]].set(jnp.asarray(sizes, jnp.int32))

    sizes = jnp.where(number % 4 == 0, named(packed, number // 4), named(ordinary, number - number // 4 - 1))
    mixed = jax.random.permutation(jax.random.fold_in(own, 3), amount)
    source_of, taker = mixed[0:amount // 2 * 2:2], mixed[1:amount // 2 * 2:2]
    margin = jnp.minimum(sizes[source_of] - 1, most - sizes[taker]) // 2
    margin = jnp.where((source_of == order[0]) | (taker == order[0]) | (sizes[taker] == 0), 0, jnp.maximum(margin, 0))
    passed = jax.random.randint(jax.random.fold_in(own, 4), (amount // 2,), 0, 1 << 20) % (margin + 1)
    sizes = sizes.at[source_of].add(-passed).at[taker].add(passed)
    members = jnp.searchsorted(jnp.cumsum(sizes), jnp.arange(rows * top), side="right").astype(jnp.int32)
    listing = members.reshape(top, rows).T
    listing = listing[jax.random.permutation(jax.random.fold_in(own, 1), rows)]
    rotation = jax.random.randint(jax.random.fold_in(own, 2), (rows, 1), 0, top)
    return jnp.take_along_axis(listing, (jnp.arange(top)[None, :] + rotation) % top, axis=1)


def portions_of(amount, total, bound, slope, full):
    loads = [(1 << 20) // math.isqrt(rank ** slope) + 1 for rank in range(1, amount + 1)]
    largest = bound if full else min(bound, max(-(-total // amount), total * loads[0] // sum(loads)))
    least = 1 if total - largest >= amount - 1 else 0
    holding, rest = [largest] + [least] * (amount - 1), total - largest - least * (amount - 1)
    while rest > 0:
        movable = [i for i in range(1, amount) if holding[i] < largest] or [i for i in range(1, amount) if holding[i] < bound]
        pool, budget = sum([loads[i] for i in movable]), rest
        for i in movable:
            extra = min(bound - holding[i], max(1, budget * loads[i] // pool), rest)
            holding[i] = holding[i] + extra
            rest = rest - extra
    return np.array(holding)


def bell_draw(stream_key, dims, scale, bound, cuts=(), kind=jnp.bfloat16):
    result = scale * jax.random.normal(stream_key, dims, jnp.float32)
    if cuts:
        result = result * levels(stream_key, dims, cuts, -0.22, 0.18)
    return jnp.clip(result, -bound, bound).astype(kind)


def setup_inputs(seed: int = 0) -> dict:
    seeds = jax.random.split(jax.random.key(seed), 12)
    adjoint = bell_draw(seeds[0], (ELEMS, VARS * NODES), 1.0, 6.0, ((0, 32),), jnp.float32)
    order = touch_ends(jax.random.randint(seeds[1], (ELEMS,), 2, 7), jax.random.fold_in(seeds[1], 1), 2, 6).astype(jnp.int32)
    mortar_trace = bell_draw(seeds[2], (MORTARS, VARS * FACE), 1.0, 6.0, ((0, 32),), jnp.float32)
    mortar_sub = touch_ends(jax.random.randint(seeds[3], (MORTARS,), 0, 4), jax.random.fold_in(seeds[3], 1), 0, 3).astype(jnp.int32)
    mortar_dest_keys = jax.random.split(jax.random.fold_in(seeds[4], 1), MORTARS // MORT_DEV)
    mortar_dest_turns = jax.random.permutation(jax.random.fold_in(seeds[4], 3), MORTARS // MORT_DEV)
    mortar_dest = jax.vmap(lambda own, number: assign_block(jax.random.fold_in(seeds[4], 2), own, number, MORT_DEV, N_GX * N_GY, 1, MCAP, 2))(mortar_dest_keys, mortar_dest_turns).reshape((MORTARS, 1))
    mortar_elem = touch_ends(jax.random.randint(seeds[5], (MORTARS,), 0, EL_DEV), jax.random.fold_in(seeds[5], 1), 0, EL_DEV - 1).astype(jnp.int32)
    mortar_face = touch_ends(jax.random.randint(seeds[6], (MORTARS,), 0, 6), jax.random.fold_in(seeds[6], 1), 0, 5).astype(jnp.int32)
    conf_trace = bell_draw(seeds[7], (CONFS, VARS * FACE), 1.0, 6.0, ((0, 32),), jnp.float32)
    conf_elem = touch_ends(jax.random.randint(seeds[8], (CONFS,), 0, EL_DEV), jax.random.fold_in(seeds[8], 1), 0, EL_DEV - 1).astype(jnp.int32)
    conf_face = touch_ends(jax.random.randint(seeds[9], (CONFS,), 0, 6), jax.random.fold_in(seeds[9], 1), 0, 5).astype(jnp.int32)
    coarse_row = draw_coarse_row(jax.random.fold_in(seeds[11], 71), 0)
    return {"adjoint": adjoint, "order": order, "mortar_trace": mortar_trace, "mortar_sub": mortar_sub, "mortar_dest": mortar_dest, "mortar_elem": mortar_elem, "mortar_face": mortar_face, "conf_trace": conf_trace, "conf_elem": conf_elem, "conf_face": conf_face, "coarse_row": coarse_row}


HIGH = lax.Precision.HIGHEST


def grid_nodes(degree):
    return -np.cos(np.pi * np.arange(degree + 1) / degree)


def lagrange_rows(degree, points):
    anchors = grid_nodes(degree)
    values = np.ones((len(points), degree + 1))
    for k in range(degree + 1):
        for other in range(degree + 1):
            if other != k:
                values[:, k] *= (points - anchors[other]) / (anchors[k] - anchors[other])
    return values


def basis_tables():
    lift = np.zeros((5, 7, 7))
    shrink = np.zeros((5, 6, 7))
    active = np.zeros((5, 7))
    top_nodes = grid_nodes(6)
    for index, degree in enumerate(range(2, 7)):
        lift[index, :degree + 1, :] = lagrange_rows(degree, top_nodes).T
        shrink[index, :degree, :degree + 1] = lagrange_rows(degree - 1, grid_nodes(degree)).T
        active[index, :degree + 1] = 1.0
    mortar = np.stack([lagrange_rows(6, (top_nodes - 1.0) / 2.0), lagrange_rows(6, (top_nodes + 1.0) / 2.0)])
    return (jnp.asarray(lift, jnp.float32), jnp.asarray(shrink, jnp.float32),
            jnp.asarray(active, jnp.float32), jnp.asarray(mortar, jnp.float32))


def project_mortars(trace, sub):
    tables = basis_tables()
    mortar = tables[3]
    count = trace.shape[0]
    field = trace.reshape(count, 5, 7, 7)
    first = jnp.where((sub // 2)[:, None, None] == 0, mortar[0], mortar[1])
    second = jnp.where((sub % 2)[:, None, None] == 0, mortar[0], mortar[1])
    partial_lift = jnp.einsum('mia,mvij->mvaj', first, field, precision=HIGH)
    lifted = jnp.einsum('mjb,mvaj->mvab', second, partial_lift, precision=HIGH)
    return lifted.reshape(count, 245)


def order_onehot(order):
    return (order[:, None] == jnp.arange(2, 7, dtype=jnp.int32)[None, :]).astype(jnp.float32)


def add_faces(adjoint, face_sum, order):
    lift, shrink, active, mortar = basis_tables()
    count = adjoint.shape[0]
    onehot = order_onehot(order)
    lift_el = jnp.einsum('eo,oai->eai', onehot, lift, precision=HIGH)
    mask_el = jnp.einsum('eo,oa->ea', onehot, active, precision=HIGH)
    field = adjoint.reshape(count, 5, 7, 7, 7)
    field = field * mask_el[:, None, :, None, None] * mask_el[:, None, None, :, None] * mask_el[:, None, None, None, :]
    faces = face_sum.reshape(count, 6, 5, 7, 7)
    faces = jnp.einsum('eai,efvij->efvaj', lift_el, faces, precision=HIGH)
    faces = jnp.einsum('ebj,efvaj->efvab', lift_el, faces, precision=HIGH)
    low = (jnp.arange(7) == 0).astype(jnp.float32)
    high = (jnp.arange(7)[None, :] == order[:, None]).astype(jnp.float32)
    field = field + low[None, None, :, None, None] * faces[:, 0][:, :, None, :, :]
    field = field + high[:, None, :, None, None] * faces[:, 1][:, :, None, :, :]
    field = field + low[None, None, None, :, None] * faces[:, 2][:, :, :, None, :]
    field = field + high[:, None, None, :, None] * faces[:, 3][:, :, :, None, :]
    field = field + low[None, None, None, None, :] * faces[:, 4][:, :, :, :, None]
    field = field + high[:, None, None, None, :] * faces[:, 5][:, :, :, :, None]
    return field


def restrict(field, order):
    lift, shrink, active, mortar = basis_tables()
    count = field.shape[0]
    shrink_el = jnp.einsum('eo,oai->eai', order_onehot(order), shrink, precision=HIGH)
    section = jnp.einsum('eai,evijk->evajk', shrink_el, field, precision=HIGH)
    section = jnp.einsum('ebj,evajk->evabk', shrink_el, section, precision=HIGH)
    section = jnp.einsum('eck,evabk->evabc', shrink_el, section, precision=HIGH)
    return section.reshape(count, 1080)


def reference(adjoint, order, mortar_trace, mortar_sub, mortar_dest, mortar_elem, mortar_face, conf_trace, conf_elem, conf_face, coarse_row):
    devices = N_GX * N_GY * N_GZ
    lifted = project_mortars(mortar_trace, mortar_sub)
    mortar_dev = jnp.arange(MORTARS, dtype=jnp.int32) // MORT_DEV
    mortar_target = ((mortar_dest[:, 0] * N_GZ + mortar_dev % N_GZ) * EL_DEV + mortar_elem) * 6 + mortar_face
    conf_dev = jnp.arange(CONFS, dtype=jnp.int32) // CONF_DEV
    conf_owner = (conf_dev // N_GZ) * N_GZ + (conf_dev % N_GZ + 1) % N_GZ
    conf_target = (conf_owner * EL_DEV + conf_elem) * 6 + conf_face
    face_sum = jnp.zeros((ELEMS * 6, 245), jnp.float32)
    face_sum = face_sum.at[mortar_target].add(lifted).at[conf_target].add(conf_trace)

    def per_device(block):
        fine = add_faces(block[0], block[1], block[2])
        return restrict(fine, block[2])

    restricted = lax.map(per_device, (adjoint.reshape(devices, EL_DEV, 5 * 343),
                                      face_sum.reshape(devices, EL_DEV * 6, 245),
                                      order.reshape(devices, EL_DEV)))
    restricted = restricted.reshape(ELEMS, 1080)
    elem_dev = jnp.arange(ELEMS, dtype=jnp.int32) // EL_DEV
    placed = ((coarse_row // EL_DEV) * N_GZ + elem_dev % N_GZ) * EL_DEV + coarse_row % EL_DEV
    return jnp.zeros((ELEMS, 1080), jnp.float32).at[placed].set(restricted)
```

```python
import functools

import jax
import jax.numpy as jnp
import ml_dtypes
import numpy as np
from jax import lax
from jax.experimental import pallas as pl
from jax.experimental.pallas import tpu as pltpu
from jax.sharding import PartitionSpec as P

VARS = 5
NODE = 7
FACE = NODE * NODE
CELL = NODE * FACE
ROW = 216
FACES = 6
ORDERS = (2, 3, 4, 5, 6)
TRACE = VARS * FACE
LANES = 256
TAG_FACE = TRACE
TAG_ROW = TRACE + 1
CELL_PAD = 384
FACE_PAD = 64


def grid_nodes(degree):
    return -np.cos(np.pi * np.arange(degree + 1) / degree)


def lagrange_rows(degree, points):
    anchors = grid_nodes(degree)
    values = np.ones((len(points), degree + 1))
    for k in range(degree + 1):
        for other in range(degree + 1):
            if other != k:
                values[:, k] *= (points - anchors[other]) / (anchors[k] - anchors[other])
    return values


def split_table(table):
    table = np.asarray(table, np.float32)
    high = table.astype(ml_dtypes.bfloat16)
    low = (table - high.astype(np.float32)).astype(ml_dtypes.bfloat16)
    return high, low


@functools.lru_cache(maxsize=None)
def basis_tables():
    top_nodes = grid_nodes(6)
    mortar = [lagrange_rows(6, (top_nodes - 1.0) / 2.0), lagrange_rows(6, (top_nodes + 1.0) / 2.0)]
    lift = np.zeros((4, LANES, LANES))
    for sub in range(4):
        both = np.kron(mortar[sub // 2], mortar[sub % 2])
        for v in range(VARS):
            part = slice(v * FACE, (v + 1) * FACE)
            lift[sub, part, part] = both
    cell = np.zeros((len(ORDERS), CELL_PAD, ROW))
    face = np.zeros((len(ORDERS), FACES, FACE_PAD, ROW))
    for index, p in enumerate(ORDERS):
        shrink = np.zeros((6, NODE))
        shrink[:p, : p + 1] = lagrange_rows(p - 1, grid_nodes(p)).T
        reduce = np.zeros((NODE, NODE))
        reduce[: p + 1, :] = lagrange_rows(p, top_nodes).T
        cell[index, :CELL] = np.einsum("ai,bj,ck->ijkabc", shrink, shrink, shrink).reshape(CELL, ROW)
        flat = shrink @ reduce
        low, high = shrink[:, 0], shrink[:, p]
        for axis, spec in enumerate(("c,ai,bj->ijcab", "c,ai,bj->ijacb", "c,ai,bj->ijabc")):
            for side, edge in enumerate((low, high)):
                face[index, 2 * axis + side, :FACE] = np.einsum(spec, edge, flat, flat).reshape(FACE, ROW)
    return (
        split_table(lift.reshape(4 * LANES, LANES)),
        split_table(cell.reshape(-1, ROW)),
        split_table(face.reshape(-1, ROW)),
    )


def iota(shape, axis):
    return lax.broadcasted_iota(jnp.int32, shape, axis)


def halves(x):
    high = x.astype(jnp.bfloat16)
    low = (x - high.astype(jnp.float32)).astype(jnp.bfloat16)
    return high, low


def dot(a, b):
    return jnp.dot(a, b, preferred_element_type=jnp.float32)


def dot3(high, low, table_high, table_low):
    return dot(high, table_high) + dot(low, table_high) + dot(high, table_low)


def earlier(member):
    count = member.shape[1]
    before = (iota((count, count), 0) < iota((count, count), 1)).astype(jnp.float32)
    return dot(member.astype(jnp.bfloat16), before.astype(jnp.bfloat16))


def owner_of(crow, peers, elements):
    first = iota((peers, crow.shape[1]), 0) * elements
    return ((crow >= first) & (crow < first + elements)).astype(jnp.float32)


def row_places(crow, peers, elements, stride):
    member = owner_of(crow, peers, elements)
    rank = earlier(member)
    base = iota(member.shape, 0).astype(jnp.float32)
    place = jnp.sum(member * (base * stride + rank), axis=0, keepdims=True)
    slot = crow.astype(jnp.float32) - jnp.sum(member * (base * elements), axis=0, keepdims=True)
    return place, slot


def onehot_rows(place, rows):
    return (iota((rows, place.shape[1]), 0).astype(jnp.float32) == place).astype(jnp.float32)


def column(onehot, values):
    return jnp.sum(onehot * values, axis=1, keepdims=True)


def pack_kernel(
    peers,
    cap,
    elements,
    trace,
    sub,
    dest,
    elem,
    face,
    crow,
    ctrace,
    celem,
    cface,
    lift_high,
    lift_low,
    out,
    conf_out,
):
    count = trace.shape[0]
    rows = peers * cap
    member = (iota((peers, count), 0) == dest[...]).astype(jnp.float32)
    base = iota(member.shape, 0).astype(jnp.float32) * cap
    place = jnp.sum(member * (base + earlier(member)), axis=0, keepdims=True)
    put = onehot_rows(place, rows)
    code = (face[...] * elements + elem[...] + 1).astype(jnp.float32)
    code_col = column(put, code)
    row_place, row_slot = row_places(crow[...], peers, elements, cap)
    row_col = column(onehot_rows(row_place, rows), row_slot + 1.0)
    eye = (iota((count, count), 0) == iota((count, count), 1)).astype(jnp.float32)
    sub_col = column(eye, sub[...].astype(jnp.float32))
    x = jnp.concatenate([trace[...], jnp.zeros((count, LANES - TRACE), jnp.float32)], axis=1)
    wide = jnp.concatenate([jnp.where(sub_col == float(s), x, 0.0) for s in range(4)], axis=1)
    high, low = halves(wide)
    lifted = dot3(high, low, lift_high[...], lift_low[...])
    lifted_high, lifted_low = halves(lifted)
    put = put.astype(jnp.bfloat16)
    packed = dot(put, lifted_high) + dot(put, lifted_low)
    lane = iota((rows, LANES), 1)
    packed = jnp.where(lane == TAG_FACE, code_col, packed)
    packed = jnp.where(lane == TAG_ROW, row_col, packed)
    out[...] = packed.reshape(peers, cap, LANES)
    confs = ctrace.shape[0]
    eye = (iota((confs, confs), 0) == iota((confs, confs), 1)).astype(jnp.float32)
    conf_col = column(eye, (cface[...] * elements + celem[...] + 1).astype(jnp.float32))
    c = jnp.concatenate([ctrace[...], jnp.zeros((confs, LANES - TRACE), jnp.float32)], axis=1)
    conf_out[...] = jnp.where(iota((confs, LANES), 1) == TAG_FACE, conf_col, c)


def cell_kernel(peers, row_cap, adjoint, order, crow, table_high, table_low, y_out, col_out, spread):
    elements = adjoint.shape[0]
    slots = peers * row_cap
    place, _ = row_places(crow[...], peers, elements, row_cap)
    take = onehot_rows(place, slots)
    order_col = column(take, order[...].astype(jnp.float32))
    elem_col = column(take, iota((1, elements), 1).astype(jnp.float32) + 1.0)
    lane = iota((slots, 128), 1)
    col_out[...] = jnp.where(lane == 0, order_col, jnp.where(lane == 1, elem_col, 0.0))
    take = take.astype(jnp.bfloat16)
    spread[...] = jnp.zeros_like(spread)
    for half, part in enumerate(halves(adjoint[...])):
        moved = dot(take, part)
        for v in range(VARS):
            spread[half, v * slots : (v + 1) * slots, :CELL] = moved[:, v * CELL : (v + 1) * CELL]
    order_rows = jnp.concatenate([order_col] * VARS, axis=0)
    high, low = spread[0], spread[1]
    wide_high = jnp.concatenate([jnp.where(order_rows == float(p), high, 0.0).astype(jnp.bfloat16) for p in ORDERS], axis=1)
    wide_low = jnp.concatenate([jnp.where(order_rows == float(p), low, 0.0).astype(jnp.bfloat16) for p in ORDERS], axis=1)
    y_out[...] = dot3(wide_high, wide_low, table_high[...], table_low[...])


def face_kernel(peers, row_cap, elements, incoming, conf, y, cols, table_high, table_low, out, spread):
    slots = peers * row_cap
    x = jnp.concatenate([incoming[...].reshape(-1, LANES), conf[...]], axis=0)
    count = x.shape[0]
    code_col = x[:, TAG_FACE : TAG_FACE + 1]
    code_row = jnp.sum(jnp.where(iota((count, count), 0) == iota((count, count), 1), code_col, 0.0), axis=0, keepdims=True)
    order_col, elem_col = cols[:, 0:1], cols[:, 1:2]
    wanted = jnp.concatenate([jnp.where(elem_col > 0.0, elem_col + float(f * elements), -1.0) for f in range(FACES)], axis=0)
    gather = (wanted == code_row).astype(jnp.bfloat16)
    high, low = halves(x)
    face_sum = dot(gather, high) + dot(gather, low)
    spread[...] = jnp.zeros_like(spread)
    for f in range(FACES):
        for v in range(VARS):
            spread[v * slots : (v + 1) * slots, f * FACE_PAD : f * FACE_PAD + FACE] = face_sum[
                f * slots : (f + 1) * slots, v * FACE : (v + 1) * FACE
            ]
    order_rows = jnp.concatenate([order_col] * VARS, axis=0)
    z = spread[...]
    wide = jnp.concatenate([jnp.where(order_rows == float(p), z, 0.0) for p in ORDERS], axis=1)
    high, low = halves(wide)
    total = y[...] + dot3(high, low, table_high[...], table_low[...])
    for v in range(VARS):
        out[:, :, v * ROW : (v + 1) * ROW] = total[v * slots : (v + 1) * slots].reshape(peers, row_cap, ROW)


def place_kernel(peers, row_cap, arrived, tags, out):
    elements = out.shape[0]
    rows = peers * row_cap
    x = arrived[...].reshape(rows, arrived.shape[2])
    slot_col = tags[:, :row_cap, TAG_ROW : TAG_ROW + 1].reshape(rows, 1)
    slot_row = jnp.sum(jnp.where(iota((rows, rows), 0) == iota((rows, rows), 1), slot_col, 0.0), axis=0, keepdims=True)
    put = (iota((elements, rows), 0).astype(jnp.float32) + 1.0 == slot_row).astype(jnp.bfloat16)
    high, low = halves(x)
    rest = (x - high.astype(jnp.float32) - low.astype(jnp.float32)).astype(jnp.bfloat16)
    out[...] = dot(put, high) + dot(put, low) + dot(put, rest)


def call(kernel, outs, *args, scratch=(), flops=0):
    sizes = [np.prod(a.shape) * a.dtype.itemsize for a in (*args, *jax.tree.leaves(outs))]
    return pl.pallas_call(
        kernel,
        out_shape=outs,
        scratch_shapes=scratch,
        compiler_params=pltpu.CompilerParams(vmem_limit_bytes=48 * 1024 * 1024),
        cost_estimate=pl.CostEstimate(flops=flops, bytes_accessed=int(sum(sizes)), transcendentals=0),
    )(*args)


def exchange(block):
    return lax.all_to_all(block, ("gx", "gy"), split_axis=0, concat_axis=0, tiled=True)


def from_behind(block, axis, distance):
    devices = range(lax.axis_size(axis))
    route = [((i - distance) % len(devices), i) for i in devices]
    return lax.ppermute(block, axis, route)


def body(
    adjoint,
    order,
    mortar_trace,
    mortar_sub,
    mortar_dest,
    mortar_elem,
    mortar_face,
    conf_trace,
    conf_elem,
    conf_face,
    coarse_row,
):
    elements = adjoint.shape[0]
    count = mortar_trace.shape[0]
    confs = conf_trace.shape[0]
    peers = lax.axis_size("gx") * lax.axis_size("gy")
    cap = max(2, 2 * count // peers)
    row_cap = max(2, elements // peers)
    slots = peers * row_cap
    assert row_cap <= cap
    lift, cell, face = [tuple(jnp.asarray(t) for t in pair) for pair in basis_tables()]
    f32 = jnp.float32
    line = lambda a: a.reshape(1, -1)
    order, coarse_row = line(order), line(coarse_row)
    outgoing, conf = call(
        functools.partial(pack_kernel, peers, cap, elements),
        (jax.ShapeDtypeStruct((peers, cap, LANES), f32), jax.ShapeDtypeStruct((confs, LANES), f32)),
        mortar_trace,
        line(mortar_sub),
        line(mortar_dest),
        line(mortar_elem),
        line(mortar_face),
        coarse_row,
        conf_trace,
        line(conf_elem),
        line(conf_face),
        *lift,
    )
    incoming = exchange(outgoing)
    conf = from_behind(conf, "gz", 1)
    y, cols = call(
        functools.partial(cell_kernel, peers, row_cap),
        (jax.ShapeDtypeStruct((VARS * slots, ROW), f32), jax.ShapeDtypeStruct((slots, 128), f32)),
        adjoint,
        order,
        coarse_row,
        *cell,
        scratch=[pltpu.VMEM((2, VARS * slots, CELL_PAD), f32)],
    )
    rows = call(
        functools.partial(face_kernel, peers, row_cap, elements),
        jax.ShapeDtypeStruct((peers, row_cap, VARS * ROW), f32),
        incoming,
        conf,
        y,
        cols,
        *face,
        scratch=[pltpu.VMEM((VARS * slots, FACES * FACE_PAD), f32)],
    )
    arrived = exchange(rows)
    return call(
        functools.partial(place_kernel, peers, row_cap),
        jax.ShapeDtypeStruct((elements, VARS * ROW), f32),
        arrived,
        incoming,
    )


def solution(mesh):
    rows = P(("gx", "gy", "gz"))
    wide = P(("gx", "gy", "gz"), None)
    return jax.shard_map(
        body,
        mesh=mesh,
        in_specs=(wide, rows, wide, rows, wide, rows, rows, wide, rows, rows, rows),
        out_specs=wide,
        check_vma=False,
    )
```

```python
import functools

import jax
import jax.numpy as jnp
import ml_dtypes
import numpy as np
from jax import lax
from jax.experimental import pallas as pl
from jax.experimental.pallas import tpu as pltpu
from jax.sharding import PartitionSpec as P

VARS = 5
NODE = 7
FACE = NODE * NODE
CELL = NODE * FACE
ROW = 216
FACES = 6
ORDERS = (2, 3, 4, 5, 6)
TRACE = VARS * FACE
LANES = 256
TAG_FACE = TRACE
TAG_ROW = TRACE + 1
CELL_PAD = 384
FACE_PAD = 64


def grid_nodes(degree):
    return -np.cos(np.pi * np.arange(degree + 1) / degree)


def lagrange_rows(degree, points):
    anchors = grid_nodes(degree)
    values = np.ones((len(points), degree + 1))
    for k in range(degree + 1):
        for other in range(degree + 1):
            if other != k:
                values[:, k] *= (points - anchors[other]) / (anchors[k] - anchors[other])
    return values


def split_table(table):
    table = np.asarray(table, np.float32)
    high = table.astype(ml_dtypes.bfloat16)
    low = (table - high.astype(np.float32)).astype(ml_dtypes.bfloat16)
    return high, low


@functools.lru_cache(maxsize=None)
def basis_tables():
    top_nodes = grid_nodes(6)
    mortar = [lagrange_rows(6, (top_nodes - 1.0) / 2.0), lagrange_rows(6, (top_nodes + 1.0) / 2.0)]
    lift = np.zeros((4, LANES, LANES))
    for sub in range(4):
        both = np.kron(mortar[sub // 2], mortar[sub % 2])
        for v in range(VARS):
            part = slice(v * FACE, (v + 1) * FACE)
            lift[sub, part, part] = both
    cell = np.zeros((len(ORDERS), CELL_PAD, ROW))
    face = np.zeros((len(ORDERS), FACES, FACE_PAD, ROW))
    for index, p in enumerate(ORDERS):
        shrink = np.zeros((6, NODE))
        shrink[:p, : p + 1] = lagrange_rows(p - 1, grid_nodes(p)).T
        reduce = np.zeros((NODE, NODE))
        reduce[: p + 1, :] = lagrange_rows(p, top_nodes).T
        cell[index, :CELL] = np.einsum("ai,bj,ck->ijkabc", shrink, shrink, shrink).reshape(CELL, ROW)
        flat = shrink @ reduce
        low, high = shrink[:, 0], shrink[:, p]
        for axis, spec in enumerate(("c,ai,bj->ijcab", "c,ai,bj->ijacb", "c,ai,bj->ijabc")):
            for side, edge in enumerate((low, high)):
                face[index, 2 * axis + side, :FACE] = np.einsum(spec, edge, flat, flat).reshape(FACE, ROW)
    return (
        split_table(lift.reshape(4 * LANES, LANES)),
        split_table(cell.reshape(-1, ROW)),
        split_table(face.reshape(-1, ROW)),
    )


def iota(shape, axis):
    return lax.broadcasted_iota(jnp.int32, shape, axis)


def halves(x):
    high = x.astype(jnp.bfloat16)
    low = (x - high.astype(jnp.float32)).astype(jnp.bfloat16)
    return high, low


def dot(a, b):
    return jnp.dot(a, b, preferred_element_type=jnp.float32)


def dot3(high, low, table_high, table_low):
    return dot(high, table_high) + dot(low, table_high) + dot(high, table_low)


def earlier(member):
    count = member.shape[1]
    before = (iota((count, count), 0) < iota((count, count), 1)).astype(jnp.float32)
    return dot(member.astype(jnp.bfloat16), before.astype(jnp.bfloat16))


def owner_of(crow, peers, elements):
    first = iota((peers, crow.shape[1]), 0) * elements
    return ((crow >= first) & (crow < first + elements)).astype(jnp.float32)


def row_places(crow, peers, elements, stride):
    member = owner_of(crow, peers, elements)
    rank = earlier(member)
    base = iota(member.shape, 0).astype(jnp.float32)
    place = jnp.sum(member * (base * stride + rank), axis=0, keepdims=True)
    slot = crow.astype(jnp.float32) - jnp.sum(member * (base * elements), axis=0, keepdims=True)
    return place, slot


def onehot_rows(place, rows):
    return (iota((rows, place.shape[1]), 0).astype(jnp.float32) == place).astype(jnp.float32)


def column(onehot, values):
    return jnp.sum(onehot * values, axis=1, keepdims=True)


def pack_kernel(
    peers,
    cap,
    elements,
    get,
    out,
    conf_out,
):
    dest, elem, face, sub, crow, cface, celem = [get(i) for i in range(7)]
    count = dest.shape[1]
    rows = peers * cap
    member = (iota((peers, count), 0) == dest).astype(jnp.float32)
    base = iota(member.shape, 0).astype(jnp.float32) * cap
    place = jnp.sum(member * (base + earlier(member)), axis=0, keepdims=True)
    put = onehot_rows(place, rows)
    code = (face * elements + elem + 1).astype(jnp.float32)
    code_col = column(put, code)
    row_place, row_slot = row_places(crow, peers, elements, cap)
    row_col = column(onehot_rows(row_place, rows), row_slot + 1.0)
    eye = (iota((count, count), 0) == iota((count, count), 1)).astype(jnp.float32)
    sub_col = column(eye, sub.astype(jnp.float32))
    x = jnp.concatenate([get(7), jnp.zeros((count, LANES - TRACE), jnp.float32)], axis=1)
    wide = jnp.concatenate([jnp.where(sub_col == float(s), x, 0.0) for s in range(4)], axis=1)
    high, low = halves(wide)
    lifted = dot3(high, low, get(9), get(10))
    lifted_high, lifted_low = halves(lifted)
    put = put.astype(jnp.bfloat16)
    packed = dot(put, lifted_high) + dot(put, lifted_low)
    lane = iota((rows, LANES), 1)
    packed = jnp.where(lane == TAG_FACE, code_col, packed)
    packed = jnp.where(lane == TAG_ROW, row_col, packed)
    out[...] = packed.reshape(peers, cap, LANES)
    confs = cface.shape[1]
    eye = (iota((confs, confs), 0) == iota((confs, confs), 1)).astype(jnp.float32)
    conf_col = column(eye, (cface * elements + celem + 1).astype(jnp.float32))
    c = jnp.concatenate([get(8), jnp.zeros((confs, LANES - TRACE), jnp.float32)], axis=1)
    conf_out[...] = jnp.where(iota((confs, LANES), 1) == TAG_FACE, conf_col, c)


def cell_kernel(peers, row_cap, get, y_out, col_out, face_high, face_low, spread):
    order, crow = get(0), get(1)
    elements = order.shape[1]
    slots = peers * row_cap
    place, _ = row_places(crow, peers, elements, row_cap)
    take = onehot_rows(place, slots)
    order_col = column(take, order.astype(jnp.float32))
    elem_col = column(take, iota((1, elements), 1).astype(jnp.float32) + 1.0)
    lane = iota((slots, 128), 1)
    col_out[...] = jnp.where(lane == 0, order_col, jnp.where(lane == 1, elem_col, 0.0))
    take = take.astype(jnp.bfloat16)
    spread[...] = jnp.zeros_like(spread)
    for half, part in enumerate(halves(get(2))):
        moved = dot(take, part)
        for v in range(VARS):
            spread[half, v * slots : (v + 1) * slots, :CELL] = moved[:, v * CELL : (v + 1) * CELL]
    order_rows = jnp.concatenate([order_col] * VARS, axis=0)
    high, low = spread[0], spread[1]
    wide_high = jnp.concatenate([jnp.where(order_rows == float(p), high, 0.0).astype(jnp.bfloat16) for p in ORDERS], axis=1)
    wide_low = jnp.concatenate([jnp.where(order_rows == float(p), low, 0.0).astype(jnp.bfloat16) for p in ORDERS], axis=1)
    y_out[...] = dot3(wide_high, wide_low, get(3), get(4))
    face_high[...] = get(5)
    face_low[...] = get(6)


def face_kernel(peers, row_cap, elements, get, incoming, conf, y, cols, table_high, table_low, out, spread):
    slots = peers * row_cap
    x = jnp.concatenate([incoming[...].reshape(-1, LANES), conf[...]], axis=0)
    count = x.shape[0]
    code_col = x[:, TAG_FACE : TAG_FACE + 1]
    code_row = jnp.sum(jnp.where(iota((count, count), 0) == iota((count, count), 1), code_col, 0.0), axis=0, keepdims=True)
    order_col, elem_col = cols[:, 0:1], cols[:, 1:2]
    wanted = jnp.concatenate([jnp.where(elem_col > 0.0, elem_col + float(f * elements), -1.0) for f in range(FACES)], axis=0)
    gather = (wanted == code_row).astype(jnp.bfloat16)
    high, low = halves(x)
    face_sum = dot(gather, high) + dot(gather, low)
    spread[...] = jnp.zeros_like(spread)
    for f in range(FACES):
        for v in range(VARS):
            spread[v * slots : (v + 1) * slots, f * FACE_PAD : f * FACE_PAD + FACE] = face_sum[
                f * slots : (f + 1) * slots, v * FACE : (v + 1) * FACE
            ]
    order_rows = jnp.concatenate([order_col] * VARS, axis=0)
    z = spread[...]
    wide = jnp.concatenate([jnp.where(order_rows == float(p), z, 0.0) for p in ORDERS], axis=1)
    high, low = halves(wide)
    total = y[...] + dot3(high, low, table_high[...], table_low[...])
    for v in range(VARS):
        out[:, :, v * ROW : (v + 1) * ROW] = total[v * slots : (v + 1) * slots].reshape(peers, row_cap, ROW)


def place_kernel(peers, row_cap, get, arrived, tags, out):
    elements = out.shape[0]
    rows = peers * row_cap
    x = arrived[...].reshape(rows, arrived.shape[2])
    slot_col = tags[:, :row_cap, TAG_ROW : TAG_ROW + 1].reshape(rows, 1)
    slot_row = jnp.sum(jnp.where(iota((rows, rows), 0) == iota((rows, rows), 1), slot_col, 0.0), axis=0, keepdims=True)
    put = (iota((elements, rows), 0).astype(jnp.float32) + 1.0 == slot_row).astype(jnp.bfloat16)
    high, low = halves(x)
    rest = (x - high.astype(jnp.float32) - low.astype(jnp.float32)).astype(jnp.bfloat16)
    out[...] = dot(put, high) + dot(put, low) + dot(put, rest)


def fetched(kernel, n_far, n_near, n_out, *refs):
    far, near, outs = refs[:n_far], refs[n_far : n_far + n_near], refs[n_far + n_near : n_far + n_near + n_out]
    rest = refs[n_far + n_near + n_out :]
    held, sems, scratch = rest[:n_far], rest[n_far], rest[n_far + 1 :]
    copies = [pltpu.make_async_copy(src, dst, sems.at[i]) for i, (src, dst) in enumerate(zip(far, held))]
    for copy in copies:
        copy.start()

    def get(i):
        copies[i].wait()
        return held[i][...]

    kernel(get, *near, *outs, *scratch)


def call(kernel, outs, far, near=(), scratch=(), flops=0):
    shapes = jax.tree.leaves(outs)
    sizes = [np.prod(a.shape) * a.dtype.itemsize for a in (*far, *near, *shapes)]
    in_specs = [pl.BlockSpec(memory_space=pltpu.HBM)] * len(far) + [pl.BlockSpec(memory_space=pltpu.VMEM)] * len(near)
    scratch = [*[pltpu.VMEM(a.shape, a.dtype) for a in far], pltpu.SemaphoreType.DMA((max(1, len(far)),)), *scratch]
    return pl.pallas_call(
        functools.partial(fetched, kernel, len(far), len(near), len(shapes)),
        in_specs=in_specs,
        out_shape=outs,
        scratch_shapes=scratch,
        compiler_params=pltpu.CompilerParams(vmem_limit_bytes=48 * 1024 * 1024),
        cost_estimate=pl.CostEstimate(flops=flops, bytes_accessed=int(sum(sizes)), transcendentals=0),
    )(*[pltpu.with_memory_space_constraint(a, pltpu.HBM) for a in far], *near)


def exchange(block):
    return lax.all_to_all(block, ("gx", "gy"), split_axis=0, concat_axis=0, tiled=True)


def from_behind(block, axis, distance):
    devices = range(lax.axis_size(axis))
    route = [((i - distance) % len(devices), i) for i in devices]
    return lax.ppermute(block, axis, route)


def body(
    adjoint,
    order,
    mortar_trace,
    mortar_sub,
    mortar_dest,
    mortar_elem,
    mortar_face,
    conf_trace,
    conf_elem,
    conf_face,
    coarse_row,
):
    elements = adjoint.shape[0]
    count = mortar_trace.shape[0]
    confs = conf_trace.shape[0]
    peers = lax.axis_size("gx") * lax.axis_size("gy")
    cap = max(2, 2 * count // peers)
    row_cap = max(2, elements // peers)
    slots = peers * row_cap
    assert row_cap <= cap
    lift, cell, face = [tuple(jnp.asarray(t) for t in pair) for pair in basis_tables()]
    f32 = jnp.float32
    line = lambda a: a.reshape(1, -1)
    order, coarse_row = line(order), line(coarse_row)
    outgoing, conf = call(
        functools.partial(pack_kernel, peers, cap, elements),
        (jax.ShapeDtypeStruct((peers, cap, LANES), f32), jax.ShapeDtypeStruct((confs, LANES), f32)),
        (
            line(mortar_dest),
            line(mortar_elem),
            line(mortar_face),
            line(mortar_sub),
            coarse_row,
            line(conf_face),
            line(conf_elem),
            mortar_trace,
            conf_trace,
            *lift,
        ),
    )
    incoming = exchange(outgoing)
    conf = from_behind(conf, "gz", 1)
    y, cols, *face = call(
        functools.partial(cell_kernel, peers, row_cap),
        (
            jax.ShapeDtypeStruct((VARS * slots, ROW), f32),
            jax.ShapeDtypeStruct((slots, 128), f32),
            *[jax.ShapeDtypeStruct(t.shape, t.dtype) for t in face],
        ),
        (order, coarse_row, adjoint, *cell, *face),
        scratch=[pltpu.VMEM((2, VARS * slots, CELL_PAD), f32)],
    )
    rows = call(
        functools.partial(face_kernel, peers, row_cap, elements),
        jax.ShapeDtypeStruct((peers, row_cap, VARS * ROW), f32),
        (),
        (incoming, conf, y, cols, *face),
        scratch=[pltpu.VMEM((VARS * slots, FACES * FACE_PAD), f32)],
    )
    arrived = exchange(rows)
    return call(
        functools.partial(place_kernel, peers, row_cap),
        jax.ShapeDtypeStruct((elements, VARS * ROW), f32),
        (),
        (arrived, incoming),
    )


def solution(mesh):
    rows = P(("gx", "gy", "gz"))
    wide = P(("gx", "gy", "gz"), None)
    return jax.shard_map(
        body,
        mesh=mesh,
        in_specs=(wide, rows, wide, rows, wide, rows, rows, wide, rows, rows, rows),
        out_specs=wide,
        check_vma=False,
    )
```

```python
import functools

import jax
import jax.numpy as jnp
import ml_dtypes
import numpy as np
from jax import lax
from jax.experimental import pallas as pl
from jax.experimental.pallas import tpu as pltpu
from jax.sharding import PartitionSpec as P

VARS = 5
NODE = 7
FACE = NODE * NODE
CELL = NODE * FACE
ROW = 216
FACES = 6
ORDERS = (2, 3, 4, 5, 6)
TRACE = VARS * FACE
LANES = 256
TAG_FACE = TRACE
TAG_ROW = TRACE + 1
CELL_PAD = 384
FACE_PAD = 64


def grid_nodes(degree):
    return -np.cos(np.pi * np.arange(degree + 1) / degree)


def lagrange_rows(degree, points):
    anchors = grid_nodes(degree)
    values = np.ones((len(points), degree + 1))
    for k in range(degree + 1):
        for other in range(degree + 1):
            if other != k:
                values[:, k] *= (points - anchors[other]) / (anchors[k] - anchors[other])
    return values


def split_table(table):
    table = np.asarray(table, np.float32)
    high = table.astype(ml_dtypes.bfloat16)
    low = (table - high.astype(np.float32)).astype(ml_dtypes.bfloat16)
    return high, low


@functools.lru_cache(maxsize=None)
def basis_tables():
    top_nodes = grid_nodes(6)
    mortar = [lagrange_rows(6, (top_nodes - 1.0) / 2.0), lagrange_rows(6, (top_nodes + 1.0) / 2.0)]
    lift = np.zeros((4, LANES, LANES))
    for sub in range(4):
        both = np.kron(mortar[sub // 2], mortar[sub % 2])
        for v in range(VARS):
            part = slice(v * FACE, (v + 1) * FACE)
            lift[sub, part, part] = both
    cell = np.zeros((len(ORDERS), CELL_PAD, ROW))
    face = np.zeros((len(ORDERS), FACES, FACE_PAD, ROW))
    for index, p in enumerate(ORDERS):
        shrink = np.zeros((6, NODE))
        shrink[:p, : p + 1] = lagrange_rows(p - 1, grid_nodes(p)).T
        reduce = np.zeros((NODE, NODE))
        reduce[: p + 1, :] = lagrange_rows(p, top_nodes).T
        cell[index, :CELL] = np.einsum("ai,bj,ck->ijkabc", shrink, shrink, shrink).reshape(CELL, ROW)
        flat = shrink @ reduce
        low, high = shrink[:, 0], shrink[:, p]
        for axis, spec in enumerate(("c,ai,bj->ijcab", "c,ai,bj->ijacb", "c,ai,bj->ijabc")):
            for side, edge in enumerate((low, high)):
                face[index, 2 * axis + side, :FACE] = np.einsum(spec, edge, flat, flat).reshape(FACE, ROW)
    return (
        split_table(lift.reshape(4 * LANES, LANES)),
        split_table(cell.reshape(-1, ROW)),
        split_table(face.reshape(-1, ROW)),
    )


def iota(shape, axis):
    return lax.broadcasted_iota(jnp.int32, shape, axis)


def halves(x):
    high = x.astype(jnp.bfloat16)
    low = (x - high.astype(jnp.float32)).astype(jnp.bfloat16)
    return high, low


def dot(a, b):
    return jnp.dot(a, b, preferred_element_type=jnp.float32)


def dot3(high, low, table_high, table_low):
    return dot(high, table_high) + dot(low, table_high) + dot(high, table_low)


def earlier(member):
    count = member.shape[1]
    before = (iota((count, count), 0) < iota((count, count), 1)).astype(jnp.float32)
    return dot(member.astype(jnp.bfloat16), before.astype(jnp.bfloat16))


def pairwise(peers):
    return peers <= 8 and peers & (peers - 1) == 0


def own_index(peers):
    if not pairwise(peers):
        return 0
    return lax.axis_index("gx") * lax.axis_size("gy") + lax.axis_index("gy")


def owner_of(crow, peers, elements, me):
    first = (iota((peers, crow.shape[1]), 0) ^ me) * elements
    return ((crow >= first) & (crow < first + elements)).astype(jnp.float32)


def row_places(crow, peers, elements, stride):
    me = own_index(peers)
    member = owner_of(crow, peers, elements, me)
    rank = earlier(member)
    block = iota(member.shape, 0)
    place = jnp.sum(member * (block * stride + rank.astype(jnp.int32)).astype(jnp.float32), axis=0, keepdims=True)
    owned = ((block ^ me) * elements).astype(jnp.float32)
    slot = crow.astype(jnp.float32) - jnp.sum(member * owned, axis=0, keepdims=True)
    return place, slot


def onehot_rows(place, rows):
    return (iota((rows, place.shape[1]), 0).astype(jnp.float32) == place).astype(jnp.float32)


def column(onehot, values):
    return jnp.sum(onehot * values, axis=1, keepdims=True)


def pack_kernel(
    peers,
    cap,
    elements,
    get,
    conf_out,
    *outs,
):
    dest, elem, face, sub, crow, cface, celem = [get(i) for i in range(7)]
    count = dest.shape[1]
    rows = peers * cap
    member = ((iota((peers, count), 0) ^ own_index(peers)) == dest).astype(jnp.float32)
    base = iota(member.shape, 0).astype(jnp.float32) * cap
    place = jnp.sum(member * (base + earlier(member)), axis=0, keepdims=True)
    put = onehot_rows(place, rows)
    code = (face * elements + elem + 1).astype(jnp.float32)
    code_col = column(put, code)
    row_place, row_slot = row_places(crow, peers, elements, cap)
    row_col = column(onehot_rows(row_place, rows), row_slot + 1.0)
    eye = (iota((count, count), 0) == iota((count, count), 1)).astype(jnp.float32)
    sub_col = column(eye, sub.astype(jnp.float32))
    x = jnp.concatenate([get(7), jnp.zeros((count, LANES - TRACE), jnp.float32)], axis=1)
    wide = jnp.concatenate([jnp.where(sub_col == float(s), x, 0.0) for s in range(4)], axis=1)
    high, low = halves(wide)
    lifted = dot3(high, low, get(9), get(10))
    lifted_high, lifted_low = halves(lifted)
    put = put.astype(jnp.bfloat16)
    packed = dot(put, lifted_high) + dot(put, lifted_low)
    lane = iota((rows, LANES), 1)
    packed = jnp.where(lane == TAG_FACE, code_col, packed)
    packed = jnp.where(lane == TAG_ROW, row_col, packed)
    if len(outs) > 1:
        for k, out in enumerate(outs):
            out[...] = packed[k * cap : (k + 1) * cap]
    else:
        outs[0][...] = packed.reshape(peers, cap, LANES)
    confs = cface.shape[1]
    eye = (iota((confs, confs), 0) == iota((confs, confs), 1)).astype(jnp.float32)
    conf_col = column(eye, (cface * elements + celem + 1).astype(jnp.float32))
    c = jnp.concatenate([get(8), jnp.zeros((confs, LANES - TRACE), jnp.float32)], axis=1)
    conf_out[...] = jnp.where(iota((confs, LANES), 1) == TAG_FACE, conf_col, c)


def cell_kernel(peers, row_cap, get, y_out, col_out, face_high, face_low, spread):
    order, crow = get(0), get(1)
    elements = order.shape[1]
    slots = peers * row_cap
    place, _ = row_places(crow, peers, elements, row_cap)
    take = onehot_rows(place, slots)
    order_col = column(take, order.astype(jnp.float32))
    elem_col = column(take, iota((1, elements), 1).astype(jnp.float32) + 1.0)
    lane = iota((slots, 128), 1)
    col_out[...] = jnp.where(lane == 0, order_col, jnp.where(lane == 1, elem_col, 0.0))
    take = take.astype(jnp.bfloat16)
    spread[...] = jnp.zeros_like(spread)
    for half, part in enumerate(halves(get(2))):
        moved = dot(take, part)
        for v in range(VARS):
            spread[half, v * slots : (v + 1) * slots, :CELL] = moved[:, v * CELL : (v + 1) * CELL]
    order_rows = jnp.concatenate([order_col] * VARS, axis=0)
    high, low = spread[0], spread[1]
    wide_high = jnp.concatenate([jnp.where(order_rows == float(p), high, 0.0).astype(jnp.bfloat16) for p in ORDERS], axis=1)
    wide_low = jnp.concatenate([jnp.where(order_rows == float(p), low, 0.0).astype(jnp.bfloat16) for p in ORDERS], axis=1)
    y_out[...] = dot3(wide_high, wide_low, get(3), get(4))
    face_high[...] = get(5)
    face_low[...] = get(6)


def face_kernel(peers, row_cap, elements, blocks, get, *refs):
    incoming, refs = refs[:blocks], refs[blocks:]
    conf, y, cols, table_high, table_low, *outs, spread = refs
    slots = peers * row_cap
    x = jnp.concatenate([*[block[...].reshape(-1, LANES) for block in incoming], conf[...]], axis=0)
    count = x.shape[0]
    code_col = x[:, TAG_FACE : TAG_FACE + 1]
    code_row = jnp.sum(jnp.where(iota((count, count), 0) == iota((count, count), 1), code_col, 0.0), axis=0, keepdims=True)
    order_col, elem_col = cols[:, 0:1], cols[:, 1:2]
    wanted = jnp.concatenate([jnp.where(elem_col > 0.0, elem_col + float(f * elements), -1.0) for f in range(FACES)], axis=0)
    gather = (wanted == code_row).astype(jnp.bfloat16)
    high, low = halves(x)
    face_sum = dot(gather, high) + dot(gather, low)
    spread[...] = jnp.zeros_like(spread)
    for f in range(FACES):
        for v in range(VARS):
            spread[v * slots : (v + 1) * slots, f * FACE_PAD : f * FACE_PAD + FACE] = face_sum[
                f * slots : (f + 1) * slots, v * FACE : (v + 1) * FACE
            ]
    order_rows = jnp.concatenate([order_col] * VARS, axis=0)
    z = spread[...]
    wide = jnp.concatenate([jnp.where(order_rows == float(p), z, 0.0) for p in ORDERS], axis=1)
    high, low = halves(wide)
    total = y[...] + dot3(high, low, table_high[...], table_low[...])
    for v in range(VARS):
        part = total[v * slots : (v + 1) * slots]
        if len(outs) > 1:
            for k, out in enumerate(outs):
                out[:, v * ROW : (v + 1) * ROW] = part[k * row_cap : (k + 1) * row_cap]
        else:
            outs[0][:, :, v * ROW : (v + 1) * ROW] = part.reshape(peers, row_cap, ROW)


def place_kernel(peers, row_cap, blocks, get, *refs):
    arrived, tags, out = refs[:blocks], refs[blocks : 2 * blocks], refs[-1]
    elements = out.shape[0]
    rows = peers * row_cap
    x = jnp.concatenate([block[...].reshape(-1, out.shape[1]) for block in arrived], axis=0)
    slot_col = jnp.concatenate([tag[..., :row_cap, TAG_ROW : TAG_ROW + 1].reshape(-1, 1) for tag in tags], axis=0)
    slot_row = jnp.sum(jnp.where(iota((rows, rows), 0) == iota((rows, rows), 1), slot_col, 0.0), axis=0, keepdims=True)
    put = (iota((elements, rows), 0).astype(jnp.float32) + 1.0 == slot_row).astype(jnp.bfloat16)
    high, low = halves(x)
    rest = (x - high.astype(jnp.float32) - low.astype(jnp.float32)).astype(jnp.bfloat16)
    out[...] = dot(put, high) + dot(put, low) + dot(put, rest)


def fetched(kernel, n_far, n_near, n_out, *refs):
    far, near, outs = refs[:n_far], refs[n_far : n_far + n_near], refs[n_far + n_near : n_far + n_near + n_out]
    rest = refs[n_far + n_near + n_out :]
    held, sems, scratch = rest[:n_far], rest[n_far], rest[n_far + 1 :]
    copies = [pltpu.make_async_copy(src, dst, sems.at[i]) for i, (src, dst) in enumerate(zip(far, held))]
    for copy in copies:
        copy.start()

    def get(i):
        copies[i].wait()
        return held[i][...]

    kernel(get, *near, *outs, *scratch)


def call(kernel, outs, far, near=(), scratch=(), flops=0):
    shapes = jax.tree.leaves(outs)
    sizes = [np.prod(a.shape) * a.dtype.itemsize for a in (*far, *near, *shapes)]
    in_specs = [pl.BlockSpec(memory_space=pltpu.HBM)] * len(far) + [pl.BlockSpec(memory_space=pltpu.VMEM)] * len(near)
    scratch = [*[pltpu.VMEM(a.shape, a.dtype) for a in far], pltpu.SemaphoreType.DMA((max(1, len(far)),)), *scratch]
    return pl.pallas_call(
        functools.partial(fetched, kernel, len(far), len(near), len(shapes)),
        in_specs=in_specs,
        out_shape=outs,
        scratch_shapes=scratch,
        compiler_params=pltpu.CompilerParams(vmem_limit_bytes=48 * 1024 * 1024),
        cost_estimate=pl.CostEstimate(flops=flops, bytes_accessed=int(sum(sizes)), transcendentals=0),
    )(*[pltpu.with_memory_space_constraint(a, pltpu.HBM) for a in far], *near)


def exchange(blocks):
    if len(blocks) == 1:
        return [lax.all_to_all(blocks[0], ("gx", "gy"), split_axis=0, concat_axis=0, tiled=True)]
    peers = len(blocks)
    arrived = {0: blocks[0]}
    for k in reversed(range(1, peers)):
        arrived[k] = lax.ppermute(blocks[k], ("gx", "gy"), [(i, i ^ k) for i in range(peers)])
    return [arrived[k] for k in range(peers)]


def message(peers, rows, lanes):
    if pairwise(peers):
        return [jax.ShapeDtypeStruct((rows, lanes), jnp.float32)] * peers
    return [jax.ShapeDtypeStruct((peers, rows, lanes), jnp.float32)]


def from_behind(block, axis, distance):
    devices = range(lax.axis_size(axis))
    route = [((i - distance) % len(devices), i) for i in devices]
    return lax.ppermute(block, axis, route)


def body(
    adjoint,
    order,
    mortar_trace,
    mortar_sub,
    mortar_dest,
    mortar_elem,
    mortar_face,
    conf_trace,
    conf_elem,
    conf_face,
    coarse_row,
):
    elements = adjoint.shape[0]
    count = mortar_trace.shape[0]
    confs = conf_trace.shape[0]
    peers = lax.axis_size("gx") * lax.axis_size("gy")
    cap = max(2, 2 * count // peers)
    row_cap = max(2, elements // peers)
    slots = peers * row_cap
    assert row_cap <= cap
    lift, cell, face = [tuple(jnp.asarray(t) for t in pair) for pair in basis_tables()]
    f32 = jnp.float32
    line = lambda a: a.reshape(1, -1)
    order, coarse_row = line(order), line(coarse_row)
    conf, *outgoing = call(
        functools.partial(pack_kernel, peers, cap, elements),
        [jax.ShapeDtypeStruct((confs, LANES), f32), *message(peers, cap, LANES)],
        (
            line(mortar_dest),
            line(mortar_elem),
            line(mortar_face),
            line(mortar_sub),
            coarse_row,
            line(conf_face),
            line(conf_elem),
            mortar_trace,
            conf_trace,
            *lift,
        ),
    )
    incoming = exchange(outgoing)
    conf = from_behind(conf, "gz", 1)
    y, cols, *face = call(
        functools.partial(cell_kernel, peers, row_cap),
        (
            jax.ShapeDtypeStruct((VARS * slots, ROW), f32),
            jax.ShapeDtypeStruct((slots, 128), f32),
            *[jax.ShapeDtypeStruct(t.shape, t.dtype) for t in face],
        ),
        (order, coarse_row, adjoint, *cell, *face),
        scratch=[pltpu.VMEM((2, VARS * slots, CELL_PAD), f32)],
    )
    rows = call(
        functools.partial(face_kernel, peers, row_cap, elements, len(incoming)),
        message(peers, row_cap, VARS * ROW),
        (),
        (*incoming, conf, y, cols, *face),
        scratch=[pltpu.VMEM((VARS * slots, FACES * FACE_PAD), f32)],
    )
    arrived = exchange(rows)
    return call(
        functools.partial(place_kernel, peers, row_cap, len(arrived)),
        jax.ShapeDtypeStruct((elements, VARS * ROW), f32),
        (),
        (*arrived, *incoming),
    )


def solution(mesh):
    rows = P(("gx", "gy", "gz"))
    wide = P(("gx", "gy", "gz"), None)
    return jax.shard_map(
        body,
        mesh=mesh,
        in_specs=(wide, rows, wide, rows, wide, rows, rows, wide, rows, rows, rows),
        out_specs=wide,
        check_vma=False,
    )
```

```python
import functools

import jax
import jax.numpy as jnp
import ml_dtypes
import numpy as np
from jax import lax
from jax.experimental import pallas as pl
from jax.experimental.pallas import tpu as pltpu
from jax.sharding import PartitionSpec as P

VARS = 5
NODE = 7
FACE = NODE * NODE
CELL = NODE * FACE
ROW = 216
FACES = 6
ORDERS = (2, 3, 4, 5, 6)
TRACE = VARS * FACE
LANES = 256
TAG_FACE = TRACE
TAG_ROW = TRACE + 1
CELL_PAD = 384
FACE_PAD = 64


def grid_nodes(degree):
    return -np.cos(np.pi * np.arange(degree + 1) / degree)


def lagrange_rows(degree, points):
    anchors = grid_nodes(degree)
    values = np.ones((len(points), degree + 1))
    for k in range(degree + 1):
        for other in range(degree + 1):
            if other != k:
                values[:, k] *= (points - anchors[other]) / (anchors[k] - anchors[other])
    return values


def split_table(table):
    table = np.asarray(table, np.float32)
    high = table.astype(ml_dtypes.bfloat16)
    low = (table - high.astype(np.float32)).astype(ml_dtypes.bfloat16)
    return high, low


@functools.lru_cache(maxsize=None)
def basis_tables():
    top_nodes = grid_nodes(6)
    mortar = [lagrange_rows(6, (top_nodes - 1.0) / 2.0), lagrange_rows(6, (top_nodes + 1.0) / 2.0)]
    lift = np.zeros((4, LANES, LANES))
    for sub in range(4):
        both = np.kron(mortar[sub // 2], mortar[sub % 2])
        for v in range(VARS):
            part = slice(v * FACE, (v + 1) * FACE)
            lift[sub, part, part] = both
    cell = np.zeros((len(ORDERS), CELL_PAD, ROW))
    face = np.zeros((len(ORDERS), FACES, FACE_PAD, ROW))
    for index, p in enumerate(ORDERS):
        shrink = np.zeros((6, NODE))
        shrink[:p, : p + 1] = lagrange_rows(p - 1, grid_nodes(p)).T
        reduce = np.zeros((NODE, NODE))
        reduce[: p + 1, :] = lagrange_rows(p, top_nodes).T
        cell[index, :CELL] = np.einsum("ai,bj,ck->ijkabc", shrink, shrink, shrink).reshape(CELL, ROW)
        flat = shrink @ reduce
        low, high = shrink[:, 0], shrink[:, p]
        for axis, spec in enumerate(("c,ai,bj->ijcab", "c,ai,bj->ijacb", "c,ai,bj->ijabc")):
            for side, edge in enumerate((low, high)):
                face[index, 2 * axis + side, :FACE] = np.einsum(spec, edge, flat, flat).reshape(FACE, ROW)
    return (
        split_table(lift.reshape(4 * LANES, LANES)),
        split_table(cell.reshape(-1, ROW)),
        split_table(face.reshape(-1, ROW)),
    )


def iota(shape, axis):
    return lax.broadcasted_iota(jnp.int32, shape, axis)


def halves(x):
    high = x.astype(jnp.bfloat16)
    low = (x - high.astype(jnp.float32)).astype(jnp.bfloat16)
    return high, low


def dot(a, b):
    return jnp.dot(a, b, preferred_element_type=jnp.float32)


def dot3(high, low, table_high, table_low):
    return dot(high, table_high) + dot(low, table_high) + dot(high, table_low)


def earlier(member):
    count = member.shape[1]
    before = (iota((count, count), 0) < iota((count, count), 1)).astype(jnp.float32)
    return dot(member.astype(jnp.bfloat16), before.astype(jnp.bfloat16))


def two_level():
    return lax.axis_size("gx") == 2


def own_index():
    return lax.axis_index("gx") * lax.axis_size("gy") if two_level() else 0


def owner_of(crow, peers, elements, me):
    first = (iota((peers, crow.shape[1]), 0) ^ me) * elements
    return ((crow >= first) & (crow < first + elements)).astype(jnp.float32)


def row_places(crow, peers, elements, stride):
    me = own_index()
    member = owner_of(crow, peers, elements, me)
    rank = earlier(member)
    block = iota(member.shape, 0)
    place = jnp.sum(member * (block * stride + rank.astype(jnp.int32)).astype(jnp.float32), axis=0, keepdims=True)
    owned = ((block ^ me) * elements).astype(jnp.float32)
    slot = crow.astype(jnp.float32) - jnp.sum(member * owned, axis=0, keepdims=True)
    return place, slot


def onehot_rows(place, rows):
    return (iota((rows, place.shape[1]), 0).astype(jnp.float32) == place).astype(jnp.float32)


def column(onehot, values):
    return jnp.sum(onehot * values, axis=1, keepdims=True)


def pack_kernel(
    peers,
    cap,
    elements,
    get,
    conf_out,
    *outs,
):
    dest, elem, face, sub, crow, cface, celem = [get(i) for i in range(7)]
    count = dest.shape[1]
    rows = peers * cap
    member = ((iota((peers, count), 0) ^ own_index()) == dest).astype(jnp.float32)
    base = iota(member.shape, 0).astype(jnp.float32) * cap
    place = jnp.sum(member * (base + earlier(member)), axis=0, keepdims=True)
    put = onehot_rows(place, rows)
    code = (face * elements + elem + 1).astype(jnp.float32)
    code_col = column(put, code)
    row_place, row_slot = row_places(crow, peers, elements, cap)
    row_col = column(onehot_rows(row_place, rows), row_slot + 1.0)
    eye = (iota((count, count), 0) == iota((count, count), 1)).astype(jnp.float32)
    sub_col = column(eye, sub.astype(jnp.float32))
    x = jnp.concatenate([get(7), jnp.zeros((count, LANES - TRACE), jnp.float32)], axis=1)
    wide = jnp.concatenate([jnp.where(sub_col == float(s), x, 0.0) for s in range(4)], axis=1)
    high, low = halves(wide)
    lifted = dot3(high, low, get(9), get(10))
    lifted_high, lifted_low = halves(lifted)
    put = put.astype(jnp.bfloat16)
    packed = dot(put, lifted_high) + dot(put, lifted_low)
    lane = iota((rows, LANES), 1)
    packed = jnp.where(lane == TAG_FACE, code_col, packed)
    packed = jnp.where(lane == TAG_ROW, row_col, packed)
    for out, part in zip(outs, jnp.split(packed, len(outs))):
        out[...] = part.reshape(out.shape)
    confs = cface.shape[1]
    eye = (iota((confs, confs), 0) == iota((confs, confs), 1)).astype(jnp.float32)
    conf_col = column(eye, (cface * elements + celem + 1).astype(jnp.float32))
    c = jnp.concatenate([get(8), jnp.zeros((confs, LANES - TRACE), jnp.float32)], axis=1)
    conf_out[...] = jnp.where(iota((confs, LANES), 1) == TAG_FACE, conf_col, c)


def cell_kernel(peers, row_cap, get, y_out, col_out, face_high, face_low, spread):
    order, crow = get(0), get(1)
    elements = order.shape[1]
    slots = peers * row_cap
    place, _ = row_places(crow, peers, elements, row_cap)
    take = onehot_rows(place, slots)
    order_col = column(take, order.astype(jnp.float32))
    elem_col = column(take, iota((1, elements), 1).astype(jnp.float32) + 1.0)
    lane = iota((slots, 128), 1)
    col_out[...] = jnp.where(lane == 0, order_col, jnp.where(lane == 1, elem_col, 0.0))
    take = take.astype(jnp.bfloat16)
    spread[...] = jnp.zeros_like(spread)
    for half, part in enumerate(halves(get(2))):
        moved = dot(take, part)
        for v in range(VARS):
            spread[half, v * slots : (v + 1) * slots, :CELL] = moved[:, v * CELL : (v + 1) * CELL]
    order_rows = jnp.concatenate([order_col] * VARS, axis=0)
    high, low = spread[0], spread[1]
    wide_high = jnp.concatenate([jnp.where(order_rows == float(p), high, 0.0).astype(jnp.bfloat16) for p in ORDERS], axis=1)
    wide_low = jnp.concatenate([jnp.where(order_rows == float(p), low, 0.0).astype(jnp.bfloat16) for p in ORDERS], axis=1)
    y_out[...] = dot3(wide_high, wide_low, get(3), get(4))
    face_high[...] = get(5)
    face_low[...] = get(6)


def face_kernel(peers, row_cap, elements, blocks, get, *refs):
    incoming, refs = refs[:blocks], refs[blocks:]
    conf, y, cols, table_high, table_low, *outs, spread = refs
    slots = peers * row_cap
    x = jnp.concatenate([*[block[...].reshape(-1, LANES) for block in incoming], conf[...]], axis=0)
    count = x.shape[0]
    code_col = x[:, TAG_FACE : TAG_FACE + 1]
    code_row = jnp.sum(jnp.where(iota((count, count), 0) == iota((count, count), 1), code_col, 0.0), axis=0, keepdims=True)
    order_col, elem_col = cols[:, 0:1], cols[:, 1:2]
    wanted = jnp.concatenate([jnp.where(elem_col > 0.0, elem_col + float(f * elements), -1.0) for f in range(FACES)], axis=0)
    gather = (wanted == code_row).astype(jnp.bfloat16)
    high, low = halves(x)
    face_sum = dot(gather, high) + dot(gather, low)
    spread[...] = jnp.zeros_like(spread)
    for f in range(FACES):
        for v in range(VARS):
            spread[v * slots : (v + 1) * slots, f * FACE_PAD : f * FACE_PAD + FACE] = face_sum[
                f * slots : (f + 1) * slots, v * FACE : (v + 1) * FACE
            ]
    order_rows = jnp.concatenate([order_col] * VARS, axis=0)
    z = spread[...]
    wide = jnp.concatenate([jnp.where(order_rows == float(p), z, 0.0) for p in ORDERS], axis=1)
    high, low = halves(wide)
    total = y[...] + dot3(high, low, table_high[...], table_low[...])
    for v in range(VARS):
        parts = jnp.split(total[v * slots : (v + 1) * slots], len(outs))
        for out, part in zip(outs, parts):
            out[:, :, v * ROW : (v + 1) * ROW] = part.reshape(-1, row_cap, ROW)


def place_kernel(peers, row_cap, blocks, get, *refs):
    arrived, tags, out = refs[:blocks], refs[blocks : 2 * blocks], refs[-1]
    elements = out.shape[0]
    rows = peers * row_cap
    x = jnp.concatenate([block[...].reshape(-1, out.shape[1]) for block in arrived], axis=0)
    slot_col = jnp.concatenate([tag[..., :row_cap, TAG_ROW : TAG_ROW + 1].reshape(-1, 1) for tag in tags], axis=0)
    slot_row = jnp.sum(jnp.where(iota((rows, rows), 0) == iota((rows, rows), 1), slot_col, 0.0), axis=0, keepdims=True)
    put = (iota((elements, rows), 0).astype(jnp.float32) + 1.0 == slot_row).astype(jnp.bfloat16)
    high, low = halves(x)
    rest = (x - high.astype(jnp.float32) - low.astype(jnp.float32)).astype(jnp.bfloat16)
    out[...] = dot(put, high) + dot(put, low) + dot(put, rest)


def fetched(kernel, n_far, n_near, n_out, *refs):
    far, near, outs = refs[:n_far], refs[n_far : n_far + n_near], refs[n_far + n_near : n_far + n_near + n_out]
    rest = refs[n_far + n_near + n_out :]
    held, sems, scratch = rest[:n_far], rest[n_far], rest[n_far + 1 :]
    copies = [pltpu.make_async_copy(src, dst, sems.at[i]) for i, (src, dst) in enumerate(zip(far, held))]
    for copy in copies:
        copy.start()

    def get(i):
        copies[i].wait()
        return held[i][...]

    kernel(get, *near, *outs, *scratch)


def call(kernel, outs, far, near=(), scratch=(), flops=0):
    shapes = jax.tree.leaves(outs)
    sizes = [np.prod(a.shape) * a.dtype.itemsize for a in (*far, *near, *shapes)]
    in_specs = [pl.BlockSpec(memory_space=pltpu.HBM)] * len(far) + [pl.BlockSpec(memory_space=pltpu.VMEM)] * len(near)
    scratch = [*[pltpu.VMEM(a.shape, a.dtype) for a in far], pltpu.SemaphoreType.DMA((max(1, len(far)),)), *scratch]
    return pl.pallas_call(
        functools.partial(fetched, kernel, len(far), len(near), len(shapes)),
        in_specs=in_specs,
        out_shape=outs,
        scratch_shapes=scratch,
        compiler_params=pltpu.CompilerParams(vmem_limit_bytes=48 * 1024 * 1024),
        cost_estimate=pl.CostEstimate(flops=flops, bytes_accessed=int(sum(sizes)), transcendentals=0),
    )(*[pltpu.with_memory_space_constraint(a, pltpu.HBM) for a in far], *near)


def exchange(blocks):
    if len(blocks) == 1:
        return [lax.all_to_all(blocks[0], ("gx", "gy"), split_axis=0, concat_axis=0, tiled=True)]
    near, far = blocks
    far = lax.ppermute(far, "gx", [(0, 1), (1, 0)])
    return [lax.all_to_all(block, "gy", split_axis=0, concat_axis=0, tiled=True) for block in (near, far)]


def message(rows, lanes):
    size_x, size_y = lax.axis_size("gx"), lax.axis_size("gy")
    blocks = 2 if two_level() else 1
    return [jax.ShapeDtypeStruct((size_x * size_y // blocks, rows, lanes), jnp.float32)] * blocks


def from_behind(block, axis, distance):
    devices = range(lax.axis_size(axis))
    route = [((i - distance) % len(devices), i) for i in devices]
    return lax.ppermute(block, axis, route)


def body(
    adjoint,
    order,
    mortar_trace,
    mortar_sub,
    mortar_dest,
    mortar_elem,
    mortar_face,
    conf_trace,
    conf_elem,
    conf_face,
    coarse_row,
):
    elements = adjoint.shape[0]
    count = mortar_trace.shape[0]
    confs = conf_trace.shape[0]
    peers = lax.axis_size("gx") * lax.axis_size("gy")
    cap = max(2, 2 * count // peers)
    row_cap = max(2, elements // peers)
    slots = peers * row_cap
    assert row_cap <= cap
    lift, cell, face = [tuple(jnp.asarray(t) for t in pair) for pair in basis_tables()]
    f32 = jnp.float32
    line = lambda a: a.reshape(1, -1)
    order, coarse_row = line(order), line(coarse_row)
    conf, *outgoing = call(
        functools.partial(pack_kernel, peers, cap, elements),
        [jax.ShapeDtypeStruct((confs, LANES), f32), *message(cap, LANES)],
        (
            line(mortar_dest),
            line(mortar_elem),
            line(mortar_face),
            line(mortar_sub),
            coarse_row,
            line(conf_face),
            line(conf_elem),
            mortar_trace,
            conf_trace,
            *lift,
        ),
    )
    incoming = exchange(outgoing)
    conf = from_behind(conf, "gz", 1)
    y, cols, *face = call(
        functools.partial(cell_kernel, peers, row_cap),
        (
            jax.ShapeDtypeStruct((VARS * slots, ROW), f32),
            jax.ShapeDtypeStruct((slots, 128), f32),
            *[jax.ShapeDtypeStruct(t.shape, t.dtype) for t in face],
        ),
        (order, coarse_row, adjoint, *cell, *face),
        scratch=[pltpu.VMEM((2, VARS * slots, CELL_PAD), f32)],
    )
    rows = call(
        functools.partial(face_kernel, peers, row_cap, elements, len(incoming)),
        message(row_cap, VARS * ROW),
        (),
        (*incoming, conf, y, cols, *face),
        scratch=[pltpu.VMEM((VARS * slots, FACES * FACE_PAD), f32)],
    )
    arrived = exchange(rows)
    return call(
        functools.partial(place_kernel, peers, row_cap, len(arrived)),
        jax.ShapeDtypeStruct((elements, VARS * ROW), f32),
        (),
        (*arrived, *incoming),
    )


def solution(mesh):
    rows = P(("gx", "gy", "gz"))
    wide = P(("gx", "gy", "gz"), None)
    return jax.shard_map(
        body,
        mesh=mesh,
        in_specs=(wide, rows, wide, rows, wide, rows, rows, wide, rows, rows, rows),
        out_specs=wide,
        check_vma=False,
    )
```

```python
import functools

import jax
import jax.numpy as jnp
import ml_dtypes
import numpy as np
from jax import lax
from jax.experimental import pallas as pl
from jax.experimental.pallas import tpu as pltpu
from jax.sharding import PartitionSpec as P

VARS = 5
NODE = 7
FACE = NODE * NODE
CELL = NODE * FACE
ROW = 216
FACES = 6
ORDERS = (2, 3, 4, 5, 6)
TRACE = VARS * FACE
LANES = 256
TAG_FACE = TRACE
TAG_ROW = TRACE + 1
CELL_PAD = 384
FACE_PAD = 64
ROWS_PAD = 1152


def grid_nodes(degree):
    return -np.cos(np.pi * np.arange(degree + 1) / degree)


def lagrange_rows(degree, points):
    anchors = grid_nodes(degree)
    values = np.ones((len(points), degree + 1))
    for k in range(degree + 1):
        for other in range(degree + 1):
            if other != k:
                values[:, k] *= (points - anchors[other]) / (anchors[k] - anchors[other])
    return values


def split_table(table):
    table = np.asarray(table, np.float32)
    high = table.astype(ml_dtypes.bfloat16)
    low = (table - high.astype(np.float32)).astype(ml_dtypes.bfloat16)
    return high, low


@functools.lru_cache(maxsize=None)
def basis_tables():
    top_nodes = grid_nodes(6)
    mortar = [lagrange_rows(6, (top_nodes - 1.0) / 2.0), lagrange_rows(6, (top_nodes + 1.0) / 2.0)]
    lift = np.zeros((4, LANES, LANES))
    for sub in range(4):
        both = np.kron(mortar[sub // 2], mortar[sub % 2])
        for v in range(VARS):
            part = slice(v * FACE, (v + 1) * FACE)
            lift[sub, part, part] = both
    cell = np.zeros((len(ORDERS), CELL_PAD, ROW))
    face = np.zeros((len(ORDERS), FACES, FACE_PAD, ROW))
    for index, p in enumerate(ORDERS):
        shrink = np.zeros((6, NODE))
        shrink[:p, : p + 1] = lagrange_rows(p - 1, grid_nodes(p)).T
        reduce = np.zeros((NODE, NODE))
        reduce[: p + 1, :] = lagrange_rows(p, top_nodes).T
        cell[index, :CELL] = np.einsum("ai,bj,ck->ijkabc", shrink, shrink, shrink).reshape(CELL, ROW)
        flat = shrink @ reduce
        low, high = shrink[:, 0], shrink[:, p]
        for axis, spec in enumerate(("c,ai,bj->ijcab", "c,ai,bj->ijacb", "c,ai,bj->ijabc")):
            for side, edge in enumerate((low, high)):
                face[index, 2 * axis + side, :FACE] = np.einsum(spec, edge, flat, flat).reshape(FACE, ROW)
    return (
        split_table(lift.reshape(4 * LANES, LANES)),
        split_table(cell.reshape(-1, ROW)),
        split_table(face.reshape(-1, ROW)),
    )


def iota(shape, axis):
    return lax.broadcasted_iota(jnp.int32, shape, axis)


def halves(x):
    high = x.astype(jnp.bfloat16)
    low = (x - high.astype(jnp.float32)).astype(jnp.bfloat16)
    return high, low


def dot(a, b):
    return jnp.dot(a, b, preferred_element_type=jnp.float32)


def dot3(high, low, table_high, table_low):
    return dot(high, table_high) + dot(low, table_high) + dot(high, table_low)


def earlier(member):
    count = member.shape[1]
    before = (iota((count, count), 0) < iota((count, count), 1)).astype(jnp.float32)
    return dot(member.astype(jnp.bfloat16), before.astype(jnp.bfloat16))


def owner_of(crow, peers, elements):
    first = iota((peers, crow.shape[1]), 0) * elements
    return ((crow >= first) & (crow < first + elements)).astype(jnp.float32)


def row_places(crow, peers, elements, stride):
    member = owner_of(crow, peers, elements)
    rank = earlier(member)
    base = iota(member.shape, 0).astype(jnp.float32)
    place = jnp.sum(member * (base * stride + rank), axis=0, keepdims=True)
    slot = crow.astype(jnp.float32) - jnp.sum(member * (base * elements), axis=0, keepdims=True)
    return place, slot


def onehot_rows(place, rows):
    return (iota((rows, place.shape[1]), 0).astype(jnp.float32) == place).astype(jnp.float32)


def column(onehot, values):
    return jnp.sum(onehot * values, axis=1, keepdims=True)


def lift_traces(trace, sub, table_high, table_low):
    count = trace.shape[0]
    eye = (iota((count, count), 0) == iota((count, count), 1)).astype(jnp.float32)
    sub_col = column(eye, sub.astype(jnp.float32))
    x = jnp.concatenate([trace, jnp.zeros((count, LANES - TRACE), jnp.float32)], axis=1)
    wide = jnp.concatenate([jnp.where(sub_col == float(s), x, 0.0) for s in range(4)], axis=1)
    high, low = halves(wide)
    return dot3(high, low, table_high, table_low)


def pack_kernel(
    peers,
    cap,
    elements,
    get,
    out,
    conf_out,
):
    dest, elem, face, sub, crow, cface, celem = [get(i) for i in range(7)]
    count = dest.shape[1]
    rows = peers * cap
    member = (iota((peers, count), 0) == dest).astype(jnp.float32)
    base = iota(member.shape, 0).astype(jnp.float32) * cap
    place = jnp.sum(member * (base + earlier(member)), axis=0, keepdims=True)
    put = onehot_rows(place, rows)
    code = (face * elements + elem + 1).astype(jnp.float32)
    code_col = column(put, code)
    row_place, row_slot = row_places(crow, peers, elements, cap)
    row_col = column(onehot_rows(row_place, rows), row_slot + 1.0)
    lifted_high, lifted_low = halves(lift_traces(get(7), sub, get(9), get(10)))
    put = put.astype(jnp.bfloat16)
    packed = dot(put, lifted_high) + dot(put, lifted_low)
    lane = iota((rows, LANES), 1)
    packed = jnp.where(lane == TAG_FACE, code_col, packed)
    packed = jnp.where(lane == TAG_ROW, row_col, packed)
    out[...] = packed.reshape(peers, cap, LANES)
    confs = cface.shape[1]
    eye = (iota((confs, confs), 0) == iota((confs, confs), 1)).astype(jnp.float32)
    conf_col = column(eye, (cface * elements + celem + 1).astype(jnp.float32))
    c = jnp.concatenate([get(8), jnp.zeros((confs, LANES - TRACE), jnp.float32)], axis=1)
    conf_out[...] = jnp.where(iota((confs, LANES), 1) == TAG_FACE, conf_col, c)


def restrict_cells(take, order_col, adjoint, table_high, table_low, spread):
    slots = take.shape[0]
    take = take.astype(jnp.bfloat16)
    spread[...] = jnp.zeros_like(spread)
    for half, part in enumerate(halves(adjoint)):
        moved = dot(take, part)
        for v in range(VARS):
            spread[half, v * slots : (v + 1) * slots, :CELL] = moved[:, v * CELL : (v + 1) * CELL]
    order_rows = jnp.concatenate([order_col] * VARS, axis=0)
    wide = [
        jnp.concatenate([jnp.where(order_rows == float(p), spread[half], 0.0).astype(jnp.bfloat16) for p in ORDERS], axis=1)
        for half in range(2)
    ]
    return dot3(*wide, table_high[...], table_low[...])


def restrict_faces(face_sum, order_col, table_high, table_low, spread):
    slots = order_col.shape[0]
    spread[...] = jnp.zeros_like(spread)
    for f in range(FACES):
        for v in range(VARS):
            spread[v * slots : (v + 1) * slots, f * FACE_PAD : f * FACE_PAD + FACE] = face_sum[
                f * slots : (f + 1) * slots, v * FACE : (v + 1) * FACE
            ]
    order_rows = jnp.concatenate([order_col] * VARS, axis=0)
    z = spread[...]
    wide = jnp.concatenate([jnp.where(order_rows == float(p), z, 0.0) for p in ORDERS], axis=1)
    high, low = halves(wide)
    return dot3(high, low, table_high[...], table_low[...])


def cell_kernel(peers, row_cap, get, y_out, col_out, spread):
    order, crow = get(0), get(1)
    elements = order.shape[1]
    slots = peers * row_cap
    place, _ = row_places(crow, peers, elements, row_cap)
    take = onehot_rows(place, slots)
    order_col = column(take, order.astype(jnp.float32))
    elem_col = column(take, iota((1, elements), 1).astype(jnp.float32) + 1.0)
    lane = iota((slots, 128), 1)
    col_out[...] = jnp.where(lane == 0, order_col, jnp.where(lane == 1, elem_col, 0.0))
    y_out[...] = restrict_cells(take, order_col, get(2), get(3), get(4), spread)


def face_kernel(peers, row_cap, elements, get, incoming, conf, y, cols, table_high, table_low, out, spread):
    slots = peers * row_cap
    x = jnp.concatenate([incoming[...].reshape(-1, LANES), conf[...]], axis=0)
    count = x.shape[0]
    code_col = x[:, TAG_FACE : TAG_FACE + 1]
    code_row = jnp.sum(jnp.where(iota((count, count), 0) == iota((count, count), 1), code_col, 0.0), axis=0, keepdims=True)
    order_col, elem_col = cols[:, 0:1], cols[:, 1:2]
    wanted = jnp.concatenate([jnp.where(elem_col > 0.0, elem_col + float(f * elements), -1.0) for f in range(FACES)], axis=0)
    gather = (wanted == code_row).astype(jnp.bfloat16)
    high, low = halves(x)
    face_sum = dot(gather, high) + dot(gather, low)
    total = y[...] + restrict_faces(face_sum, order_col, table_high, table_low, spread)
    for v in range(VARS):
        out[:, :, v * ROW : (v + 1) * ROW] = total[v * slots : (v + 1) * slots].reshape(peers, row_cap, ROW)


def place_rows(x, slot_col, elements):
    rows = x.shape[0]
    slot_row = jnp.sum(jnp.where(iota((rows, rows), 0) == iota((rows, rows), 1), slot_col, 0.0), axis=0, keepdims=True)
    put = (iota((elements, rows), 0).astype(jnp.float32) + 1.0 == slot_row).astype(jnp.bfloat16)
    high, low = halves(x)
    rest = (x - high.astype(jnp.float32) - low.astype(jnp.float32)).astype(jnp.bfloat16)
    return dot(put, high) + dot(put, low) + dot(put, rest)


def place_kernel(peers, row_cap, get, arrived, tags, out):
    elements = out.shape[0]
    rows = peers * row_cap
    x = arrived[...].reshape(rows, arrived.shape[2])
    slot_col = tags[:, :row_cap, TAG_ROW : TAG_ROW + 1].reshape(rows, 1)
    out[...] = place_rows(x, slot_col, elements)


def lift_kernel(peers, elements, get, out):
    dest, elem, face, sub = [get(i) for i in range(4)]
    count = dest.shape[1]
    code = ((face * peers + dest) * elements + elem + 1).astype(jnp.float32)
    tags = jnp.concatenate([code, jnp.zeros((1, LANES - count), jnp.float32)], axis=1)
    out[count:, :] = jnp.where(iota((8, LANES), 0) == 0, tags, 0.0)
    out[:count, :] = lift_traces(get(4), sub, get(5), get(6))


def rows_kernel(
    peers,
    row_cap,
    get,
    adjoint,
    order,
    crow,
    cell_high,
    cell_low,
    face_high,
    face_low,
    conf,
    celem,
    cface,
    out,
    cell_spread,
    face_spread,
):
    elements = order.shape[1]
    slots = peers * row_cap
    place, slot = row_places(crow[...], peers, elements, row_cap)
    take = onehot_rows(place, slots)
    order_col = column(take, order[...].astype(jnp.float32))
    elem_col = column(take, iota((1, elements), 1).astype(jnp.float32) + 1.0)
    slot_col = column(take, slot + 1.0)
    wanted = jnp.concatenate([elem_col + float(f * elements) for f in range(FACES)], axis=0)
    code = (cface[...] * elements + celem[...] + 1).astype(jnp.float32)
    gather = (wanted == code).astype(jnp.bfloat16)
    high, low = halves(conf[...])
    face_sum = dot(gather, high) + dot(gather, low)
    total = restrict_cells(take, order_col, adjoint[...], cell_high, cell_low, cell_spread)
    total = total + restrict_faces(face_sum, order_col, face_high, face_low, face_spread)
    for v in range(VARS):
        part = total[v * slots : (v + 1) * slots]
        out[:, :, v * ROW : (v + 1) * ROW] = part.reshape(peers, row_cap, ROW)
    tags = jnp.concatenate([elem_col, order_col, slot_col], axis=1)
    out[:, :, VARS * ROW : VARS * ROW + 3] = tags.reshape(peers, row_cap, 3)


def finish_kernel(peers, row_cap, elements, get, arrived, traces, face_high, face_low, out, spread):
    rows = peers * row_cap
    block = traces.shape[0] // peers
    x = arrived[...].reshape(rows, arrived.shape[2])
    elem_col, order_col, slot_col = [x[:, VARS * ROW + i : VARS * ROW + i + 1] for i in range(3)]
    source = (iota((rows, 1), 0) // row_cap * elements).astype(jnp.float32)
    wanted = jnp.concatenate([elem_col + source + float(f * peers * elements) for f in range(FACES)], axis=0)
    face_sum = None
    for k in range(peers):
        part = traces[k * block : (k + 1) * block, :]
        gather = (wanted == part[block - 8 : block - 7, :block]).astype(jnp.bfloat16)
        high, low = halves(part)
        add = dot(gather, high) + dot(gather, low)
        face_sum = add if face_sum is None else face_sum + add
    total = restrict_faces(face_sum, order_col, face_high, face_low, spread)
    total = x[:, : VARS * ROW] + jnp.concatenate([total[v * rows : (v + 1) * rows] for v in range(VARS)], axis=1)
    out[...] = place_rows(total, slot_col, elements)


def fetched(kernel, n_far, n_pass, n_near, n_out, *refs):
    far, near, outs = refs[:n_far], refs[n_far : n_far + n_near], refs[n_far + n_near : n_far + n_near + n_out]
    rest = refs[n_far + n_near + n_out :]
    n_held = n_far - n_pass
    held, sems, scratch = rest[:n_held], rest[n_held], rest[n_held + 1 :]
    held = (*held, *outs[n_out - n_pass :])
    copies = [pltpu.make_async_copy(src, dst, sems.at[i]) for i, (src, dst) in enumerate(zip(far, held))]
    for copy in copies:
        copy.start()

    def get(i):
        copies[i].wait()
        return held[i][...]

    kernel(get, *near, *outs[: n_out - n_pass], *scratch)
    for copy in copies[n_held:]:
        copy.wait()


def like(a):
    return jax.ShapeDtypeStruct(a.shape, a.dtype)


def call(kernel, outs, far, near=(), scratch=(), hand_on=(), flops=0):
    outs = [*outs, *[like(a) for a in hand_on]]
    sizes = [np.prod(a.shape) * a.dtype.itemsize for a in (*far, *near, *outs)]
    held = [pltpu.VMEM(a.shape, a.dtype) for a in far]
    far = (*far, *hand_on)
    in_specs = [pl.BlockSpec(memory_space=pltpu.HBM)] * len(far) + [pl.BlockSpec(memory_space=pltpu.VMEM)] * len(near)
    return pl.pallas_call(
        functools.partial(fetched, kernel, len(far), len(hand_on), len(near), len(outs)),
        in_specs=in_specs,
        out_shape=outs,
        scratch_shapes=[*held, pltpu.SemaphoreType.DMA((max(1, len(far)),)), *scratch],
        compiler_params=pltpu.CompilerParams(vmem_limit_bytes=48 * 1024 * 1024),
        cost_estimate=pl.CostEstimate(flops=flops, bytes_accessed=int(sum(sizes)), transcendentals=0),
    )(*[pltpu.with_memory_space_constraint(a, pltpu.HBM) for a in far], *near)


def exchange(block):
    return lax.all_to_all(block, ("gx", "gy"), split_axis=0, concat_axis=0, tiled=True)


def from_behind(block, axis, distance):
    devices = range(lax.axis_size(axis))
    route = [((i - distance) % len(devices), i) for i in devices]
    return lax.ppermute(block, axis, route)


def body(
    adjoint,
    order,
    mortar_trace,
    mortar_sub,
    mortar_dest,
    mortar_elem,
    mortar_face,
    conf_trace,
    conf_elem,
    conf_face,
    coarse_row,
):
    elements = adjoint.shape[0]
    count = mortar_trace.shape[0]
    confs = conf_trace.shape[0]
    peers = lax.axis_size("gx") * lax.axis_size("gy")
    cap = max(2, 2 * count // peers)
    row_cap = max(2, elements // peers)
    slots = peers * row_cap
    assert row_cap <= cap
    lift, cell, face = [tuple(jnp.asarray(t) for t in pair) for pair in basis_tables()]
    f32 = jnp.float32
    line = lambda a: a.reshape(1, -1)
    order, coarse_row = line(order), line(coarse_row)
    whole = (adjoint, order, coarse_row, *cell, *face)
    mortar = (line(mortar_dest), line(mortar_elem), line(mortar_face), line(mortar_sub))
    if peers <= 8:
        conf, conf_elem, conf_face = [from_behind(a, "gz", 1) for a in (conf_trace, line(conf_elem), line(conf_face))]
        lifted, *whole = call(
            functools.partial(lift_kernel, peers, elements),
            [jax.ShapeDtypeStruct((count + 8, LANES), f32)],
            (*mortar, mortar_trace, *lift),
            hand_on=whole,
        )
        lifted = lax.all_gather(lifted, ("gx", "gy"), axis=0, tiled=True)
        (rows,) = call(
            functools.partial(rows_kernel, peers, row_cap),
            [jax.ShapeDtypeStruct((peers, row_cap, ROWS_PAD), f32)],
            (),
            (*whole, conf, conf_elem, conf_face),
            scratch=[
                pltpu.VMEM((2, VARS * slots, CELL_PAD), f32),
                pltpu.VMEM((VARS * slots, FACES * FACE_PAD), f32),
            ],
        )
        (out,) = call(
            functools.partial(finish_kernel, peers, row_cap, elements),
            [jax.ShapeDtypeStruct((elements, VARS * ROW), f32)],
            (),
            (exchange(rows), lifted, *whole[-2:]),
            scratch=[pltpu.VMEM((VARS * slots, FACES * FACE_PAD), f32)],
        )
        return out
    outgoing, conf = call(
        functools.partial(pack_kernel, peers, cap, elements),
        [jax.ShapeDtypeStruct((peers, cap, LANES), f32), jax.ShapeDtypeStruct((confs, LANES), f32)],
        (*mortar, coarse_row, line(conf_face), line(conf_elem), mortar_trace, conf_trace, *lift),
    )
    incoming = exchange(outgoing)
    conf = from_behind(conf, "gz", 1)
    y, cols, *face = call(
        functools.partial(cell_kernel, peers, row_cap),
        [jax.ShapeDtypeStruct((VARS * slots, ROW), f32), jax.ShapeDtypeStruct((slots, 128), f32)],
        (order, coarse_row, adjoint, *cell),
        scratch=[pltpu.VMEM((2, VARS * slots, CELL_PAD), f32)],
        hand_on=face,
    )
    (rows,) = call(
        functools.partial(face_kernel, peers, row_cap, elements),
        [jax.ShapeDtypeStruct((peers, row_cap, VARS * ROW), f32)],
        (),
        (incoming, conf, y, cols, *face),
        scratch=[pltpu.VMEM((VARS * slots, FACES * FACE_PAD), f32)],
    )
    (out,) = call(
        functools.partial(place_kernel, peers, row_cap),
        [jax.ShapeDtypeStruct((elements, VARS * ROW), f32)],
        (),
        (exchange(rows), incoming),
    )
    return out


def solution(mesh):
    rows = P(("gx", "gy", "gz"))
    wide = P(("gx", "gy", "gz"), None)
    return jax.shard_map(
        body,
        mesh=mesh,
        in_specs=(wide, rows, wide, rows, wide, rows, rows, wide, rows, rows, rows),
        out_specs=wide,
        check_vma=False,
    )
```

```python
import functools

import jax
import jax.numpy as jnp
import ml_dtypes
import numpy as np
from jax import lax
from jax.experimental import pallas as pl
from jax.experimental.pallas import tpu as pltpu
from jax.sharding import PartitionSpec as P

VARS = 5
NODE = 7
FACE = NODE * NODE
CELL = NODE * FACE
ROW = 216
FACES = 6
ORDERS = (2, 3, 4, 5, 6)
TRACE = VARS * FACE
LANES = 256
TAG_FACE = TRACE
TAG_ROW = TRACE + 1
CELL_PAD = 384
FACE_PAD = 64
ROWS_PAD = 1152


def grid_nodes(degree):
    return -np.cos(np.pi * np.arange(degree + 1) / degree)


def lagrange_rows(degree, points):
    anchors = grid_nodes(degree)
    values = np.ones((len(points), degree + 1))
    for k in range(degree + 1):
        for other in range(degree + 1):
            if other != k:
                values[:, k] *= (points - anchors[other]) / (anchors[k] - anchors[other])
    return values


def split_table(table):
    table = np.asarray(table, np.float32)
    high = table.astype(ml_dtypes.bfloat16)
    low = (table - high.astype(np.float32)).astype(ml_dtypes.bfloat16)
    return high, low


@functools.lru_cache(maxsize=None)
def basis_tables():
    top_nodes = grid_nodes(6)
    mortar = [lagrange_rows(6, (top_nodes - 1.0) / 2.0), lagrange_rows(6, (top_nodes + 1.0) / 2.0)]
    lift = np.zeros((4, LANES, LANES))
    for sub in range(4):
        both = np.kron(mortar[sub // 2], mortar[sub % 2])
        for v in range(VARS):
            part = slice(v * FACE, (v + 1) * FACE)
            lift[sub, part, part] = both
    cell = np.zeros((len(ORDERS), CELL_PAD, ROW))
    face = np.zeros((len(ORDERS), FACES, FACE_PAD, ROW))
    for index, p in enumerate(ORDERS):
        shrink = np.zeros((6, NODE))
        shrink[:p, : p + 1] = lagrange_rows(p - 1, grid_nodes(p)).T
        reduce = np.zeros((NODE, NODE))
        reduce[: p + 1, :] = lagrange_rows(p, top_nodes).T
        cell[index, :CELL] = np.einsum("ai,bj,ck->ijkabc", shrink, shrink, shrink).reshape(CELL, ROW)
        flat = shrink @ reduce
        low, high = shrink[:, 0], shrink[:, p]
        for axis, spec in enumerate(("c,ai,bj->ijcab", "c,ai,bj->ijacb", "c,ai,bj->ijabc")):
            for side, edge in enumerate((low, high)):
                face[index, 2 * axis + side, :FACE] = np.einsum(spec, edge, flat, flat).reshape(FACE, ROW)
    return (
        split_table(lift.reshape(4 * LANES, LANES)),
        split_table(cell.reshape(-1, ROW)),
        split_table(face.reshape(-1, ROW)),
    )


def iota(shape, axis):
    return lax.broadcasted_iota(jnp.int32, shape, axis)


def halves(x):
    high = x.astype(jnp.bfloat16)
    low = (x - high.astype(jnp.float32)).astype(jnp.bfloat16)
    return high, low


def dot(a, b):
    return jnp.dot(a, b, preferred_element_type=jnp.float32)


def dot3(high, low, table_high, table_low):
    return dot(high, table_high) + dot(low, table_high) + dot(high, table_low)


def earlier(member):
    count = member.shape[1]
    before = (iota((count, count), 0) < iota((count, count), 1)).astype(jnp.float32)
    return dot(member.astype(jnp.bfloat16), before.astype(jnp.bfloat16))


def owner_of(crow, peers, elements):
    first = iota((peers, crow.shape[1]), 0) * elements
    return ((crow >= first) & (crow < first + elements)).astype(jnp.float32)


def row_places(crow, peers, elements, stride):
    member = owner_of(crow, peers, elements)
    rank = earlier(member)
    base = iota(member.shape, 0).astype(jnp.float32)
    place = jnp.sum(member * (base * stride + rank), axis=0, keepdims=True)
    slot = crow.astype(jnp.float32) - jnp.sum(member * (base * elements), axis=0, keepdims=True)
    return place, slot


def onehot_rows(place, rows):
    return (iota((rows, place.shape[1]), 0).astype(jnp.float32) == place).astype(jnp.float32)


def column(onehot, values):
    return jnp.sum(onehot * values, axis=1, keepdims=True)


def lift_traces(trace, sub, table_high, table_low):
    count = trace.shape[0]
    eye = (iota((count, count), 0) == iota((count, count), 1)).astype(jnp.float32)
    sub_col = column(eye, sub.astype(jnp.float32))
    x = jnp.concatenate([trace, jnp.zeros((count, LANES - TRACE), jnp.float32)], axis=1)
    wide = jnp.concatenate([jnp.where(sub_col == float(s), x, 0.0) for s in range(4)], axis=1)
    high, low = halves(wide)
    return dot3(high, low, table_high, table_low)


def pack_kernel(
    peers,
    cap,
    elements,
    get,
    out,
    conf_out,
):
    dest, elem, face, sub, crow, cface, celem = [get(i) for i in range(7)]
    count = dest.shape[1]
    rows = peers * cap
    member = (iota((peers, count), 0) == dest).astype(jnp.float32)
    base = iota(member.shape, 0).astype(jnp.float32) * cap
    place = jnp.sum(member * (base + earlier(member)), axis=0, keepdims=True)
    put = onehot_rows(place, rows)
    code = (face * elements + elem + 1).astype(jnp.float32)
    code_col = column(put, code)
    row_place, row_slot = row_places(crow, peers, elements, cap)
    row_col = column(onehot_rows(row_place, rows), row_slot + 1.0)
    lifted_high, lifted_low = halves(lift_traces(get(7), sub, get(9), get(10)))
    put = put.astype(jnp.bfloat16)
    packed = dot(put, lifted_high) + dot(put, lifted_low)
    lane = iota((rows, LANES), 1)
    packed = jnp.where(lane == TAG_FACE, code_col, packed)
    packed = jnp.where(lane == TAG_ROW, row_col, packed)
    out[...] = packed.reshape(peers, cap, LANES)
    confs = cface.shape[1]
    eye = (iota((confs, confs), 0) == iota((confs, confs), 1)).astype(jnp.float32)
    conf_col = column(eye, (cface * elements + celem + 1).astype(jnp.float32))
    c = jnp.concatenate([get(8), jnp.zeros((confs, LANES - TRACE), jnp.float32)], axis=1)
    conf_out[...] = jnp.where(iota((confs, LANES), 1) == TAG_FACE, conf_col, c)


def restrict_cells(take, order_col, adjoint, table_high, table_low, spread):
    slots = take.shape[0]
    take = take.astype(jnp.bfloat16)
    spread[...] = jnp.zeros_like(spread)
    for half, part in enumerate(halves(adjoint)):
        moved = dot(take, part)
        for v in range(VARS):
            spread[half, v * slots : (v + 1) * slots, :CELL] = moved[:, v * CELL : (v + 1) * CELL]
    order_rows = jnp.concatenate([order_col] * VARS, axis=0)
    wide = [
        jnp.concatenate([jnp.where(order_rows == float(p), spread[half], 0.0).astype(jnp.bfloat16) for p in ORDERS], axis=1)
        for half in range(2)
    ]
    return dot3(*wide, table_high[...], table_low[...])


def restrict_faces(face_sum, order_col, table_high, table_low, spread):
    slots = order_col.shape[0]
    spread[...] = jnp.zeros_like(spread)
    for f in range(FACES):
        for v in range(VARS):
            spread[v * slots : (v + 1) * slots, f * FACE_PAD : f * FACE_PAD + FACE] = face_sum[
                f * slots : (f + 1) * slots, v * FACE : (v + 1) * FACE
            ]
    order_rows = jnp.concatenate([order_col] * VARS, axis=0)
    z = spread[...]
    wide = jnp.concatenate([jnp.where(order_rows == float(p), z, 0.0) for p in ORDERS], axis=1)
    high, low = halves(wide)
    return dot3(high, low, table_high[...], table_low[...])


def cell_kernel(peers, row_cap, get, y_out, col_out, spread):
    order, crow = get(0), get(1)
    elements = order.shape[1]
    slots = peers * row_cap
    place, _ = row_places(crow, peers, elements, row_cap)
    take = onehot_rows(place, slots)
    order_col = column(take, order.astype(jnp.float32))
    elem_col = column(take, iota((1, elements), 1).astype(jnp.float32) + 1.0)
    lane = iota((slots, 128), 1)
    col_out[...] = jnp.where(lane == 0, order_col, jnp.where(lane == 1, elem_col, 0.0))
    y_out[...] = restrict_cells(take, order_col, get(2), get(3), get(4), spread)


def face_kernel(peers, row_cap, elements, get, incoming, conf, y, cols, table_high, table_low, out, spread):
    slots = peers * row_cap
    x = jnp.concatenate([incoming[...].reshape(-1, LANES), conf[...]], axis=0)
    count = x.shape[0]
    code_col = x[:, TAG_FACE : TAG_FACE + 1]
    code_row = jnp.sum(jnp.where(iota((count, count), 0) == iota((count, count), 1), code_col, 0.0), axis=0, keepdims=True)
    order_col, elem_col = cols[:, 0:1], cols[:, 1:2]
    wanted = jnp.concatenate([jnp.where(elem_col > 0.0, elem_col + float(f * elements), -1.0) for f in range(FACES)], axis=0)
    gather = (wanted == code_row).astype(jnp.bfloat16)
    high, low = halves(x)
    face_sum = dot(gather, high) + dot(gather, low)
    total = y[...] + restrict_faces(face_sum, order_col, table_high, table_low, spread)
    for v in range(VARS):
        out[:, :, v * ROW : (v + 1) * ROW] = total[v * slots : (v + 1) * slots].reshape(peers, row_cap, ROW)


def place_rows(x, slot_col, elements):
    rows = x.shape[0]
    slot_row = jnp.sum(jnp.where(iota((rows, rows), 0) == iota((rows, rows), 1), slot_col, 0.0), axis=0, keepdims=True)
    put = (iota((elements, rows), 0).astype(jnp.float32) + 1.0 == slot_row).astype(jnp.bfloat16)
    high, low = halves(x)
    rest = (x - high.astype(jnp.float32) - low.astype(jnp.float32)).astype(jnp.bfloat16)
    return dot(put, high) + dot(put, low) + dot(put, rest)


def place_kernel(peers, row_cap, get, arrived, tags, out):
    elements = out.shape[0]
    rows = peers * row_cap
    x = arrived[...].reshape(rows, arrived.shape[2])
    slot_col = tags[:, :row_cap, TAG_ROW : TAG_ROW + 1].reshape(rows, 1)
    out[...] = place_rows(x, slot_col, elements)


def lift_kernel(peers, elements, get, out):
    dest, elem, face, sub = [get(i) for i in range(4)]
    count = dest.shape[1]
    code = ((face * peers + dest) * elements + elem + 1).astype(jnp.float32)
    tags = jnp.concatenate([code, jnp.zeros((1, LANES - count), jnp.float32)], axis=1)
    out[count:, :] = jnp.where(iota((8, LANES), 0) == 0, tags, 0.0)
    out[:count, :] = lift_traces(get(4), sub, get(5), get(6))


def rows_kernel(
    peers,
    row_cap,
    get,
    adjoint,
    order,
    crow,
    cell_high,
    cell_low,
    face_high,
    face_low,
    conf,
    celem,
    cface,
    out,
    cell_spread,
    face_spread,
):
    elements = order.shape[1]
    slots = peers * row_cap
    place, slot = row_places(crow[...], peers, elements, row_cap)
    take = onehot_rows(place, slots)
    order_col = column(take, order[...].astype(jnp.float32))
    elem_col = column(take, iota((1, elements), 1).astype(jnp.float32) + 1.0)
    slot_col = column(take, slot + 1.0)
    wanted = jnp.concatenate([elem_col + float(f * elements) for f in range(FACES)], axis=0)
    code = (cface[...] * elements + celem[...] + 1).astype(jnp.float32)
    gather = (wanted == code).astype(jnp.bfloat16)
    high, low = halves(conf[...])
    face_sum = dot(gather, high) + dot(gather, low)
    total = restrict_cells(take, order_col, adjoint[...], cell_high, cell_low, cell_spread)
    total = total + restrict_faces(face_sum, order_col, face_high, face_low, face_spread)
    for v in range(VARS):
        part = total[v * slots : (v + 1) * slots]
        out[:, :, v * ROW : (v + 1) * ROW] = part.reshape(peers, row_cap, ROW)
    tags = jnp.concatenate([elem_col, order_col, slot_col], axis=1)
    out[:, :, VARS * ROW : VARS * ROW + 3] = tags.reshape(peers, row_cap, 3)


def finish_kernel(peers, row_cap, elements, get, arrived, face_high, face_low, out, spread):
    rows = peers * row_cap
    traces = get(0)
    block = traces.shape[0] // peers
    x = arrived[...].reshape(rows, arrived.shape[2])
    elem_col, order_col, slot_col = [x[:, VARS * ROW + i : VARS * ROW + i + 1] for i in range(3)]
    source = (iota((rows, 1), 0) // row_cap * elements).astype(jnp.float32)
    wanted = jnp.concatenate([elem_col + source + float(f * peers * elements) for f in range(FACES)], axis=0)
    face_sum = None
    for k in range(peers):
        part = traces[k * block : (k + 1) * block, :]
        gather = (wanted == part[block - 8 : block - 7, :block]).astype(jnp.bfloat16)
        high, low = halves(part)
        add = dot(gather, high) + dot(gather, low)
        face_sum = add if face_sum is None else face_sum + add
    total = restrict_faces(face_sum, order_col, face_high, face_low, spread)
    total = x[:, : VARS * ROW] + jnp.concatenate([total[v * rows : (v + 1) * rows] for v in range(VARS)], axis=1)
    out[...] = place_rows(total, slot_col, elements)


def fetched(kernel, n_far, n_pass, n_near, n_out, *refs):
    far, near, outs = refs[:n_far], refs[n_far : n_far + n_near], refs[n_far + n_near : n_far + n_near + n_out]
    rest = refs[n_far + n_near + n_out :]
    n_held = n_far - n_pass
    held, sems, scratch = rest[:n_held], rest[n_held], rest[n_held + 1 :]
    held = (*held, *outs[n_out - n_pass :])
    copies = [pltpu.make_async_copy(src, dst, sems.at[i]) for i, (src, dst) in enumerate(zip(far, held))]
    for copy in copies:
        copy.start()

    def get(i):
        copies[i].wait()
        return held[i][...]

    kernel(get, *near, *outs[: n_out - n_pass], *scratch)
    for copy in copies[n_held:]:
        copy.wait()


def like(a):
    return jax.ShapeDtypeStruct(a.shape, a.dtype)


def call(kernel, outs, far, near=(), scratch=(), hand_on=(), flops=0):
    outs = [*outs, *[like(a) for a in hand_on]]
    sizes = [np.prod(a.shape) * a.dtype.itemsize for a in (*far, *near, *outs)]
    held = [pltpu.VMEM(a.shape, a.dtype) for a in far]
    far = (*far, *hand_on)
    in_specs = [pl.BlockSpec(memory_space=pltpu.HBM)] * len(far) + [pl.BlockSpec(memory_space=pltpu.VMEM)] * len(near)
    return pl.pallas_call(
        functools.partial(fetched, kernel, len(far), len(hand_on), len(near), len(outs)),
        in_specs=in_specs,
        out_shape=outs,
        scratch_shapes=[*held, pltpu.SemaphoreType.DMA((max(1, len(far)),)), *scratch],
        compiler_params=pltpu.CompilerParams(vmem_limit_bytes=48 * 1024 * 1024),
        cost_estimate=pl.CostEstimate(flops=flops, bytes_accessed=int(sum(sizes)), transcendentals=0),
    )(*[pltpu.with_memory_space_constraint(a, pltpu.HBM) for a in far], *near)


def exchange(block):
    return lax.all_to_all(block, ("gx", "gy"), split_axis=0, concat_axis=0, tiled=True)


def from_behind(block, axis, distance):
    devices = range(lax.axis_size(axis))
    route = [((i - distance) % len(devices), i) for i in devices]
    return lax.ppermute(block, axis, route)


def body(
    adjoint,
    order,
    mortar_trace,
    mortar_sub,
    mortar_dest,
    mortar_elem,
    mortar_face,
    conf_trace,
    conf_elem,
    conf_face,
    coarse_row,
):
    elements = adjoint.shape[0]
    count = mortar_trace.shape[0]
    confs = conf_trace.shape[0]
    peers = lax.axis_size("gx") * lax.axis_size("gy")
    cap = max(2, 2 * count // peers)
    row_cap = max(2, elements // peers)
    slots = peers * row_cap
    assert row_cap <= cap
    lift, cell, face = [tuple(jnp.asarray(t) for t in pair) for pair in basis_tables()]
    f32 = jnp.float32
    line = lambda a: a.reshape(1, -1)
    order, coarse_row = line(order), line(coarse_row)
    whole = (adjoint, order, coarse_row, *cell, *face)
    mortar = (line(mortar_dest), line(mortar_elem), line(mortar_face), line(mortar_sub))
    if peers <= 8:
        conf, conf_elem, conf_face = [from_behind(a, "gz", 1) for a in (conf_trace, line(conf_elem), line(conf_face))]
        lifted, *whole = call(
            functools.partial(lift_kernel, peers, elements),
            [pltpu.HBM((count + 8, LANES), f32)],
            (*mortar, mortar_trace, *lift),
            hand_on=whole,
        )
        lifted = lax.all_gather(lifted, ("gx", "gy"), axis=0, tiled=True)
        (rows,) = call(
            functools.partial(rows_kernel, peers, row_cap),
            [jax.ShapeDtypeStruct((peers, row_cap, ROWS_PAD), f32)],
            (),
            (*whole, conf, conf_elem, conf_face),
            scratch=[
                pltpu.VMEM((2, VARS * slots, CELL_PAD), f32),
                pltpu.VMEM((VARS * slots, FACES * FACE_PAD), f32),
            ],
        )
        (out,) = call(
            functools.partial(finish_kernel, peers, row_cap, elements),
            [jax.ShapeDtypeStruct((elements, VARS * ROW), f32)],
            (lifted,),
            (exchange(rows), *whole[-2:]),
            scratch=[pltpu.VMEM((VARS * slots, FACES * FACE_PAD), f32)],
        )
        return out
    outgoing, conf = call(
        functools.partial(pack_kernel, peers, cap, elements),
        [jax.ShapeDtypeStruct((peers, cap, LANES), f32), jax.ShapeDtypeStruct((confs, LANES), f32)],
        (*mortar, coarse_row, line(conf_face), line(conf_elem), mortar_trace, conf_trace, *lift),
    )
    incoming = exchange(outgoing)
    conf = from_behind(conf, "gz", 1)
    y, cols, *face = call(
        functools.partial(cell_kernel, peers, row_cap),
        [jax.ShapeDtypeStruct((VARS * slots, ROW), f32), jax.ShapeDtypeStruct((slots, 128), f32)],
        (order, coarse_row, adjoint, *cell),
        scratch=[pltpu.VMEM((2, VARS * slots, CELL_PAD), f32)],
        hand_on=face,
    )
    (rows,) = call(
        functools.partial(face_kernel, peers, row_cap, elements),
        [jax.ShapeDtypeStruct((peers, row_cap, VARS * ROW), f32)],
        (),
        (incoming, conf, y, cols, *face),
        scratch=[pltpu.VMEM((VARS * slots, FACES * FACE_PAD), f32)],
    )
    (out,) = call(
        functools.partial(place_kernel, peers, row_cap),
        [jax.ShapeDtypeStruct((elements, VARS * ROW), f32)],
        (),
        (exchange(rows), incoming),
    )
    return out


def solution(mesh):
    rows = P(("gx", "gy", "gz"))
    wide = P(("gx", "gy", "gz"), None)
    return jax.shard_map(
        body,
        mesh=mesh,
        in_specs=(wide, rows, wide, rows, wide, rows, rows, wide, rows, rows, rows),
        out_specs=wide,
        check_vma=False,
    )
```

```python
import functools

import jax
import jax.numpy as jnp
import ml_dtypes
import numpy as np
from jax import lax
from jax.experimental import pallas as pl
from jax.experimental.pallas import tpu as pltpu
from jax.sharding import PartitionSpec as P

VARS = 5
NODE = 7
FACE = NODE * NODE
CELL = NODE * FACE
ROW = 216
FACES = 6
ORDERS = (2, 3, 4, 5, 6)
TRACE = VARS * FACE
TRACE_PAD = 256
FLAT = 36
SENT = VARS * FLAT
CELL_PAD = 384
FACE_PAD = 40
FACES_PAD = 256


def grid_nodes(degree):
    return -np.cos(np.pi * np.arange(degree + 1) / degree)


def lagrange_rows(degree, points):
    anchors = grid_nodes(degree)
    values = np.ones((len(points), degree + 1))
    for k in range(degree + 1):
        for other in range(degree + 1):
            if other != k:
                values[:, k] *= (points - anchors[other]) / (anchors[k] - anchors[other])
    return values


def split_table(table):
    table = np.asarray(table, np.float32)
    high = table.astype(ml_dtypes.bfloat16)
    low = (table - high.astype(np.float32)).astype(ml_dtypes.bfloat16)
    return high, low


@functools.lru_cache(maxsize=None)
def basis_tables():
    top_nodes = grid_nodes(6)
    mortar = [lagrange_rows(6, (top_nodes - 1.0) / 2.0), lagrange_rows(6, (top_nodes + 1.0) / 2.0)]
    flat = lagrange_rows(5, top_nodes)
    lift = np.zeros((5, TRACE_PAD, SENT))
    for sub in range(5):
        both = (mortar[sub // 2] @ flat, mortar[sub % 2] @ flat) if sub < 4 else (flat, flat)
        for v in range(VARS):
            lift[sub, v * FACE : (v + 1) * FACE, v * FLAT : (v + 1) * FLAT] = np.kron(*both)
    cell = np.zeros((len(ORDERS), CELL_PAD, ROW))
    face = np.zeros((len(ORDERS), FACES_PAD, ROW))
    for index, p in enumerate(ORDERS):
        shrink = np.zeros((6, NODE))
        shrink[:p, : p + 1] = lagrange_rows(p - 1, grid_nodes(p)).T
        cell[index, :CELL] = np.einsum("ai,bj,ck->ijkabc", shrink, shrink, shrink).reshape(CELL, ROW)
        lower = np.zeros((6, 6))
        lower[:p] = lagrange_rows(p - 1, grid_nodes(5)).T
        low, high = shrink[:, 0], shrink[:, p]
        for axis, spec in enumerate(("c,ai,bj->ijcab", "c,ai,bj->ijacb", "c,ai,bj->ijabc")):
            for side, edge in enumerate((low, high)):
                first = (2 * axis + side) * FACE_PAD
                face[index, first : first + FLAT] = np.einsum(spec, edge, lower, lower).reshape(FLAT, ROW)
    return (
        split_table(lift.reshape(-1, SENT)),
        split_table(cell.reshape(-1, ROW)),
        split_table(face.reshape(-1, ROW)),
    )


def iota(shape, axis):
    return lax.broadcasted_iota(jnp.int32, shape, axis)


def halves(x):
    high = x.astype(jnp.bfloat16)
    low = (x - high.astype(jnp.float32)).astype(jnp.bfloat16)
    return high, low


def dot(a, b):
    return jnp.dot(a, b, preferred_element_type=jnp.float32)


def dot3(high, low, table_high, table_low):
    return dot(high, table_high) + dot(low, table_high) + dot(high, table_low)


def earlier(member):
    count = member.shape[1]
    before = (iota((count, count), 0) < iota((count, count), 1)).astype(jnp.float32)
    return dot(member.astype(jnp.bfloat16), before.astype(jnp.bfloat16))


def owner_of(crow, peers, elements):
    first = iota((peers, crow.shape[1]), 0) * elements
    return ((crow >= first) & (crow < first + elements)).astype(jnp.float32)


def row_places(crow, peers, elements, stride):
    member = owner_of(crow, peers, elements)
    rank = earlier(member)
    base = iota(member.shape, 0).astype(jnp.float32)
    place = jnp.sum(member * (base * stride + rank), axis=0, keepdims=True)
    slot = crow.astype(jnp.float32) - jnp.sum(member * (base * elements), axis=0, keepdims=True)
    return place, slot


def onehot_rows(place, rows):
    return (iota((rows, place.shape[1]), 0).astype(jnp.float32) == place).astype(jnp.float32)


def column(onehot, values):
    return jnp.sum(onehot * values, axis=1, keepdims=True)


def pad_lanes(x, lanes):
    return jnp.concatenate([x, jnp.zeros((x.shape[0], lanes - x.shape[1]), x.dtype)], axis=1)


def pack_kernel(peers, cap, row_cap, elements, get, out, conf_out):
    dest, elem, face, sub, crow, cface, celem = [get(i) for i in range(7)]
    count, confs = dest.shape[1], cface.shape[1]
    groups, slots = -(-cap // row_cap), peers * row_cap
    member = (iota((peers, count), 0) == dest).astype(jnp.float32)
    rank = jnp.sum(member * earlier(member), axis=0, keepdims=True)
    group = sum([(rank >= float(g * row_cap)).astype(jnp.float32) for g in range(1, groups)], jnp.zeros_like(rank))
    place = group * float(slots - row_cap) + dest.astype(jnp.float32) * float(row_cap) + rank
    put = onehot_rows(place, groups * slots)
    code_col = column(put, (face * elements + elem + 1).astype(jnp.float32))
    row_place, row_slot = row_places(crow, peers, elements, row_cap)
    row_col = column(onehot_rows(row_place, slots), row_slot + 1.0)
    eye = (iota((count, count), 0) == iota((count, count), 1)).astype(jnp.float32)
    sub_col = column(eye, sub.astype(jnp.float32))
    x = pad_lanes(get(7), TRACE_PAD)
    wide = jnp.concatenate([jnp.where(sub_col == float(s), x, 0.0) for s in range(4)], axis=1)
    table_high, table_low = get(9), get(10)
    split = 4 * TRACE_PAD
    lifted = dot3(*halves(wide), table_high[:split], table_low[:split])
    lifted_high, lifted_low = halves(lifted)
    put = put.astype(jnp.bfloat16)
    packed = dot(put, lifted_high) + dot(put, lifted_low)
    for g in range(groups):
        part = packed[g * slots : (g + 1) * slots]
        out[:, :, g * SENT : (g + 1) * SENT] = part.reshape(peers, row_cap, SENT)
    tags = jnp.concatenate([*[code_col[g * slots : (g + 1) * slots] for g in range(groups)], row_col], axis=1)
    out[:, :, groups * SENT : groups * (SENT + 1) + 1] = tags.reshape(peers, row_cap, groups + 1)
    eye = (iota((confs, confs), 0) == iota((confs, confs), 1)).astype(jnp.float32)
    conf_col = column(eye, (cface * elements + celem + 1).astype(jnp.float32))
    conf = dot3(*halves(pad_lanes(get(8), TRACE_PAD)), table_high[split:], table_low[split:])
    conf_out[:, :SENT] = conf
    conf_out[:, SENT : SENT + 1] = conf_col


def cell_kernel(peers, row_cap, get, y_out, col_out, face_high, face_low, spread):
    order, crow = get(0), get(1)
    elements = order.shape[1]
    slots = peers * row_cap
    place, _ = row_places(crow, peers, elements, row_cap)
    take = onehot_rows(place, slots)
    order_col = column(take, order.astype(jnp.float32))
    elem_col = column(take, iota((1, elements), 1).astype(jnp.float32) + 1.0)
    lane = iota((slots, 128), 1)
    col_out[...] = jnp.where(lane == 0, order_col, jnp.where(lane == 1, elem_col, 0.0))
    take = take.astype(jnp.bfloat16)
    spread[...] = jnp.zeros_like(spread)
    for half, part in enumerate(halves(get(2))):
        moved = dot(take, part)
        for v in range(VARS):
            spread[half, v * slots : (v + 1) * slots, :CELL] = moved[:, v * CELL : (v + 1) * CELL]
    order_rows = jnp.concatenate([order_col] * VARS, axis=0)
    high, low = spread[0], spread[1]
    wide_high = jnp.concatenate([jnp.where(order_rows == float(p), high, 0.0).astype(jnp.bfloat16) for p in ORDERS], axis=1)
    wide_low = jnp.concatenate([jnp.where(order_rows == float(p), low, 0.0).astype(jnp.bfloat16) for p in ORDERS], axis=1)
    y_out[...] = dot3(wide_high, wide_low, get(3), get(4))
    face_high[...] = get(5)
    face_low[...] = get(6)


def face_kernel(peers, row_cap, elements, groups, get, incoming, conf, y, cols, table_high, table_low, out, spread):
    slots = peers * row_cap
    message = incoming[...].reshape(slots, incoming.shape[2])
    first_tag = groups * SENT
    x = jnp.concatenate([*[message[:, g * SENT : (g + 1) * SENT] for g in range(groups)], conf[:, :SENT]], axis=0)
    code_col = jnp.concatenate(
        [*[message[:, first_tag + g : first_tag + g + 1] for g in range(groups)], conf[:, SENT : SENT + 1]], axis=0
    )
    count = x.shape[0]
    code_row = jnp.sum(jnp.where(iota((count, count), 0) == iota((count, count), 1), code_col, 0.0), axis=0, keepdims=True)
    order_col, elem_col = cols[:, 0:1], cols[:, 1:2]
    wanted = jnp.concatenate([jnp.where(elem_col > 0.0, elem_col + float(f * elements), -1.0) for f in range(FACES)], axis=0)
    gather = (wanted == code_row).astype(jnp.bfloat16)
    high, low = halves(x)
    face_sum = dot(gather, high) + dot(gather, low)
    spread[...] = jnp.zeros_like(spread)
    for f in range(FACES):
        for v in range(VARS):
            spread[v * slots : (v + 1) * slots, f * FACE_PAD : f * FACE_PAD + FLAT] = face_sum[
                f * slots : (f + 1) * slots, v * FLAT : (v + 1) * FLAT
            ]
    order_rows = jnp.concatenate([order_col] * VARS, axis=0)
    z = spread[...]
    wide = jnp.concatenate([jnp.where(order_rows == float(p), z, 0.0) for p in ORDERS], axis=1)
    high, low = halves(wide)
    total = y[...] + dot3(high, low, table_high[...], table_low[...])
    for v in range(VARS):
        out[:, :, v * ROW : (v + 1) * ROW] = total[v * slots : (v + 1) * slots].reshape(peers, row_cap, ROW)


def place_kernel(peers, row_cap, tag, get, arrived, message, out):
    elements = out.shape[0]
    rows = peers * row_cap
    x = arrived[...].reshape(rows, arrived.shape[2])
    slot_col = message[:, :, tag : tag + 1].reshape(rows, 1)
    slot_row = jnp.sum(jnp.where(iota((rows, rows), 0) == iota((rows, rows), 1), slot_col, 0.0), axis=0, keepdims=True)
    put = (iota((elements, rows), 0).astype(jnp.float32) + 1.0 == slot_row).astype(jnp.bfloat16)
    high, low = halves(x)
    rest = (x - high.astype(jnp.float32) - low.astype(jnp.float32)).astype(jnp.bfloat16)
    out[...] = dot(put, high) + dot(put, low) + dot(put, rest)


def fetched(kernel, n_far, n_near, n_out, *refs):
    far, near, outs = refs[:n_far], refs[n_far : n_far + n_near], refs[n_far + n_near : n_far + n_near + n_out]
    rest = refs[n_far + n_near + n_out :]
    held, sems, scratch = rest[:n_far], rest[n_far], rest[n_far + 1 :]
    copies = [pltpu.make_async_copy(src, dst, sems.at[i]) for i, (src, dst) in enumerate(zip(far, held))]
    for copy in copies:
        copy.start()

    def get(i):
        copies[i].wait()
        return held[i][...]

    kernel(get, *near, *outs, *scratch)


def call(kernel, outs, far, near=(), scratch=(), flops=0):
    shapes = jax.tree.leaves(outs)
    sizes = [np.prod(a.shape) * a.dtype.itemsize for a in (*far, *near, *shapes)]
    in_specs = [pl.BlockSpec(memory_space=pltpu.HBM)] * len(far) + [pl.BlockSpec(memory_space=pltpu.VMEM)] * len(near)
    scratch = [*[pltpu.VMEM(a.shape, a.dtype) for a in far], pltpu.SemaphoreType.DMA((max(1, len(far)),)), *scratch]
    return pl.pallas_call(
        functools.partial(fetched, kernel, len(far), len(near), len(shapes)),
        in_specs=in_specs,
        out_shape=outs,
        scratch_shapes=scratch,
        compiler_params=pltpu.CompilerParams(vmem_limit_bytes=48 * 1024 * 1024),
        cost_estimate=pl.CostEstimate(flops=flops, bytes_accessed=int(sum(sizes)), transcendentals=0),
    )(*[pltpu.with_memory_space_constraint(a, pltpu.HBM) for a in far], *near)


def exchange(block):
    return lax.all_to_all(block, ("gx", "gy"), split_axis=0, concat_axis=0, tiled=True)


def from_behind(block, axis, distance):
    devices = range(lax.axis_size(axis))
    route = [((i - distance) % len(devices), i) for i in devices]
    return lax.ppermute(block, axis, route)


def body(
    adjoint,
    order,
    mortar_trace,
    mortar_sub,
    mortar_dest,
    mortar_elem,
    mortar_face,
    conf_trace,
    conf_elem,
    conf_face,
    coarse_row,
):
    elements = adjoint.shape[0]
    count = mortar_trace.shape[0]
    confs = conf_trace.shape[0]
    peers = lax.axis_size("gx") * lax.axis_size("gy")
    cap = max(2, 2 * count // peers)
    row_cap = max(2, elements // peers)
    slots = peers * row_cap
    groups = -(-cap // row_cap)
    lanes = -(-(groups * (SENT + 1) + 1) // 128) * 128
    lift, cell, face = [tuple(jnp.asarray(t) for t in pair) for pair in basis_tables()]
    f32 = jnp.float32
    line = lambda a: a.reshape(1, -1)
    order, coarse_row = line(order), line(coarse_row)
    outgoing, conf = call(
        functools.partial(pack_kernel, peers, cap, row_cap, elements),
        (jax.ShapeDtypeStruct((peers, row_cap, lanes), f32), jax.ShapeDtypeStruct((confs, TRACE_PAD), f32)),
        (
            line(mortar_dest),
            line(mortar_elem),
            line(mortar_face),
            line(mortar_sub),
            coarse_row,
            line(conf_face),
            line(conf_elem),
            mortar_trace,
            conf_trace,
            *lift,
        ),
    )
    incoming = exchange(outgoing)
    conf = from_behind(conf, "gz", 1)
    y, cols, *face = call(
        functools.partial(cell_kernel, peers, row_cap),
        (
            jax.ShapeDtypeStruct((VARS * slots, ROW), f32),
            jax.ShapeDtypeStruct((slots, 128), f32),
            *[jax.ShapeDtypeStruct(t.shape, t.dtype) for t in face],
        ),
        (order, coarse_row, adjoint, *cell, *face),
        scratch=[pltpu.VMEM((2, VARS * slots, CELL_PAD), f32)],
    )
    rows = call(
        functools.partial(face_kernel, peers, row_cap, elements, groups),
        jax.ShapeDtypeStruct((peers, row_cap, VARS * ROW), f32),
        (),
        (incoming, conf, y, cols, *face),
        scratch=[pltpu.VMEM((VARS * slots, FACES_PAD), f32)],
    )
    arrived = exchange(rows)
    return call(
        functools.partial(place_kernel, peers, row_cap, groups * (SENT + 1)),
        jax.ShapeDtypeStruct((elements, VARS * ROW), f32),
        (),
        (arrived, incoming),
    )


def solution(mesh):
    rows = P(("gx", "gy", "gz"))
    wide = P(("gx", "gy", "gz"), None)
    return jax.shard_map(
        body,
        mesh=mesh,
        in_specs=(wide, rows, wide, rows, wide, rows, rows, wide, rows, rows, rows),
        out_specs=wide,
        check_vma=False,
    )
```

```python
import functools

import jax
import jax.numpy as jnp
import ml_dtypes
import numpy as np
from jax import lax
from jax.experimental import pallas as pl
from jax.experimental.pallas import tpu as pltpu
from jax.sharding import PartitionSpec as P

VARS = 5
NODE = 7
FACE = NODE * NODE
CELL = NODE * FACE
ROW = 216
FACES = 6
ORDERS = (2, 3, 4, 5, 6)
TRACE = VARS * FACE
TRACE_PAD = 256
FLAT = 36
SENT = VARS * FLAT
CELL_PAD = 384
FACE_PAD = 40
FACES_PAD = 256


def grid_nodes(degree):
    return -np.cos(np.pi * np.arange(degree + 1) / degree)


def lagrange_rows(degree, points):
    anchors = grid_nodes(degree)
    values = np.ones((len(points), degree + 1))
    for k in range(degree + 1):
        for other in range(degree + 1):
            if other != k:
                values[:, k] *= (points - anchors[other]) / (anchors[k] - anchors[other])
    return values


def split_table(table):
    table = np.asarray(table, np.float32)
    high = table.astype(ml_dtypes.bfloat16)
    low = (table - high.astype(np.float32)).astype(ml_dtypes.bfloat16)
    return high, low


@functools.lru_cache(maxsize=None)
def basis_tables():
    top_nodes = grid_nodes(6)
    mortar = [lagrange_rows(6, (top_nodes - 1.0) / 2.0), lagrange_rows(6, (top_nodes + 1.0) / 2.0)]
    flat = lagrange_rows(5, top_nodes)
    lift = np.zeros((5, TRACE_PAD, SENT))
    for sub in range(5):
        both = (mortar[sub // 2] @ flat, mortar[sub % 2] @ flat) if sub < 4 else (flat, flat)
        for v in range(VARS):
            lift[sub, v * FACE : (v + 1) * FACE, v * FLAT : (v + 1) * FLAT] = np.kron(*both)
    cell = np.zeros((len(ORDERS), CELL_PAD, ROW))
    face = np.zeros((len(ORDERS), FACES_PAD, ROW))
    for index, p in enumerate(ORDERS):
        shrink = np.zeros((6, NODE))
        shrink[:p, : p + 1] = lagrange_rows(p - 1, grid_nodes(p)).T
        cell[index, :CELL] = np.einsum("ai,bj,ck->ijkabc", shrink, shrink, shrink).reshape(CELL, ROW)
        lower = np.zeros((6, 6))
        lower[:p] = lagrange_rows(p - 1, grid_nodes(5)).T
        low, high = shrink[:, 0], shrink[:, p]
        for axis, spec in enumerate(("c,ai,bj->ijcab", "c,ai,bj->ijacb", "c,ai,bj->ijabc")):
            for side, edge in enumerate((low, high)):
                first = (2 * axis + side) * FACE_PAD
                face[index, first : first + FLAT] = np.einsum(spec, edge, lower, lower).reshape(FLAT, ROW)
    return (
        split_table(lift.reshape(-1, SENT)),
        split_table(cell.reshape(-1, ROW)),
        split_table(face.reshape(-1, ROW)),
    )


def iota(shape, axis):
    return lax.broadcasted_iota(jnp.int32, shape, axis)


def halves(x):
    high = x.astype(jnp.bfloat16)
    low = (x - high.astype(jnp.float32)).astype(jnp.bfloat16)
    return high, low


def dot(a, b):
    return jnp.dot(a, b, preferred_element_type=jnp.float32)


def dot3(high, low, table_high, table_low):
    return dot(high, table_high) + dot(low, table_high) + dot(high, table_low)


def earlier(member):
    count = member.shape[1]
    before = (iota((count, count), 0) < iota((count, count), 1)).astype(jnp.float32)
    return dot(member.astype(jnp.bfloat16), before.astype(jnp.bfloat16))


def owner_of(crow, peers, elements):
    first = iota((peers, crow.shape[1]), 0) * elements
    return ((crow >= first) & (crow < first + elements)).astype(jnp.float32)


def row_places(crow, peers, elements, stride):
    member = owner_of(crow, peers, elements)
    rank = earlier(member)
    base = iota(member.shape, 0).astype(jnp.float32)
    place = jnp.sum(member * (base * stride + rank), axis=0, keepdims=True)
    slot = crow.astype(jnp.float32) - jnp.sum(member * (base * elements), axis=0, keepdims=True)
    return place, slot


def onehot_rows(place, rows):
    return (iota((rows, place.shape[1]), 0).astype(jnp.float32) == place).astype(jnp.float32)


def column(onehot, values):
    return jnp.sum(onehot * values, axis=1, keepdims=True)


def pad_lanes(x, lanes):
    return jnp.concatenate([x, jnp.zeros((x.shape[0], lanes - x.shape[1]), x.dtype)], axis=1)


def pack_kernel(peers, cap, row_cap, elements, get, out, conf_out):
    dest, elem, face, sub, crow, cface, celem = [get(i) for i in range(7)]
    count, confs = dest.shape[1], cface.shape[1]
    groups, slots = -(-cap // row_cap), peers * row_cap
    member = (iota((peers, count), 0) == dest).astype(jnp.float32)
    rank = jnp.sum(member * earlier(member), axis=0, keepdims=True)
    group = sum([(rank >= float(g * row_cap)).astype(jnp.float32) for g in range(1, groups)], jnp.zeros_like(rank))
    place = group * float(slots - row_cap) + dest.astype(jnp.float32) * float(row_cap) + rank
    put = onehot_rows(place, groups * slots)
    code_col = column(put, (face * elements + elem + 1).astype(jnp.float32))
    row_place, row_slot = row_places(crow, peers, elements, row_cap)
    row_col = column(onehot_rows(row_place, slots), row_slot + 1.0)
    eye = (iota((count, count), 0) == iota((count, count), 1)).astype(jnp.float32)
    sub_col = column(eye, sub.astype(jnp.float32))
    x = pad_lanes(get(7), TRACE_PAD)
    wide = jnp.concatenate([jnp.where(sub_col == float(s), x, 0.0) for s in range(4)], axis=1)
    table_high, table_low = get(9), get(10)
    split = 4 * TRACE_PAD
    lifted = dot3(*halves(wide), table_high[:split], table_low[:split])
    lifted_high, lifted_low = halves(lifted)
    put = put.astype(jnp.bfloat16)
    packed = dot(put, lifted_high) + dot(put, lifted_low)
    for g in range(groups):
        part = packed[g * slots : (g + 1) * slots]
        out[:, :, g * SENT : (g + 1) * SENT] = part.reshape(peers, row_cap, SENT)
    tags = jnp.concatenate([*[code_col[g * slots : (g + 1) * slots] for g in range(groups)], row_col], axis=1)
    out[:, :, groups * SENT : groups * (SENT + 1) + 1] = tags.reshape(peers, row_cap, groups + 1)
    eye = (iota((confs, confs), 0) == iota((confs, confs), 1)).astype(jnp.float32)
    conf_col = column(eye, (cface * elements + celem + 1).astype(jnp.float32))
    conf = dot3(*halves(pad_lanes(get(8), TRACE_PAD)), table_high[split:], table_low[split:])
    conf_out[:, :SENT] = conf
    conf_out[:, SENT : SENT + 1] = conf_col


def restrict_cells(take, order_col, adjoint, table_high, table_low, spread):
    slots = take.shape[0]
    take = take.astype(jnp.bfloat16)
    spread[...] = jnp.zeros_like(spread)
    for half, part in enumerate(halves(adjoint)):
        moved = dot(take, part)
        for v in range(VARS):
            spread[half, v * slots : (v + 1) * slots, :CELL] = moved[:, v * CELL : (v + 1) * CELL]
    order_rows = jnp.concatenate([order_col] * VARS, axis=0)
    wide = [
        jnp.concatenate([jnp.where(order_rows == float(p), spread[half], 0.0).astype(jnp.bfloat16) for p in ORDERS], axis=1)
        for half in range(2)
    ]
    return dot3(*wide, table_high[...], table_low[...])


def restrict_faces(face_sum, order_col, table_high, table_low, spread):
    slots = order_col.shape[0]
    spread[...] = jnp.zeros_like(spread)
    for f in range(FACES):
        for v in range(VARS):
            spread[v * slots : (v + 1) * slots, f * FACE_PAD : f * FACE_PAD + FLAT] = face_sum[
                f * slots : (f + 1) * slots, v * FLAT : (v + 1) * FLAT
            ]
    order_rows = jnp.concatenate([order_col] * VARS, axis=0)
    z = spread[...]
    wide = jnp.concatenate([jnp.where(order_rows == float(p), z, 0.0) for p in ORDERS], axis=1)
    high, low = halves(wide)
    return dot3(high, low, table_high[...], table_low[...])


def rows_kernel(
    peers,
    row_cap,
    elements,
    groups,
    get,
    order,
    crow,
    adjoint,
    cell_high,
    cell_low,
    face_high,
    face_low,
    incoming,
    conf,
    out,
    cell_spread,
    face_spread,
):
    slots = peers * row_cap
    place, _ = row_places(crow[...], peers, elements, row_cap)
    take = onehot_rows(place, slots)
    order_col = column(take, order[...].astype(jnp.float32))
    elem_col = column(take, iota((1, elements), 1).astype(jnp.float32) + 1.0)
    total = restrict_cells(take, order_col, adjoint[...], cell_high, cell_low, cell_spread)
    message = incoming[...].reshape(slots, incoming.shape[2])
    first_tag = groups * SENT
    x = jnp.concatenate([*[message[:, g * SENT : (g + 1) * SENT] for g in range(groups)], conf[:, :SENT]], axis=0)
    code_col = jnp.concatenate(
        [*[message[:, first_tag + g : first_tag + g + 1] for g in range(groups)], conf[:, SENT : SENT + 1]], axis=0
    )
    count = x.shape[0]
    code_row = jnp.sum(jnp.where(iota((count, count), 0) == iota((count, count), 1), code_col, 0.0), axis=0, keepdims=True)
    wanted = jnp.concatenate([jnp.where(elem_col > 0.0, elem_col + float(f * elements), -1.0) for f in range(FACES)], axis=0)
    gather = (wanted == code_row).astype(jnp.bfloat16)
    high, low = halves(x)
    face_sum = dot(gather, high) + dot(gather, low)
    total = total + restrict_faces(face_sum, order_col, face_high, face_low, face_spread)
    for v in range(VARS):
        out[:, :, v * ROW : (v + 1) * ROW] = total[v * slots : (v + 1) * slots].reshape(peers, row_cap, ROW)


def place_kernel(peers, row_cap, tag, get, arrived, message, out):
    elements = out.shape[0]
    rows = peers * row_cap
    x = arrived[...].reshape(rows, arrived.shape[2])
    slot_col = message[:, :, tag : tag + 1].reshape(rows, 1)
    slot_row = jnp.sum(jnp.where(iota((rows, rows), 0) == iota((rows, rows), 1), slot_col, 0.0), axis=0, keepdims=True)
    put = (iota((elements, rows), 0).astype(jnp.float32) + 1.0 == slot_row).astype(jnp.bfloat16)
    high, low = halves(x)
    rest = (x - high.astype(jnp.float32) - low.astype(jnp.float32)).astype(jnp.bfloat16)
    out[...] = dot(put, high) + dot(put, low) + dot(put, rest)


def fetched(kernel, n_far, n_pass, n_near, n_out, *refs):
    far, near, outs = refs[:n_far], refs[n_far : n_far + n_near], refs[n_far + n_near : n_far + n_near + n_out]
    rest = refs[n_far + n_near + n_out :]
    n_held = n_far - n_pass
    held, sems, scratch = rest[:n_held], rest[n_held], rest[n_held + 1 :]
    held = (*held, *outs[n_out - n_pass :])
    copies = [pltpu.make_async_copy(src, dst, sems.at[i]) for i, (src, dst) in enumerate(zip(far, held))]
    for copy in copies:
        copy.start()

    def get(i):
        copies[i].wait()
        return held[i][...]

    kernel(get, *near, *outs[: n_out - n_pass], *scratch)
    for copy in copies[n_held:]:
        copy.wait()


def like(a):
    return jax.ShapeDtypeStruct(a.shape, a.dtype)


def call(kernel, outs, far, near=(), scratch=(), hand_on=(), flops=0):
    outs = [*outs, *[like(a) for a in hand_on]]
    sizes = [np.prod(a.shape) * a.dtype.itemsize for a in (*far, *near, *outs)]
    held = [pltpu.VMEM(a.shape, a.dtype) for a in far]
    far = (*far, *hand_on)
    in_specs = [pl.BlockSpec(memory_space=pltpu.HBM)] * len(far) + [pl.BlockSpec(memory_space=pltpu.VMEM)] * len(near)
    return pl.pallas_call(
        functools.partial(fetched, kernel, len(far), len(hand_on), len(near), len(outs)),
        in_specs=in_specs,
        out_shape=outs,
        scratch_shapes=[*held, pltpu.SemaphoreType.DMA((max(1, len(far)),)), *scratch],
        compiler_params=pltpu.CompilerParams(vmem_limit_bytes=48 * 1024 * 1024),
        cost_estimate=pl.CostEstimate(flops=flops, bytes_accessed=int(sum(sizes)), transcendentals=0),
    )(*[pltpu.with_memory_space_constraint(a, pltpu.HBM) for a in far], *near)


def exchange(block):
    return lax.all_to_all(block, ("gx", "gy"), split_axis=0, concat_axis=0, tiled=True)


def from_behind(block, axis, distance):
    devices = range(lax.axis_size(axis))
    route = [((i - distance) % len(devices), i) for i in devices]
    return lax.ppermute(block, axis, route)


def body(
    adjoint,
    order,
    mortar_trace,
    mortar_sub,
    mortar_dest,
    mortar_elem,
    mortar_face,
    conf_trace,
    conf_elem,
    conf_face,
    coarse_row,
):
    elements = adjoint.shape[0]
    count = mortar_trace.shape[0]
    confs = conf_trace.shape[0]
    peers = lax.axis_size("gx") * lax.axis_size("gy")
    cap = max(2, 2 * count // peers)
    row_cap = max(2, elements // peers)
    slots = peers * row_cap
    groups = -(-cap // row_cap)
    lanes = -(-(groups * (SENT + 1) + 1) // 128) * 128
    lift, cell, face = [tuple(jnp.asarray(t) for t in pair) for pair in basis_tables()]
    f32 = jnp.float32
    line = lambda a: a.reshape(1, -1)
    order, coarse_row = line(order), line(coarse_row)
    outgoing, conf, *whole = call(
        functools.partial(pack_kernel, peers, cap, row_cap, elements),
        [jax.ShapeDtypeStruct((peers, row_cap, lanes), f32), jax.ShapeDtypeStruct((confs, TRACE_PAD), f32)],
        (
            line(mortar_dest),
            line(mortar_elem),
            line(mortar_face),
            line(mortar_sub),
            coarse_row,
            line(conf_face),
            line(conf_elem),
            mortar_trace,
            conf_trace,
            *lift,
        ),
        hand_on=(order, coarse_row, adjoint, *cell, *face),
    )
    conf = from_behind(conf, "gz", 1)
    incoming = exchange(outgoing)
    (rows,) = call(
        functools.partial(rows_kernel, peers, row_cap, elements, groups),
        [jax.ShapeDtypeStruct((peers, row_cap, VARS * ROW), f32)],
        (),
        (*whole, incoming, conf),
        scratch=[pltpu.VMEM((2, VARS * slots, CELL_PAD), f32), pltpu.VMEM((VARS * slots, FACES_PAD), f32)],
    )
    (out,) = call(
        functools.partial(place_kernel, peers, row_cap, groups * (SENT + 1)),
        [jax.ShapeDtypeStruct((elements, VARS * ROW), f32)],
        (),
        (exchange(rows), incoming),
    )
    return out


def solution(mesh):
    rows = P(("gx", "gy", "gz"))
    wide = P(("gx", "gy", "gz"), None)
    return jax.shard_map(
        body,
        mesh=mesh,
        in_specs=(wide, rows, wide, rows, wide, rows, rows, wide, rows, rows, rows),
        out_specs=wide,
        check_vma=False,
    )
```

```python
import functools

import jax
import jax.numpy as jnp
import ml_dtypes
import numpy as np
from jax import lax
from jax.experimental import pallas as pl
from jax.experimental.pallas import tpu as pltpu
from jax.sharding import PartitionSpec as P

VARS = 5
NODE = 7
FACE = NODE * NODE
CELL = NODE * FACE
ROW = 216
FACES = 6
ORDERS = (2, 3, 4, 5, 6)
TRACE = VARS * FACE
TRACE_PAD = 256
FLAT = 36
SENT = VARS * FLAT
CELL_PAD = 384
FACE_PAD = 40
FACES_PAD = 256


def grid_nodes(degree):
    return -np.cos(np.pi * np.arange(degree + 1) / degree)


def lagrange_rows(degree, points):
    anchors = grid_nodes(degree)
    values = np.ones((len(points), degree + 1))
    for k in range(degree + 1):
        for other in range(degree + 1):
            if other != k:
                values[:, k] *= (points - anchors[other]) / (anchors[k] - anchors[other])
    return values


def split_table(table):
    table = np.asarray(table, np.float32)
    high = table.astype(ml_dtypes.bfloat16)
    low = (table - high.astype(np.float32)).astype(ml_dtypes.bfloat16)
    return high, low


@functools.lru_cache(maxsize=None)
def basis_tables():
    top_nodes = grid_nodes(6)
    mortar = [lagrange_rows(6, (top_nodes - 1.0) / 2.0), lagrange_rows(6, (top_nodes + 1.0) / 2.0)]
    flat = lagrange_rows(5, top_nodes)
    lift = np.zeros((5, TRACE_PAD, SENT))
    for sub in range(5):
        both = (mortar[sub // 2] @ flat, mortar[sub % 2] @ flat) if sub < 4 else (flat, flat)
        for v in range(VARS):
            lift[sub, v * FACE : (v + 1) * FACE, v * FLAT : (v + 1) * FLAT] = np.kron(*both)
    cell = np.zeros((len(ORDERS), CELL_PAD, ROW))
    face = np.zeros((len(ORDERS), FACES_PAD, ROW))
    for index, p in enumerate(ORDERS):
        shrink = np.zeros((6, NODE))
        shrink[:p, : p + 1] = lagrange_rows(p - 1, grid_nodes(p)).T
        cell[index, :CELL] = np.einsum("ai,bj,ck->ijkabc", shrink, shrink, shrink).reshape(CELL, ROW)
        lower = np.zeros((6, 6))
        lower[:p] = lagrange_rows(p - 1, grid_nodes(5)).T
        low, high = shrink[:, 0], shrink[:, p]
        for axis, spec in enumerate(("c,ai,bj->ijcab", "c,ai,bj->ijacb", "c,ai,bj->ijabc")):
            for side, edge in enumerate((low, high)):
                first = (2 * axis + side) * FACE_PAD
                face[index, first : first + FLAT] = np.einsum(spec, edge, lower, lower).reshape(FLAT, ROW)
    return (
        split_table(lift[:4].reshape(-1, SENT)),
        split_table(lift[4]),
        split_table(cell.reshape(-1, ROW)),
        split_table(face.reshape(-1, ROW)),
    )


def iota(shape, axis):
    return lax.broadcasted_iota(jnp.int32, shape, axis)


def halves(x):
    high = x.astype(jnp.bfloat16)
    low = (x - high.astype(jnp.float32)).astype(jnp.bfloat16)
    return high, low


def dot(a, b):
    return jnp.dot(a, b, preferred_element_type=jnp.float32)


def dot3(high, low, table_high, table_low):
    return dot(high, table_high) + dot(low, table_high) + dot(high, table_low)


def earlier(member):
    count = member.shape[1]
    before = (iota((count, count), 0) < iota((count, count), 1)).astype(jnp.float32)
    return dot(member.astype(jnp.bfloat16), before.astype(jnp.bfloat16))


def owner_of(crow, peers, elements):
    first = iota((peers, crow.shape[1]), 0) * elements
    return ((crow >= first) & (crow < first + elements)).astype(jnp.float32)


def row_places(crow, peers, elements, stride):
    member = owner_of(crow, peers, elements)
    rank = earlier(member)
    base = iota(member.shape, 0).astype(jnp.float32)
    place = jnp.sum(member * (base * stride + rank), axis=0, keepdims=True)
    slot = crow.astype(jnp.float32) - jnp.sum(member * (base * elements), axis=0, keepdims=True)
    return place, slot


def onehot_rows(place, rows):
    return (iota((rows, place.shape[1]), 0).astype(jnp.float32) == place).astype(jnp.float32)


def column(onehot, values):
    return jnp.sum(onehot * values, axis=1, keepdims=True)


def pad_lanes(x, lanes):
    return jnp.concatenate([x, jnp.zeros((x.shape[0], lanes - x.shape[1]), x.dtype)], axis=1)


def conf_kernel(elements, get, out):
    cface, celem = get(0), get(1)
    confs = cface.shape[1]
    eye = (iota((confs, confs), 0) == iota((confs, confs), 1)).astype(jnp.float32)
    code_col = column(eye, (cface * elements + celem + 1).astype(jnp.float32))
    out[...] = jnp.where(iota((confs, TRACE_PAD), 1) == TRACE, code_col, pad_lanes(get(2), TRACE_PAD))


def pack_kernel(peers, cap, row_cap, elements, get, *refs):
    *ints, trace, table_high, table_low, out = refs
    dest, elem, face, sub, crow = [ref[...] for ref in ints]
    count = dest.shape[1]
    groups, slots = -(-cap // row_cap), peers * row_cap
    member = (iota((peers, count), 0) == dest).astype(jnp.float32)
    rank = jnp.sum(member * earlier(member), axis=0, keepdims=True)
    group = sum([(rank >= float(g * row_cap)).astype(jnp.float32) for g in range(1, groups)], jnp.zeros_like(rank))
    place = group * float(slots - row_cap) + dest.astype(jnp.float32) * float(row_cap) + rank
    put = onehot_rows(place, groups * slots)
    code_col = column(put, (face * elements + elem + 1).astype(jnp.float32))
    row_place, row_slot = row_places(crow, peers, elements, row_cap)
    row_col = column(onehot_rows(row_place, slots), row_slot + 1.0)
    eye = (iota((count, count), 0) == iota((count, count), 1)).astype(jnp.float32)
    sub_col = column(eye, sub.astype(jnp.float32))
    x = pad_lanes(trace[...], TRACE_PAD)
    wide = jnp.concatenate([jnp.where(sub_col == float(s), x, 0.0) for s in range(4)], axis=1)
    lifted = dot3(*halves(wide), table_high[...], table_low[...])
    lifted_high, lifted_low = halves(lifted)
    put = put.astype(jnp.bfloat16)
    packed = dot(put, lifted_high) + dot(put, lifted_low)
    for g in range(groups):
        part = packed[g * slots : (g + 1) * slots]
        out[:, :, g * SENT : (g + 1) * SENT] = part.reshape(peers, row_cap, SENT)
    tags = jnp.concatenate([*[code_col[g * slots : (g + 1) * slots] for g in range(groups)], row_col], axis=1)
    out[:, :, groups * SENT : groups * (SENT + 1) + 1] = tags.reshape(peers, row_cap, groups + 1)


def cell_kernel(peers, row_cap, get, conf, y_out, col_out, conf_out, spread):
    order, crow = get(0), get(1)
    elements = order.shape[1]
    slots = peers * row_cap
    place, _ = row_places(crow, peers, elements, row_cap)
    take = onehot_rows(place, slots)
    order_col = column(take, order.astype(jnp.float32))
    elem_col = column(take, iota((1, elements), 1).astype(jnp.float32) + 1.0)
    lane = iota((slots, 128), 1)
    col_out[...] = jnp.where(lane == 0, order_col, jnp.where(lane == 1, elem_col, 0.0))
    take = take.astype(jnp.bfloat16)
    spread[...] = jnp.zeros_like(spread)
    for half, part in enumerate(halves(get(2))):
        moved = dot(take, part)
        for v in range(VARS):
            spread[half, v * slots : (v + 1) * slots, :CELL] = moved[:, v * CELL : (v + 1) * CELL]
    order_rows = jnp.concatenate([order_col] * VARS, axis=0)
    high, low = spread[0], spread[1]
    wide_high = jnp.concatenate([jnp.where(order_rows == float(p), high, 0.0).astype(jnp.bfloat16) for p in ORDERS], axis=1)
    wide_low = jnp.concatenate([jnp.where(order_rows == float(p), low, 0.0).astype(jnp.bfloat16) for p in ORDERS], axis=1)
    y_out[...] = dot3(wide_high, wide_low, get(3), get(4))
    conf_out[:, :SENT] = dot3(*halves(conf[...]), get(5), get(6))
    conf_out[:, SENT : SENT + 1] = conf[:, TRACE : TRACE + 1]


def face_kernel(peers, row_cap, elements, groups, get, incoming, conf, y, cols, table_high, table_low, out, spread):
    slots = peers * row_cap
    message = incoming[...].reshape(slots, incoming.shape[2])
    first_tag = groups * SENT
    x = jnp.concatenate([*[message[:, g * SENT : (g + 1) * SENT] for g in range(groups)], conf[:, :SENT]], axis=0)
    code_col = jnp.concatenate(
        [*[message[:, first_tag + g : first_tag + g + 1] for g in range(groups)], conf[:, SENT : SENT + 1]], axis=0
    )
    count = x.shape[0]
    code_row = jnp.sum(jnp.where(iota((count, count), 0) == iota((count, count), 1), code_col, 0.0), axis=0, keepdims=True)
    order_col, elem_col = cols[:, 0:1], cols[:, 1:2]
    wanted = jnp.concatenate([jnp.where(elem_col > 0.0, elem_col + float(f * elements), -1.0) for f in range(FACES)], axis=0)
    gather = (wanted == code_row).astype(jnp.bfloat16)
    high, low = halves(x)
    face_sum = dot(gather, high) + dot(gather, low)
    spread[...] = jnp.zeros_like(spread)
    for f in range(FACES):
        for v in range(VARS):
            spread[v * slots : (v + 1) * slots, f * FACE_PAD : f * FACE_PAD + FLAT] = face_sum[
                f * slots : (f + 1) * slots, v * FLAT : (v + 1) * FLAT
            ]
    order_rows = jnp.concatenate([order_col] * VARS, axis=0)
    z = spread[...]
    wide = jnp.concatenate([jnp.where(order_rows == float(p), z, 0.0) for p in ORDERS], axis=1)
    high, low = halves(wide)
    total = y[...] + dot3(high, low, table_high[...], table_low[...])
    for v in range(VARS):
        out[:, :, v * ROW : (v + 1) * ROW] = total[v * slots : (v + 1) * slots].reshape(peers, row_cap, ROW)


def place_kernel(peers, row_cap, tag, get, arrived, message, out):
    elements = out.shape[0]
    rows = peers * row_cap
    x = arrived[...].reshape(rows, arrived.shape[2])
    slot_col = message[:, :, tag : tag + 1].reshape(rows, 1)
    slot_row = jnp.sum(jnp.where(iota((rows, rows), 0) == iota((rows, rows), 1), slot_col, 0.0), axis=0, keepdims=True)
    put = (iota((elements, rows), 0).astype(jnp.float32) + 1.0 == slot_row).astype(jnp.bfloat16)
    high, low = halves(x)
    rest = (x - high.astype(jnp.float32) - low.astype(jnp.float32)).astype(jnp.bfloat16)
    out[...] = dot(put, high) + dot(put, low) + dot(put, rest)


def fetched(kernel, n_far, n_pass, n_near, n_out, *refs):
    far, near, outs = refs[:n_far], refs[n_far : n_far + n_near], refs[n_far + n_near : n_far + n_near + n_out]
    rest = refs[n_far + n_near + n_out :]
    n_held = n_far - n_pass
    held, sems, scratch = rest[:n_held], rest[n_held], rest[n_held + 1 :]
    held = (*held, *outs[n_out - n_pass :])
    copies = [pltpu.make_async_copy(src, dst, sems.at[i]) for i, (src, dst) in enumerate(zip(far, held))]
    for copy in copies:
        copy.start()

    def get(i):
        copies[i].wait()
        return held[i][...]

    kernel(get, *near, *outs[: n_out - n_pass], *scratch)
    for copy in copies[n_held:]:
        copy.wait()


def like(a):
    return jax.ShapeDtypeStruct(a.shape, a.dtype)


def call(kernel, outs, far, near=(), scratch=(), hand_on=(), flops=0):
    outs = [*outs, *[like(a) for a in hand_on]]
    sizes = [np.prod(a.shape) * a.dtype.itemsize for a in (*far, *near, *outs)]
    held = [pltpu.VMEM(a.shape, a.dtype) for a in far]
    far = (*far, *hand_on)
    in_specs = [pl.BlockSpec(memory_space=pltpu.HBM)] * len(far) + [pl.BlockSpec(memory_space=pltpu.VMEM)] * len(near)
    return pl.pallas_call(
        functools.partial(fetched, kernel, len(far), len(hand_on), len(near), len(outs)),
        in_specs=in_specs,
        out_shape=outs,
        scratch_shapes=[*held, pltpu.SemaphoreType.DMA((max(1, len(far)),)), *scratch],
        compiler_params=pltpu.CompilerParams(vmem_limit_bytes=48 * 1024 * 1024),
        cost_estimate=pl.CostEstimate(flops=flops, bytes_accessed=int(sum(sizes)), transcendentals=0),
    )(*[pltpu.with_memory_space_constraint(a, pltpu.HBM) for a in far], *near)


def exchange(block):
    return lax.all_to_all(block, ("gx", "gy"), split_axis=0, concat_axis=0, tiled=True)


def from_behind(block, axis, distance):
    devices = range(lax.axis_size(axis))
    route = [((i - distance) % len(devices), i) for i in devices]
    return lax.ppermute(block, axis, route)


def body(
    adjoint,
    order,
    mortar_trace,
    mortar_sub,
    mortar_dest,
    mortar_elem,
    mortar_face,
    conf_trace,
    conf_elem,
    conf_face,
    coarse_row,
):
    elements = adjoint.shape[0]
    count = mortar_trace.shape[0]
    confs = conf_trace.shape[0]
    peers = lax.axis_size("gx") * lax.axis_size("gy")
    cap = max(2, 2 * count // peers)
    row_cap = max(2, elements // peers)
    slots = peers * row_cap
    groups = -(-cap // row_cap)
    lanes = -(-(groups * (SENT + 1) + 1) // 128) * 128
    lift, conf_lift, cell, face = [tuple(jnp.asarray(t) for t in pair) for pair in basis_tables()]
    f32 = jnp.float32
    line = lambda a: a.reshape(1, -1)
    order, coarse_row = line(order), line(coarse_row)
    conf, *mortar = call(
        functools.partial(conf_kernel, elements),
        [jax.ShapeDtypeStruct((confs, TRACE_PAD), f32)],
        (line(conf_face), line(conf_elem), conf_trace),
        hand_on=(
            line(mortar_dest),
            line(mortar_elem),
            line(mortar_face),
            line(mortar_sub),
            coarse_row,
            mortar_trace,
            *lift,
        ),
    )
    conf = from_behind(conf, "gz", 1)
    (outgoing,) = call(
        functools.partial(pack_kernel, peers, cap, row_cap, elements),
        [jax.ShapeDtypeStruct((peers, row_cap, lanes), f32)],
        (),
        mortar,
    )
    incoming = exchange(outgoing)
    y, cols, conf, *face = call(
        functools.partial(cell_kernel, peers, row_cap),
        [
            jax.ShapeDtypeStruct((VARS * slots, ROW), f32),
            jax.ShapeDtypeStruct((slots, 128), f32),
            jax.ShapeDtypeStruct((confs, TRACE_PAD), f32),
        ],
        (order, coarse_row, adjoint, *cell, *conf_lift),
        (conf,),
        scratch=[pltpu.VMEM((2, VARS * slots, CELL_PAD), f32)],
        hand_on=face,
    )
    (rows,) = call(
        functools.partial(face_kernel, peers, row_cap, elements, groups),
        [jax.ShapeDtypeStruct((peers, row_cap, VARS * ROW), f32)],
        (),
        (incoming, conf, y, cols, *face),
        scratch=[pltpu.VMEM((VARS * slots, FACES_PAD), f32)],
    )
    (out,) = call(
        functools.partial(place_kernel, peers, row_cap, groups * (SENT + 1)),
        [jax.ShapeDtypeStruct((elements, VARS * ROW), f32)],
        (),
        (exchange(rows), incoming),
    )
    return out


def solution(mesh):
    rows = P(("gx", "gy", "gz"))
    wide = P(("gx", "gy", "gz"), None)
    return jax.shard_map(
        body,
        mesh=mesh,
        in_specs=(wide, rows, wide, rows, wide, rows, rows, wide, rows, rows, rows),
        out_specs=wide,
        check_vma=False,
    )
```

```python
import functools

import jax
import jax.numpy as jnp
import ml_dtypes
import numpy as np
from jax import lax
from jax.experimental import pallas as pl
from jax.experimental.pallas import tpu as pltpu
from jax.sharding import PartitionSpec as P

VARS = 5
NODE = 7
FACE = NODE * NODE
CELL = NODE * FACE
ROW = 216
FACES = 6
ORDERS = (2, 3, 4, 5, 6)
TRACE = VARS * FACE
TRACE_PAD = 256
FLAT = 36
SENT = VARS * FLAT
CELL_PAD = 384
FACE_PAD = 40
FACES_PAD = 256


def grid_nodes(degree):
    return -np.cos(np.pi * np.arange(degree + 1) / degree)


def lagrange_rows(degree, points):
    anchors = grid_nodes(degree)
    values = np.ones((len(points), degree + 1))
    for k in range(degree + 1):
        for other in range(degree + 1):
            if other != k:
                values[:, k] *= (points - anchors[other]) / (anchors[k] - anchors[other])
    return values


def split_table(table):
    table = np.asarray(table, np.float32)
    high = table.astype(ml_dtypes.bfloat16)
    low = (table - high.astype(np.float32)).astype(ml_dtypes.bfloat16)
    return high, low


@functools.lru_cache(maxsize=None)
def basis_tables():
    top_nodes = grid_nodes(6)
    mortar = [lagrange_rows(6, (top_nodes - 1.0) / 2.0), lagrange_rows(6, (top_nodes + 1.0) / 2.0)]
    flat = lagrange_rows(5, top_nodes)
    lift = np.zeros((5, TRACE_PAD, SENT))
    for sub in range(5):
        both = (mortar[sub // 2] @ flat, mortar[sub % 2] @ flat) if sub < 4 else (flat, flat)
        for v in range(VARS):
            lift[sub, v * FACE : (v + 1) * FACE, v * FLAT : (v + 1) * FLAT] = np.kron(*both)
    cell = np.zeros((len(ORDERS), CELL_PAD, ROW))
    face = np.zeros((len(ORDERS), FACES_PAD, ROW))
    for index, p in enumerate(ORDERS):
        shrink = np.zeros((6, NODE))
        shrink[:p, : p + 1] = lagrange_rows(p - 1, grid_nodes(p)).T
        cell[index, :CELL] = np.einsum("ai,bj,ck->ijkabc", shrink, shrink, shrink).reshape(CELL, ROW)
        lower = np.zeros((6, 6))
        lower[:p] = lagrange_rows(p - 1, grid_nodes(5)).T
        low, high = shrink[:, 0], shrink[:, p]
        for axis, spec in enumerate(("c,ai,bj->ijcab", "c,ai,bj->ijacb", "c,ai,bj->ijabc")):
            for side, edge in enumerate((low, high)):
                first = (2 * axis + side) * FACE_PAD
                face[index, first : first + FLAT] = np.einsum(spec, edge, lower, lower).reshape(FLAT, ROW)
    return (
        split_table(lift.reshape(-1, SENT)),
        split_table(cell.reshape(-1, ROW)),
        split_table(face.reshape(-1, ROW)),
    )


def iota(shape, axis):
    return lax.broadcasted_iota(jnp.int32, shape, axis)


def halves(x):
    high = x.astype(jnp.bfloat16)
    low = (x - high.astype(jnp.float32)).astype(jnp.bfloat16)
    return high, low


def dot(a, b):
    return jnp.dot(a, b, preferred_element_type=jnp.float32)


def dot3(high, low, table_high, table_low):
    return dot(high, table_high) + dot(low, table_high) + dot(high, table_low)


def earlier(member):
    count = member.shape[1]
    before = (iota((count, count), 0) < iota((count, count), 1)).astype(jnp.float32)
    return dot(member.astype(jnp.bfloat16), before.astype(jnp.bfloat16))


def device_of(shape):
    size_x, size_y = lax.axis_size("gx"), lax.axis_size("gy")
    rank = iota(shape, 0)
    return rank % size_x * size_y + rank // size_x


def owner_of(crow, peers, elements):
    first = device_of((peers, crow.shape[1])) * elements
    return ((crow >= first) & (crow < first + elements)).astype(jnp.float32)


def row_places(crow, peers, elements, stride):
    member = owner_of(crow, peers, elements)
    rank = earlier(member)
    block = iota(member.shape, 0).astype(jnp.float32)
    place = jnp.sum(member * (block * stride + rank), axis=0, keepdims=True)
    owned = (device_of(member.shape) * elements).astype(jnp.float32)
    slot = crow.astype(jnp.float32) - jnp.sum(member * owned, axis=0, keepdims=True)
    return place, slot


def onehot_rows(place, rows):
    return (iota((rows, place.shape[1]), 0).astype(jnp.float32) == place).astype(jnp.float32)


def column(onehot, values):
    return jnp.sum(onehot * values, axis=1, keepdims=True)


def pad_lanes(x, lanes):
    return jnp.concatenate([x, jnp.zeros((x.shape[0], lanes - x.shape[1]), x.dtype)], axis=1)


def pack_kernel(peers, cap, row_cap, elements, get, out, conf_out):
    dest, elem, face, sub, crow, cface, celem = [get(i) for i in range(7)]
    count, confs = dest.shape[1], cface.shape[1]
    groups, slots = -(-cap // row_cap), peers * row_cap
    member = (device_of((peers, count)) == dest).astype(jnp.float32)
    block = jnp.sum(member * iota(member.shape, 0).astype(jnp.float32), axis=0, keepdims=True)
    rank = jnp.sum(member * earlier(member), axis=0, keepdims=True)
    group = sum([(rank >= float(g * row_cap)).astype(jnp.float32) for g in range(1, groups)], jnp.zeros_like(rank))
    place = group * float(slots - row_cap) + block * float(row_cap) + rank
    put = onehot_rows(place, groups * slots)
    code_col = column(put, (face * elements + elem + 1).astype(jnp.float32))
    row_place, row_slot = row_places(crow, peers, elements, row_cap)
    row_col = column(onehot_rows(row_place, slots), row_slot + 1.0)
    eye = (iota((count, count), 0) == iota((count, count), 1)).astype(jnp.float32)
    sub_col = column(eye, sub.astype(jnp.float32))
    x = pad_lanes(get(7), TRACE_PAD)
    wide = jnp.concatenate([jnp.where(sub_col == float(s), x, 0.0) for s in range(4)], axis=1)
    table_high, table_low = get(9), get(10)
    split = 4 * TRACE_PAD
    lifted = dot3(*halves(wide), table_high[:split], table_low[:split])
    lifted_high, lifted_low = halves(lifted)
    put = put.astype(jnp.bfloat16)
    packed = dot(put, lifted_high) + dot(put, lifted_low)
    for g in range(groups):
        part = packed[g * slots : (g + 1) * slots]
        out[:, :, g * SENT : (g + 1) * SENT] = part.reshape(peers, row_cap, SENT)
    tags = jnp.concatenate([*[code_col[g * slots : (g + 1) * slots] for g in range(groups)], row_col], axis=1)
    out[:, :, groups * SENT : groups * (SENT + 1) + 1] = tags.reshape(peers, row_cap, groups + 1)
    eye = (iota((confs, confs), 0) == iota((confs, confs), 1)).astype(jnp.float32)
    conf_col = column(eye, (cface * elements + celem + 1).astype(jnp.float32))
    conf = dot3(*halves(pad_lanes(get(8), TRACE_PAD)), table_high[split:], table_low[split:])
    conf_out[:, :SENT] = conf
    conf_out[:, SENT : SENT + 1] = conf_col


def cell_kernel(peers, row_cap, get, y_out, col_out, face_high, face_low, spread):
    order, crow = get(0), get(1)
    elements = order.shape[1]
    slots = peers * row_cap
    place, _ = row_places(crow, peers, elements, row_cap)
    take = onehot_rows(place, slots)
    order_col = column(take, order.astype(jnp.float32))
    elem_col = column(take, iota((1, elements), 1).astype(jnp.float32) + 1.0)
    lane = iota((slots, 128), 1)
    col_out[...] = jnp.where(lane == 0, order_col, jnp.where(lane == 1, elem_col, 0.0))
    take = take.astype(jnp.bfloat16)
    spread[...] = jnp.zeros_like(spread)
    for half, part in enumerate(halves(get(2))):
        moved = dot(take, part)
        for v in range(VARS):
            spread[half, v * slots : (v + 1) * slots, :CELL] = moved[:, v * CELL : (v + 1) * CELL]
    order_rows = jnp.concatenate([order_col] * VARS, axis=0)
    high, low = spread[0], spread[1]
    wide_high = jnp.concatenate([jnp.where(order_rows == float(p), high, 0.0).astype(jnp.bfloat16) for p in ORDERS], axis=1)
    wide_low = jnp.concatenate([jnp.where(order_rows == float(p), low, 0.0).astype(jnp.bfloat16) for p in ORDERS], axis=1)
    y_out[...] = dot3(wide_high, wide_low, get(3), get(4))
    face_high[...] = get(5)
    face_low[...] = get(6)


def face_kernel(peers, row_cap, elements, groups, get, incoming, conf, y, cols, table_high, table_low, out, spread):
    slots = peers * row_cap
    message = incoming[...].reshape(slots, incoming.shape[2])
    first_tag = groups * SENT
    x = jnp.concatenate([*[message[:, g * SENT : (g + 1) * SENT] for g in range(groups)], conf[:, :SENT]], axis=0)
    code_col = jnp.concatenate(
        [*[message[:, first_tag + g : first_tag + g + 1] for g in range(groups)], conf[:, SENT : SENT + 1]], axis=0
    )
    count = x.shape[0]
    code_row = jnp.sum(jnp.where(iota((count, count), 0) == iota((count, count), 1), code_col, 0.0), axis=0, keepdims=True)
    order_col, elem_col = cols[:, 0:1], cols[:, 1:2]
    wanted = jnp.concatenate([jnp.where(elem_col > 0.0, elem_col + float(f * elements), -1.0) for f in range(FACES)], axis=0)
    gather = (wanted == code_row).astype(jnp.bfloat16)
    high, low = halves(x)
    face_sum = dot(gather, high) + dot(gather, low)
    spread[...] = jnp.zeros_like(spread)
    for f in range(FACES):
        for v in range(VARS):
            spread[v * slots : (v + 1) * slots, f * FACE_PAD : f * FACE_PAD + FLAT] = face_sum[
                f * slots : (f + 1) * slots, v * FLAT : (v + 1) * FLAT
            ]
    order_rows = jnp.concatenate([order_col] * VARS, axis=0)
    z = spread[...]
    wide = jnp.concatenate([jnp.where(order_rows == float(p), z, 0.0) for p in ORDERS], axis=1)
    high, low = halves(wide)
    total = y[...] + dot3(high, low, table_high[...], table_low[...])
    for v in range(VARS):
        out[:, :, v * ROW : (v + 1) * ROW] = total[v * slots : (v + 1) * slots].reshape(peers, row_cap, ROW)


def place_kernel(peers, row_cap, tag, get, arrived, message, out):
    elements = out.shape[0]
    rows = peers * row_cap
    x = arrived[...].reshape(rows, arrived.shape[2])
    slot_col = message[:, :, tag : tag + 1].reshape(rows, 1)
    slot_row = jnp.sum(jnp.where(iota((rows, rows), 0) == iota((rows, rows), 1), slot_col, 0.0), axis=0, keepdims=True)
    put = (iota((elements, rows), 0).astype(jnp.float32) + 1.0 == slot_row).astype(jnp.bfloat16)
    high, low = halves(x)
    rest = (x - high.astype(jnp.float32) - low.astype(jnp.float32)).astype(jnp.bfloat16)
    out[...] = dot(put, high) + dot(put, low) + dot(put, rest)


def fetched(kernel, n_far, n_near, n_out, *refs):
    far, near, outs = refs[:n_far], refs[n_far : n_far + n_near], refs[n_far + n_near : n_far + n_near + n_out]
    rest = refs[n_far + n_near + n_out :]
    held, sems, scratch = rest[:n_far], rest[n_far], rest[n_far + 1 :]
    copies = [pltpu.make_async_copy(src, dst, sems.at[i]) for i, (src, dst) in enumerate(zip(far, held))]
    for copy in copies:
        copy.start()

    def get(i):
        copies[i].wait()
        return held[i][...]

    kernel(get, *near, *outs, *scratch)


def call(kernel, outs, far, near=(), scratch=(), flops=0):
    shapes = jax.tree.leaves(outs)
    sizes = [np.prod(a.shape) * a.dtype.itemsize for a in (*far, *near, *shapes)]
    in_specs = [pl.BlockSpec(memory_space=pltpu.HBM)] * len(far) + [pl.BlockSpec(memory_space=pltpu.VMEM)] * len(near)
    scratch = [*[pltpu.VMEM(a.shape, a.dtype) for a in far], pltpu.SemaphoreType.DMA((max(1, len(far)),)), *scratch]
    return pl.pallas_call(
        functools.partial(fetched, kernel, len(far), len(near), len(shapes)),
        in_specs=in_specs,
        out_shape=outs,
        scratch_shapes=scratch,
        compiler_params=pltpu.CompilerParams(vmem_limit_bytes=48 * 1024 * 1024),
        cost_estimate=pl.CostEstimate(flops=flops, bytes_accessed=int(sum(sizes)), transcendentals=0),
    )(*[pltpu.with_memory_space_constraint(a, pltpu.HBM) for a in far], *near)


def exchange(block):
    return lax.all_to_all(block, ("gy", "gx"), split_axis=0, concat_axis=0, tiled=True)


def from_behind(block, axis, distance):
    devices = range(lax.axis_size(axis))
    route = [((i - distance) % len(devices), i) for i in devices]
    return lax.ppermute(block, axis, route)


def body(
    adjoint,
    order,
    mortar_trace,
    mortar_sub,
    mortar_dest,
    mortar_elem,
    mortar_face,
    conf_trace,
    conf_elem,
    conf_face,
    coarse_row,
):
    elements = adjoint.shape[0]
    count = mortar_trace.shape[0]
    confs = conf_trace.shape[0]
    peers = lax.axis_size("gx") * lax.axis_size("gy")
    cap = max(2, 2 * count // peers)
    row_cap = max(2, elements // peers)
    slots = peers * row_cap
    groups = -(-cap // row_cap)
    lanes = -(-(groups * (SENT + 1) + 1) // 128) * 128
    lift, cell, face = [tuple(jnp.asarray(t) for t in pair) for pair in basis_tables()]
    f32 = jnp.float32
    line = lambda a: a.reshape(1, -1)
    order, coarse_row = line(order), line(coarse_row)
    outgoing, conf = call(
        functools.partial(pack_kernel, peers, cap, row_cap, elements),
        (jax.ShapeDtypeStruct((peers, row_cap, lanes), f32), jax.ShapeDtypeStruct((confs, TRACE_PAD), f32)),
        (
            line(mortar_dest),
            line(mortar_elem),
            line(mortar_face),
            line(mortar_sub),
            coarse_row,
            line(conf_face),
            line(conf_elem),
            mortar_trace,
            conf_trace,
            *lift,
        ),
    )
    incoming = exchange(outgoing)
    conf = from_behind(conf, "gz", 1)
    y, cols, *face = call(
        functools.partial(cell_kernel, peers, row_cap),
        (
            jax.ShapeDtypeStruct((VARS * slots, ROW), f32),
            jax.ShapeDtypeStruct((slots, 128), f32),
            *[jax.ShapeDtypeStruct(t.shape, t.dtype) for t in face],
        ),
        (order, coarse_row, adjoint, *cell, *face),
        scratch=[pltpu.VMEM((2, VARS * slots, CELL_PAD), f32)],
    )
    rows = call(
        functools.partial(face_kernel, peers, row_cap, elements, groups),
        jax.ShapeDtypeStruct((peers, row_cap, VARS * ROW), f32),
        (),
        (incoming, conf, y, cols, *face),
        scratch=[pltpu.VMEM((VARS * slots, FACES_PAD), f32)],
    )
    arrived = exchange(rows)
    return call(
        functools.partial(place_kernel, peers, row_cap, groups * (SENT + 1)),
        jax.ShapeDtypeStruct((elements, VARS * ROW), f32),
        (),
        (arrived, incoming),
    )


def solution(mesh):
    rows = P(("gx", "gy", "gz"))
    wide = P(("gx", "gy", "gz"), None)
    return jax.shard_map(
        body,
        mesh=mesh,
        in_specs=(wide, rows, wide, rows, wide, rows, rows, wide, rows, rows, rows),
        out_specs=wide,
        check_vma=False,
    )
```

```python
import functools

import jax
import jax.numpy as jnp
import ml_dtypes
import numpy as np
from jax import lax
from jax.experimental import pallas as pl
from jax.experimental.pallas import tpu as pltpu
from jax.sharding import PartitionSpec as P

VARS = 5
NODE = 7
FACE = NODE * NODE
CELL = NODE * FACE
ROW = 216
FACES = 6
ORDERS = (2, 3, 4, 5, 6)
TRACE = VARS * FACE
TRACE_PAD = 256
FLAT = 36
SENT = VARS * FLAT
STEP = 192
TAG_FACE = SENT
TAG_ROW = SENT + 1
CELL_PAD = 384
FACE_PAD = 40
FACES_PAD = 256


def grid_nodes(degree):
    return -np.cos(np.pi * np.arange(degree + 1) / degree)


def lagrange_rows(degree, points):
    anchors = grid_nodes(degree)
    values = np.ones((len(points), degree + 1))
    for k in range(degree + 1):
        for other in range(degree + 1):
            if other != k:
                values[:, k] *= (points - anchors[other]) / (anchors[k] - anchors[other])
    return values


def split_table(table):
    table = np.asarray(table, np.float32)
    high = table.astype(ml_dtypes.bfloat16)
    low = (table - high.astype(np.float32)).astype(ml_dtypes.bfloat16)
    return high, low


@functools.lru_cache(maxsize=None)
def basis_tables():
    top_nodes = grid_nodes(6)
    mortar = [lagrange_rows(6, (top_nodes - 1.0) / 2.0), lagrange_rows(6, (top_nodes + 1.0) / 2.0)]
    flat = lagrange_rows(5, top_nodes)
    lift = np.zeros((5, TRACE_PAD, STEP))
    for sub in range(5):
        both = (mortar[sub // 2] @ flat, mortar[sub % 2] @ flat) if sub < 4 else (flat, flat)
        for v in range(VARS):
            lift[sub, v * FACE : (v + 1) * FACE, v * FLAT : (v + 1) * FLAT] = np.kron(*both)
    cell = np.zeros((len(ORDERS), CELL_PAD, ROW))
    face = np.zeros((len(ORDERS), FACES_PAD, ROW))
    for index, p in enumerate(ORDERS):
        shrink = np.zeros((6, NODE))
        shrink[:p, : p + 1] = lagrange_rows(p - 1, grid_nodes(p)).T
        cell[index, :CELL] = np.einsum("ai,bj,ck->ijkabc", shrink, shrink, shrink).reshape(CELL, ROW)
        lower = np.zeros((6, 6))
        lower[:p] = lagrange_rows(p - 1, grid_nodes(5)).T
        low, high = shrink[:, 0], shrink[:, p]
        for axis, spec in enumerate(("c,ai,bj->ijcab", "c,ai,bj->ijacb", "c,ai,bj->ijabc")):
            for side, edge in enumerate((low, high)):
                first = (2 * axis + side) * FACE_PAD
                face[index, first : first + FLAT] = np.einsum(spec, edge, lower, lower).reshape(FLAT, ROW)
    return (
        split_table(lift[:4].reshape(-1, STEP)),
        split_table(lift[4]),
        split_table(cell.reshape(-1, ROW)),
        split_table(face.reshape(-1, ROW)),
    )


def iota(shape, axis):
    return lax.broadcasted_iota(jnp.int32, shape, axis)


def halves(x):
    high = x.astype(jnp.bfloat16)
    low = (x - high.astype(jnp.float32)).astype(jnp.bfloat16)
    return high, low


def dot(a, b):
    return jnp.dot(a, b, preferred_element_type=jnp.float32)


def dot3(high, low, table_high, table_low):
    return dot(high, table_high) + dot(low, table_high) + dot(high, table_low)


def earlier(member):
    count = member.shape[1]
    before = (iota((count, count), 0) < iota((count, count), 1)).astype(jnp.float32)
    return dot(member.astype(jnp.bfloat16), before.astype(jnp.bfloat16))


def device_of(shape):
    size_x, size_y = lax.axis_size("gx"), lax.axis_size("gy")
    rank = iota(shape, 0)
    return rank % size_x * size_y + rank // size_x


def owner_of(crow, peers, elements):
    first = device_of((peers, crow.shape[1])) * elements
    return ((crow >= first) & (crow < first + elements)).astype(jnp.float32)


def row_places(crow, peers, elements, stride):
    member = owner_of(crow, peers, elements)
    rank = earlier(member)
    block = iota(member.shape, 0).astype(jnp.float32)
    place = jnp.sum(member * (block * stride + rank), axis=0, keepdims=True)
    owned = (device_of(member.shape) * elements).astype(jnp.float32)
    slot = crow.astype(jnp.float32) - jnp.sum(member * owned, axis=0, keepdims=True)
    return place, slot


def onehot_rows(place, rows):
    return (iota((rows, place.shape[1]), 0).astype(jnp.float32) == place).astype(jnp.float32)


def column(onehot, values):
    return jnp.sum(onehot * values, axis=1, keepdims=True)


def pad_lanes(x, lanes):
    return jnp.concatenate([x, jnp.zeros((x.shape[0], lanes - x.shape[1]), x.dtype)], axis=1)


def pack_kernel(peers, cap, row_cap, elements, get, out, conf_out, message, sent):
    dest, sub, elem, face, crow = [get(i) for i in range(5)]
    count = dest.shape[1]
    groups, slots = -(-cap // row_cap), peers * row_cap
    member = (device_of((peers, count)) == dest).astype(jnp.float32)
    block = jnp.sum(member * iota(member.shape, 0).astype(jnp.float32), axis=0, keepdims=True)
    rank = jnp.sum(member * earlier(member), axis=0, keepdims=True)
    group = sum([(rank >= float(g * row_cap)).astype(jnp.float32) for g in range(1, groups)], jnp.zeros_like(rank))
    place = group * float(slots - row_cap) + block * float(row_cap) + rank
    put = onehot_rows(place, groups * slots)
    code_col = column(put, (face * elements + elem + 1).astype(jnp.float32))
    row_place, row_slot = row_places(crow, peers, elements, row_cap)
    row_col = column(onehot_rows(row_place, slots), row_slot + 1.0)
    eye = (iota((count, count), 0) == iota((count, count), 1)).astype(jnp.float32)
    sub_col = column(eye, sub.astype(jnp.float32))
    x = pad_lanes(get(5), TRACE_PAD)
    wide = jnp.concatenate([jnp.where(sub_col == float(s), x, 0.0) for s in range(4)], axis=1)
    lifted_high, lifted_low = halves(dot3(*halves(wide), get(6), get(7)))
    put = put.astype(jnp.bfloat16)
    packed = dot(put, lifted_high) + dot(put, lifted_low)
    packed = jnp.where(iota(packed.shape, 1) == TAG_FACE, code_col, packed)
    for g in range(groups):
        part = packed[g * slots : (g + 1) * slots]
        if g == 0:
            part = jnp.where(iota(part.shape, 1) == TAG_ROW, row_col, part)
        message[:, :, g * STEP : (g + 1) * STEP] = part.reshape(peers, row_cap, STEP)
    send = pltpu.make_async_copy(message, out, sent.at[0])
    send.start()
    cface, celem = get(8), get(9)
    confs = cface.shape[1]
    eye = (iota((confs, confs), 0) == iota((confs, confs), 1)).astype(jnp.float32)
    conf_col = column(eye, (cface * elements + celem + 1).astype(jnp.float32))
    conf = dot3(*halves(pad_lanes(get(10), TRACE_PAD)), get(11), get(12))
    conf_out[...] = jnp.where(iota(conf.shape, 1) == TAG_FACE, conf_col, conf)
    send.wait()


def cell_kernel(peers, row_cap, get, y_out, col_out, spread):
    order, crow = get(0), get(1)
    elements = order.shape[1]
    slots = peers * row_cap
    place, _ = row_places(crow, peers, elements, row_cap)
    take = onehot_rows(place, slots)
    order_col = column(take, order.astype(jnp.float32))
    elem_col = column(take, iota((1, elements), 1).astype(jnp.float32) + 1.0)
    lane = iota((slots, 128), 1)
    col_out[...] = jnp.where(lane == 0, order_col, jnp.where(lane == 1, elem_col, 0.0))
    take = take.astype(jnp.bfloat16)
    spread[...] = jnp.zeros_like(spread)
    for half, part in enumerate(halves(get(2))):
        moved = dot(take, part)
        for v in range(VARS):
            spread[half, v * slots : (v + 1) * slots, :CELL] = moved[:, v * CELL : (v + 1) * CELL]
    order_rows = jnp.concatenate([order_col] * VARS, axis=0)
    high, low = spread[0], spread[1]
    wide_high = jnp.concatenate([jnp.where(order_rows == float(p), high, 0.0).astype(jnp.bfloat16) for p in ORDERS], axis=1)
    wide_low = jnp.concatenate([jnp.where(order_rows == float(p), low, 0.0).astype(jnp.bfloat16) for p in ORDERS], axis=1)
    y_out[...] = dot3(wide_high, wide_low, get(3), get(4))


def face_kernel(peers, row_cap, elements, groups, get, incoming, conf, y, cols, table_high, table_low, out, spread):
    slots = peers * row_cap
    message = incoming[...].reshape(slots, incoming.shape[2])
    x = jnp.concatenate([*[message[:, g * STEP : (g + 1) * STEP] for g in range(groups)], conf[...]], axis=0)
    code_col = x[:, TAG_FACE : TAG_FACE + 1]
    count = x.shape[0]
    code_row = jnp.sum(jnp.where(iota((count, count), 0) == iota((count, count), 1), code_col, 0.0), axis=0, keepdims=True)
    order_col, elem_col = cols[:, 0:1], cols[:, 1:2]
    wanted = jnp.concatenate([jnp.where(elem_col > 0.0, elem_col + float(f * elements), -1.0) for f in range(FACES)], axis=0)
    gather = (wanted == code_row).astype(jnp.bfloat16)
    high, low = halves(x)
    face_sum = dot(gather, high) + dot(gather, low)
    spread[...] = jnp.zeros_like(spread)
    for f in range(FACES):
        for v in range(VARS):
            spread[v * slots : (v + 1) * slots, f * FACE_PAD : f * FACE_PAD + FLAT] = face_sum[
                f * slots : (f + 1) * slots, v * FLAT : (v + 1) * FLAT
            ]
    order_rows = jnp.concatenate([order_col] * VARS, axis=0)
    z = spread[...]
    wide = jnp.concatenate([jnp.where(order_rows == float(p), z, 0.0) for p in ORDERS], axis=1)
    high, low = halves(wide)
    total = y[...] + dot3(high, low, table_high[...], table_low[...])
    for v in range(VARS):
        out[:, :, v * ROW : (v + 1) * ROW] = total[v * slots : (v + 1) * slots].reshape(peers, row_cap, ROW)


def place_kernel(peers, row_cap, get, arrived, message, out):
    elements = out.shape[0]
    rows = peers * row_cap
    x = arrived[...].reshape(rows, arrived.shape[2])
    slot_col = message[:, :, TAG_ROW : TAG_ROW + 1].reshape(rows, 1)
    slot_row = jnp.sum(jnp.where(iota((rows, rows), 0) == iota((rows, rows), 1), slot_col, 0.0), axis=0, keepdims=True)
    put = (iota((elements, rows), 0).astype(jnp.float32) + 1.0 == slot_row).astype(jnp.bfloat16)
    high, low = halves(x)
    rest = (x - high.astype(jnp.float32) - low.astype(jnp.float32)).astype(jnp.bfloat16)
    out[...] = dot(put, high) + dot(put, low) + dot(put, rest)


def fetched(kernel, n_far, n_pass, n_near, n_out, *refs):
    far, near, outs = refs[:n_far], refs[n_far : n_far + n_near], refs[n_far + n_near : n_far + n_near + n_out]
    rest = refs[n_far + n_near + n_out :]
    n_held = n_far - n_pass
    held, sems, scratch = rest[:n_held], rest[n_held], rest[n_held + 1 :]
    held = (*held, *outs[n_out - n_pass :])
    copies = [pltpu.make_async_copy(src, dst, sems.at[i]) for i, (src, dst) in enumerate(zip(far, held))]
    for copy in copies:
        copy.start()

    def get(i):
        copies[i].wait()
        return held[i][...]

    kernel(get, *near, *outs[: n_out - n_pass], *scratch)
    for copy in copies[n_held:]:
        copy.wait()


def like(a):
    return jax.ShapeDtypeStruct(a.shape, a.dtype)


def call(kernel, outs, far, near=(), scratch=(), hand_on=(), out_far=(), flops=0):
    outs = [*outs, *[like(a) for a in hand_on]]
    out_specs = [pl.BlockSpec(memory_space=pltpu.HBM if i in out_far else pltpu.VMEM) for i in range(len(outs))]
    outs = [pltpu.HBM(a.shape, a.dtype) if i in out_far else a for i, a in enumerate(outs)]
    sizes = [np.prod(a.shape) * a.dtype.itemsize for a in (*far, *near, *outs)]
    held = [pltpu.VMEM(a.shape, a.dtype) for a in far]
    far = (*far, *hand_on)
    in_specs = [pl.BlockSpec(memory_space=pltpu.HBM)] * len(far) + [pl.BlockSpec(memory_space=pltpu.VMEM)] * len(near)
    return pl.pallas_call(
        functools.partial(fetched, kernel, len(far), len(hand_on), len(near), len(outs)),
        in_specs=in_specs,
        out_specs=out_specs,
        out_shape=outs,
        scratch_shapes=[*held, pltpu.SemaphoreType.DMA((max(1, len(far)),)), *scratch],
        compiler_params=pltpu.CompilerParams(vmem_limit_bytes=48 * 1024 * 1024),
        cost_estimate=pl.CostEstimate(flops=flops, bytes_accessed=int(sum(sizes)), transcendentals=0),
    )(*[pltpu.with_memory_space_constraint(a, pltpu.HBM) for a in far], *near)


def exchange(block):
    return lax.all_to_all(block, ("gy", "gx"), split_axis=0, concat_axis=0, tiled=True)


def from_behind(block, axis, distance):
    devices = range(lax.axis_size(axis))
    route = [((i - distance) % len(devices), i) for i in devices]
    return lax.ppermute(block, axis, route)


def body(
    adjoint,
    order,
    mortar_trace,
    mortar_sub,
    mortar_dest,
    mortar_elem,
    mortar_face,
    conf_trace,
    conf_elem,
    conf_face,
    coarse_row,
):
    elements = adjoint.shape[0]
    count = mortar_trace.shape[0]
    confs = conf_trace.shape[0]
    peers = lax.axis_size("gx") * lax.axis_size("gy")
    cap = max(2, 2 * count // peers)
    row_cap = max(2, elements // peers)
    slots = peers * row_cap
    groups = -(-cap // row_cap)
    lanes = groups * STEP
    lift, conf_lift, cell, face = [tuple(jnp.asarray(t) for t in pair) for pair in basis_tables()]
    f32 = jnp.float32
    line = lambda a: a.reshape(1, -1)
    order, coarse_row = line(order), line(coarse_row)
    outgoing, conf = call(
        functools.partial(pack_kernel, peers, cap, row_cap, elements),
        [jax.ShapeDtypeStruct((peers, row_cap, lanes), f32), jax.ShapeDtypeStruct((confs, STEP), f32)],
        (
            line(mortar_dest),
            line(mortar_sub),
            line(mortar_elem),
            line(mortar_face),
            coarse_row,
            mortar_trace,
            *lift,
            line(conf_face),
            line(conf_elem),
            conf_trace,
            *conf_lift,
        ),
        scratch=[pltpu.VMEM((peers, row_cap, lanes), f32), pltpu.SemaphoreType.DMA((1,))],
        out_far=(0,),
    )
    incoming = exchange(outgoing)
    conf = from_behind(conf, "gz", 1)
    y, cols, *face = call(
        functools.partial(cell_kernel, peers, row_cap),
        [jax.ShapeDtypeStruct((VARS * slots, ROW), f32), jax.ShapeDtypeStruct((slots, 128), f32)],
        (order, coarse_row, adjoint, *cell),
        scratch=[pltpu.VMEM((2, VARS * slots, CELL_PAD), f32)],
        hand_on=face,
    )
    (rows,) = call(
        functools.partial(face_kernel, peers, row_cap, elements, groups),
        [jax.ShapeDtypeStruct((peers, row_cap, VARS * ROW), f32)],
        (),
        (incoming, conf, y, cols, *face),
        scratch=[pltpu.VMEM((VARS * slots, FACES_PAD), f32)],
    )
    (out,) = call(
        functools.partial(place_kernel, peers, row_cap),
        [jax.ShapeDtypeStruct((elements, VARS * ROW), f32)],
        (),
        (exchange(rows), incoming),
    )
    return out


def solution(mesh):
    rows = P(("gx", "gy", "gz"))
    wide = P(("gx", "gy", "gz"), None)
    return jax.shard_map(
        body,
        mesh=mesh,
        in_specs=(wide, rows, wide, rows, wide, rows, rows, wide, rows, rows, rows),
        out_specs=wide,
        check_vma=False,
    )
```

```python
import functools

import jax
import jax.numpy as jnp
import ml_dtypes
import numpy as np
from jax import lax
from jax.experimental import pallas as pl
from jax.experimental.pallas import tpu as pltpu
from jax.sharding import PartitionSpec as P

VARS = 5
NODE = 7
FACE = NODE * NODE
CELL = NODE * FACE
ROW = 216
FACES = 6
ORDERS = (2, 3, 4, 5, 6)
TRACE = VARS * FACE
TRACE_PAD = 256
FLAT = 36
SENT = VARS * FLAT
STEP = 192
TAG_FACE = SENT
ROWS_PAD = 1152
TAG_SLOT = VARS * ROW
CELL_PAD = 384
FACE_PAD = 40
FACES_PAD = 256


def grid_nodes(degree):
    return -np.cos(np.pi * np.arange(degree + 1) / degree)


def lagrange_rows(degree, points):
    anchors = grid_nodes(degree)
    values = np.ones((len(points), degree + 1))
    for k in range(degree + 1):
        for other in range(degree + 1):
            if other != k:
                values[:, k] *= (points - anchors[other]) / (anchors[k] - anchors[other])
    return values


def split_table(table):
    table = np.asarray(table, np.float32)
    high = table.astype(ml_dtypes.bfloat16)
    low = (table - high.astype(np.float32)).astype(ml_dtypes.bfloat16)
    return high, low


@functools.lru_cache(maxsize=None)
def basis_tables():
    top_nodes = grid_nodes(6)
    mortar = [lagrange_rows(6, (top_nodes - 1.0) / 2.0), lagrange_rows(6, (top_nodes + 1.0) / 2.0)]
    flat = lagrange_rows(5, top_nodes)
    lift = np.zeros((5, TRACE_PAD, STEP))
    for sub in range(5):
        both = (mortar[sub // 2] @ flat, mortar[sub % 2] @ flat) if sub < 4 else (flat, flat)
        for v in range(VARS):
            lift[sub, v * FACE : (v + 1) * FACE, v * FLAT : (v + 1) * FLAT] = np.kron(*both)
    cell = np.zeros((len(ORDERS), CELL_PAD, ROW))
    face = np.zeros((len(ORDERS), FACES_PAD, ROW))
    for index, p in enumerate(ORDERS):
        shrink = np.zeros((6, NODE))
        shrink[:p, : p + 1] = lagrange_rows(p - 1, grid_nodes(p)).T
        cell[index, :CELL] = np.einsum("ai,bj,ck->ijkabc", shrink, shrink, shrink).reshape(CELL, ROW)
        lower = np.zeros((6, 6))
        lower[:p] = lagrange_rows(p - 1, grid_nodes(5)).T
        low, high = shrink[:, 0], shrink[:, p]
        for axis, spec in enumerate(("c,ai,bj->ijcab", "c,ai,bj->ijacb", "c,ai,bj->ijabc")):
            for side, edge in enumerate((low, high)):
                first = (2 * axis + side) * FACE_PAD
                face[index, first : first + FLAT] = np.einsum(spec, edge, lower, lower).reshape(FLAT, ROW)
    return (
        split_table(lift[:4].reshape(-1, STEP)),
        split_table(lift[4]),
        split_table(cell.reshape(-1, ROW)),
        split_table(face.reshape(-1, ROW)),
    )


def iota(shape, axis):
    return lax.broadcasted_iota(jnp.int32, shape, axis)


def halves(x):
    high = x.astype(jnp.bfloat16)
    low = (x - high.astype(jnp.float32)).astype(jnp.bfloat16)
    return high, low


def dot(a, b):
    return jnp.dot(a, b, preferred_element_type=jnp.float32)


def dot3(high, low, table_high, table_low):
    return dot(high, table_high) + dot(low, table_high) + dot(high, table_low)


def earlier(member):
    count = member.shape[1]
    before = (iota((count, count), 0) < iota((count, count), 1)).astype(jnp.float32)
    return dot(member.astype(jnp.bfloat16), before.astype(jnp.bfloat16))


def device_of(shape):
    size_x, size_y = lax.axis_size("gx"), lax.axis_size("gy")
    rank = iota(shape, 0)
    return rank % size_x * size_y + rank // size_x


def pairwise():
    size_y = lax.axis_size("gy")
    return lax.axis_size("gx") == 2 and size_y <= 4 and size_y & (size_y - 1) == 0


def trace_device_of(shape):
    if not pairwise():
        return device_of(shape)
    size_y = lax.axis_size("gy")
    return iota(shape, 0) ^ (lax.axis_index("gx") * size_y + lax.axis_index("gy"))


def owner_of(crow, peers, elements):
    first = device_of((peers, crow.shape[1])) * elements
    return ((crow >= first) & (crow < first + elements)).astype(jnp.float32)


def row_places(crow, peers, elements, stride):
    member = owner_of(crow, peers, elements)
    rank = earlier(member)
    block = iota(member.shape, 0).astype(jnp.float32)
    place = jnp.sum(member * (block * stride + rank), axis=0, keepdims=True)
    owned = (device_of(member.shape) * elements).astype(jnp.float32)
    slot = crow.astype(jnp.float32) - jnp.sum(member * owned, axis=0, keepdims=True)
    return place, slot


def onehot_rows(place, rows):
    return (iota((rows, place.shape[1]), 0).astype(jnp.float32) == place).astype(jnp.float32)


def column(onehot, values):
    return jnp.sum(onehot * values, axis=1, keepdims=True)


def pad_lanes(x, lanes):
    return jnp.concatenate([x, jnp.zeros((x.shape[0], lanes - x.shape[1]), x.dtype)], axis=1)


def pack_kernel(peers, cap, row_cap, elements, get, conf_out, *outs):
    dest, sub, elem, face = [get(i) for i in range(4)]
    count = dest.shape[1]
    groups, slots = -(-cap // row_cap), peers * row_cap
    member = (trace_device_of((peers, count)) == dest).astype(jnp.float32)
    block = jnp.sum(member * iota(member.shape, 0).astype(jnp.float32), axis=0, keepdims=True)
    rank = jnp.sum(member * earlier(member), axis=0, keepdims=True)
    group = sum([(rank >= float(g * row_cap)).astype(jnp.float32) for g in range(1, groups)], jnp.zeros_like(rank))
    place = group * float(slots - row_cap) + block * float(row_cap) + rank
    put = onehot_rows(place, groups * slots)
    code_col = column(put, (face * elements + elem + 1).astype(jnp.float32))
    eye = (iota((count, count), 0) == iota((count, count), 1)).astype(jnp.float32)
    sub_col = column(eye, sub.astype(jnp.float32))
    x = pad_lanes(get(4), TRACE_PAD)
    wide = jnp.concatenate([jnp.where(sub_col == float(s), x, 0.0) for s in range(4)], axis=1)
    lifted_high, lifted_low = halves(dot3(*halves(wide), get(5), get(6)))
    put = put.astype(jnp.bfloat16)
    packed = dot(put, lifted_high) + dot(put, lifted_low)
    packed = jnp.where(iota(packed.shape, 1) == TAG_FACE, code_col, packed)
    for g in range(groups):
        for out, part in zip(outs, jnp.split(packed[g * slots : (g + 1) * slots], len(outs))):
            out[:, :, g * STEP : (g + 1) * STEP] = part.reshape(-1, row_cap, STEP)
    cface, celem = get(7), get(8)
    confs = cface.shape[1]
    eye = (iota((confs, confs), 0) == iota((confs, confs), 1)).astype(jnp.float32)
    conf_col = column(eye, (cface * elements + celem + 1).astype(jnp.float32))
    conf = dot3(*halves(pad_lanes(get(9), TRACE_PAD)), get(10), get(11))
    conf_out[...] = jnp.where(iota(conf.shape, 1) == TAG_FACE, conf_col, conf)


def pair_kernel(get, near, far, *outs):
    for k, out in enumerate(outs):
        out[0] = near[k]
        out[1] = far[k]


def cell_kernel(peers, row_cap, get, y_out, col_out, spread):
    order, crow = get(0), get(1)
    elements = order.shape[1]
    slots = peers * row_cap
    place, slot = row_places(crow, peers, elements, row_cap)
    take = onehot_rows(place, slots)
    order_col = column(take, order.astype(jnp.float32))
    elem_col = column(take, iota((1, elements), 1).astype(jnp.float32) + 1.0)
    lane = iota((slots, 128), 1)
    slot_col = column(take, slot + 1.0)
    col_out[...] = jnp.where(lane == 0, order_col, jnp.where(lane == 1, elem_col, slot_col))
    take = take.astype(jnp.bfloat16)
    spread[...] = jnp.zeros_like(spread)
    for half, part in enumerate(halves(get(2))):
        moved = dot(take, part)
        for v in range(VARS):
            spread[half, v * slots : (v + 1) * slots, :CELL] = moved[:, v * CELL : (v + 1) * CELL]
    order_rows = jnp.concatenate([order_col] * VARS, axis=0)
    high, low = spread[0], spread[1]
    wide_high = jnp.concatenate([jnp.where(order_rows == float(p), high, 0.0).astype(jnp.bfloat16) for p in ORDERS], axis=1)
    wide_low = jnp.concatenate([jnp.where(order_rows == float(p), low, 0.0).astype(jnp.bfloat16) for p in ORDERS], axis=1)
    y_out[...] = dot3(wide_high, wide_low, get(3), get(4))


def face_kernel(peers, row_cap, elements, groups, blocks, get, *refs):
    incoming, (conf, y, cols, table_high, table_low, out, spread) = refs[:blocks], refs[blocks:]
    slots = peers * row_cap
    message = jnp.concatenate([ref[...].reshape(-1, ref.shape[2]) for ref in incoming], axis=0)
    x = jnp.concatenate([*[message[:, g * STEP : (g + 1) * STEP] for g in range(groups)], conf[...]], axis=0)
    code_col = x[:, TAG_FACE : TAG_FACE + 1]
    count = x.shape[0]
    code_row = jnp.sum(jnp.where(iota((count, count), 0) == iota((count, count), 1), code_col, 0.0), axis=0, keepdims=True)
    order_col, elem_col = cols[:, 0:1], cols[:, 1:2]
    wanted = jnp.concatenate([jnp.where(elem_col > 0.0, elem_col + float(f * elements), -1.0) for f in range(FACES)], axis=0)
    gather = (wanted == code_row).astype(jnp.bfloat16)
    high, low = halves(x)
    face_sum = dot(gather, high) + dot(gather, low)
    spread[...] = jnp.zeros_like(spread)
    for f in range(FACES):
        for v in range(VARS):
            spread[v * slots : (v + 1) * slots, f * FACE_PAD : f * FACE_PAD + FLAT] = face_sum[
                f * slots : (f + 1) * slots, v * FLAT : (v + 1) * FLAT
            ]
    order_rows = jnp.concatenate([order_col] * VARS, axis=0)
    z = spread[...]
    wide = jnp.concatenate([jnp.where(order_rows == float(p), z, 0.0) for p in ORDERS], axis=1)
    high, low = halves(wide)
    total = y[...] + dot3(high, low, table_high[...], table_low[...])
    for v in range(VARS):
        out[:, :, v * ROW : (v + 1) * ROW] = total[v * slots : (v + 1) * slots].reshape(peers, row_cap, ROW)
    out[:, :, TAG_SLOT : TAG_SLOT + 1] = cols[:, 2:3].reshape(peers, row_cap, 1)


def place_kernel(peers, row_cap, get, arrived, out):
    elements = out.shape[0]
    rows = peers * row_cap
    message = arrived[...].reshape(rows, arrived.shape[2])
    x, slot_col = message[:, :TAG_SLOT], message[:, TAG_SLOT : TAG_SLOT + 1]
    slot_row = jnp.sum(jnp.where(iota((rows, rows), 0) == iota((rows, rows), 1), slot_col, 0.0), axis=0, keepdims=True)
    put = (iota((elements, rows), 0).astype(jnp.float32) + 1.0 == slot_row).astype(jnp.bfloat16)
    high, low = halves(x)
    rest = (x - high.astype(jnp.float32) - low.astype(jnp.float32)).astype(jnp.bfloat16)
    out[...] = dot(put, high) + dot(put, low) + dot(put, rest)


def fetched(kernel, n_far, n_pass, n_near, n_out, *refs):
    far, near, outs = refs[:n_far], refs[n_far : n_far + n_near], refs[n_far + n_near : n_far + n_near + n_out]
    rest = refs[n_far + n_near + n_out :]
    n_held = n_far - n_pass
    held, sems, scratch = rest[:n_held], rest[n_held], rest[n_held + 1 :]
    held = (*held, *outs[n_out - n_pass :])
    copies = [pltpu.make_async_copy(src, dst, sems.at[i]) for i, (src, dst) in enumerate(zip(far, held))]
    for copy in copies:
        copy.start()

    def get(i):
        copies[i].wait()
        return held[i][...]

    kernel(get, *near, *outs[: n_out - n_pass], *scratch)
    for copy in copies[n_held:]:
        copy.wait()


def like(a):
    return jax.ShapeDtypeStruct(a.shape, a.dtype)


def call(kernel, outs, far, near=(), scratch=(), hand_on=(), flops=0):
    outs = [*outs, *[like(a) for a in hand_on]]
    sizes = [np.prod(a.shape) * a.dtype.itemsize for a in (*far, *near, *outs)]
    held = [pltpu.VMEM(a.shape, a.dtype) for a in far]
    far = (*far, *hand_on)
    in_specs = [pl.BlockSpec(memory_space=pltpu.HBM)] * len(far) + [pl.BlockSpec(memory_space=pltpu.VMEM)] * len(near)
    return pl.pallas_call(
        functools.partial(fetched, kernel, len(far), len(hand_on), len(near), len(outs)),
        in_specs=in_specs,
        out_shape=outs,
        scratch_shapes=[*held, pltpu.SemaphoreType.DMA((max(1, len(far)),)), *scratch],
        compiler_params=pltpu.CompilerParams(vmem_limit_bytes=48 * 1024 * 1024),
        cost_estimate=pl.CostEstimate(flops=flops, bytes_accessed=int(sum(sizes)), transcendentals=0),
    )(*[pltpu.with_memory_space_constraint(a, pltpu.HBM) for a in far], *near)


def exchange(block):
    return lax.all_to_all(block, ("gy", "gx"), split_axis=0, concat_axis=0, tiled=True)


def exchange_traces(blocks):
    if len(blocks) == 1:
        return [exchange(blocks[0])]
    near, far = blocks
    far = lax.ppermute(far, "gx", [(0, 1), (1, 0)])
    size_y = near.shape[0]
    pair = jax.ShapeDtypeStruct((2, *near.shape[1:]), near.dtype)
    own, *others = call(pair_kernel, [pair] * size_y, (), (near, far))
    hops = [[(i, i ^ k) for i in range(size_y)] for k in range(1, size_y)]
    return [own, *[lax.ppermute(other, "gy", hop) for other, hop in zip(others, hops)]]


def from_behind(block, axis, distance):
    devices = range(lax.axis_size(axis))
    route = [((i - distance) % len(devices), i) for i in devices]
    return lax.ppermute(block, axis, route)


def body(
    adjoint,
    order,
    mortar_trace,
    mortar_sub,
    mortar_dest,
    mortar_elem,
    mortar_face,
    conf_trace,
    conf_elem,
    conf_face,
    coarse_row,
):
    elements = adjoint.shape[0]
    count = mortar_trace.shape[0]
    confs = conf_trace.shape[0]
    peers = lax.axis_size("gx") * lax.axis_size("gy")
    cap = max(2, 2 * count // peers)
    row_cap = max(2, elements // peers)
    slots = peers * row_cap
    groups = -(-cap // row_cap)
    lanes = groups * STEP
    lift, conf_lift, cell, face = [tuple(jnp.asarray(t) for t in pair) for pair in basis_tables()]
    f32 = jnp.float32
    line = lambda a: a.reshape(1, -1)
    order, coarse_row = line(order), line(coarse_row)
    blocks = 2 if pairwise() else 1
    conf, *outgoing = call(
        functools.partial(pack_kernel, peers, cap, row_cap, elements),
        [
            jax.ShapeDtypeStruct((confs, STEP), f32),
            *[jax.ShapeDtypeStruct((peers // blocks, row_cap, lanes), f32)] * blocks,
        ],
        (
            line(mortar_dest),
            line(mortar_sub),
            line(mortar_elem),
            line(mortar_face),
            mortar_trace,
            *lift,
            line(conf_face),
            line(conf_elem),
            conf_trace,
            *conf_lift,
        ),
    )
    incoming = exchange_traces(outgoing)
    conf = from_behind(conf, "gz", 1)
    y, cols, *face = call(
        functools.partial(cell_kernel, peers, row_cap),
        [jax.ShapeDtypeStruct((VARS * slots, ROW), f32), jax.ShapeDtypeStruct((slots, 128), f32)],
        (order, coarse_row, adjoint, *cell),
        scratch=[pltpu.VMEM((2, VARS * slots, CELL_PAD), f32)],
        hand_on=face,
    )
    (rows,) = call(
        functools.partial(face_kernel, peers, row_cap, elements, groups, len(incoming)),
        [jax.ShapeDtypeStruct((peers, row_cap, ROWS_PAD), f32)],
        (),
        (*incoming, conf, y, cols, *face),
        scratch=[pltpu.VMEM((VARS * slots, FACES_PAD), f32)],
    )
    (out,) = call(
        functools.partial(place_kernel, peers, row_cap),
        [jax.ShapeDtypeStruct((elements, VARS * ROW), f32)],
        (),
        (exchange(rows),),
    )
    return out


def solution(mesh):
    rows = P(("gx", "gy", "gz"))
    wide = P(("gx", "gy", "gz"), None)
    return jax.shard_map(
        body,
        mesh=mesh,
        in_specs=(wide, rows, wide, rows, wide, rows, rows, wide, rows, rows, rows),
        out_specs=wide,
        check_vma=False,
    )
```

```python
import functools

import jax
import jax.numpy as jnp
import ml_dtypes
import numpy as np
from jax import lax
from jax.experimental import pallas as pl
from jax.experimental.pallas import tpu as pltpu
from jax.sharding import PartitionSpec as P

VARS = 5
NODE = 7
FACE = NODE * NODE
CELL = NODE * FACE
ROW = 216
FACES = 6
ORDERS = (2, 3, 4, 5, 6)
TRACE = VARS * FACE
TRACE_PAD = 256
FLAT = 36
SENT = VARS * FLAT
STEP = SENT + 1
TAG_FACE = SENT
TAG_SLOT = VARS * ROW
ROW_STEP = TAG_SLOT + 1
CELL_PAD = 384
FACE_PAD = 40
FACES_PAD = 256


def grid_nodes(degree):
    return -np.cos(np.pi * np.arange(degree + 1) / degree)


def lagrange_rows(degree, points):
    anchors = grid_nodes(degree)
    values = np.ones((len(points), degree + 1))
    for k in range(degree + 1):
        for other in range(degree + 1):
            if other != k:
                values[:, k] *= (points - anchors[other]) / (anchors[k] - anchors[other])
    return values


def split_table(table):
    table = np.asarray(table, np.float32)
    high = table.astype(ml_dtypes.bfloat16)
    low = (table - high.astype(np.float32)).astype(ml_dtypes.bfloat16)
    return high, low


@functools.lru_cache(maxsize=None)
def basis_tables():
    top_nodes = grid_nodes(6)
    mortar = [lagrange_rows(6, (top_nodes - 1.0) / 2.0), lagrange_rows(6, (top_nodes + 1.0) / 2.0)]
    flat = lagrange_rows(5, top_nodes)
    lift = np.zeros((5, TRACE_PAD, STEP))
    for sub in range(5):
        both = (mortar[sub // 2] @ flat, mortar[sub % 2] @ flat) if sub < 4 else (flat, flat)
        for v in range(VARS):
            lift[sub, v * FACE : (v + 1) * FACE, v * FLAT : (v + 1) * FLAT] = np.kron(*both)
    cell = np.zeros((len(ORDERS), CELL_PAD, ROW))
    face = np.zeros((len(ORDERS), FACES_PAD, ROW))
    for index, p in enumerate(ORDERS):
        shrink = np.zeros((6, NODE))
        shrink[:p, : p + 1] = lagrange_rows(p - 1, grid_nodes(p)).T
        cell[index, :CELL] = np.einsum("ai,bj,ck->ijkabc", shrink, shrink, shrink).reshape(CELL, ROW)
        lower = np.zeros((6, 6))
        lower[:p] = lagrange_rows(p - 1, grid_nodes(5)).T
        low, high = shrink[:, 0], shrink[:, p]
        for axis, spec in enumerate(("c,ai,bj->ijcab", "c,ai,bj->ijacb", "c,ai,bj->ijabc")):
            for side, edge in enumerate((low, high)):
                first = (2 * axis + side) * FACE_PAD
                face[index, first : first + FLAT] = np.einsum(spec, edge, lower, lower).reshape(FLAT, ROW)
    return (
        split_table(lift[:2].reshape(-1, STEP)) + split_table(lift[2:4].reshape(-1, STEP)),
        split_table(lift[4]),
        split_table(cell.reshape(-1, ROW)),
        split_table(face.reshape(-1, ROW)),
    )


def iota(shape, axis):
    return lax.broadcasted_iota(jnp.int32, shape, axis)


def halves(x):
    high = x.astype(jnp.bfloat16)
    low = (x - high.astype(jnp.float32)).astype(jnp.bfloat16)
    return high, low


def dot(a, b):
    return jnp.dot(a, b, preferred_element_type=jnp.float32)


def dot3(high, low, table_high, table_low):
    return dot(high, table_high) + dot(low, table_high) + dot(high, table_low)


def earlier(member):
    count = member.shape[1]
    before = (iota((count, count), 0) < iota((count, count), 1)).astype(jnp.float32)
    return dot(member.astype(jnp.bfloat16), before.astype(jnp.bfloat16))


def device_of(shape):
    size_x, size_y = lax.axis_size("gx"), lax.axis_size("gy")
    rank = iota(shape, 0)
    return rank % size_x * size_y + rank // size_x


def sublanes(row_cap):
    return 2 if row_cap % 2 == 0 else 1


def place_of(member, per_group):
    peers, count = member.shape
    block = jnp.sum(member * iota(member.shape, 0).astype(jnp.float32), axis=0, keepdims=True)
    rank = jnp.sum(member * earlier(member), axis=0, keepdims=True)
    group = jnp.zeros_like(rank)
    for first in range(per_group, count, per_group):
        group = group + (rank >= float(first)).astype(jnp.float32)
    return group * float((peers - 1) * per_group) + block * float(per_group) + rank


def owner_of(crow, peers, elements):
    first = device_of((peers, crow.shape[1])) * elements
    return ((crow >= first) & (crow < first + elements)).astype(jnp.float32)


def row_places(crow, peers, row_cap, elements):
    member = owner_of(crow, peers, elements)
    owned = (device_of(member.shape) * elements).astype(jnp.float32)
    slot = crow.astype(jnp.float32) - jnp.sum(member * owned, axis=0, keepdims=True)
    return place_of(member, sublanes(row_cap)), slot


def onehot_rows(place, rows):
    return (iota((rows, place.shape[1]), 0).astype(jnp.float32) == place).astype(jnp.float32)


def column(onehot, values):
    return jnp.sum(onehot * values, axis=1, keepdims=True)


def pad_lanes(x, lanes):
    return jnp.concatenate([x, jnp.zeros((x.shape[0], lanes - x.shape[1]), x.dtype)], axis=1)


def pack_kernel(peers, cap, per_group, elements, get, out, conf_out, message, sent):
    dest, sub, trace = [get(i) for i in range(3)]
    groups, rows = -(-cap // per_group), peers * per_group
    member = (device_of((peers, dest.shape[1])) == dest).astype(jnp.float32)
    put = onehot_rows(place_of(member, per_group), groups * rows)
    sub_col = column(put, sub.astype(jnp.float32))
    move = put.astype(jnp.bfloat16)
    high, low = [dot(move, half) for half in halves(pad_lanes(trace, TRACE_PAD))]
    packed = jnp.zeros((groups * rows, STEP), jnp.float32)
    for first in (0, 2):
        wide = [
            jnp.concatenate([jnp.where(sub_col == float(s), x, 0.0).astype(jnp.bfloat16) for s in (first, first + 1)], axis=1)
            for x in (high, low)
        ]
        packed = packed + dot3(*wide, get(3 + first), get(4 + first))
    code_col = column(put, (get(8) * elements + get(7) + 1).astype(jnp.float32))
    packed = jnp.where(iota(packed.shape, 1) == TAG_FACE, code_col, packed)
    for g in range(groups):
        message[:, :, g * STEP : (g + 1) * STEP] = packed[g * rows : (g + 1) * rows].reshape(peers, per_group, STEP)
    send = pltpu.make_async_copy(message, out, sent.at[0])
    send.start()
    cface, celem = get(9), get(10)
    confs = cface.shape[1]
    eye = (iota((confs, confs), 0) == iota((confs, confs), 1)).astype(jnp.float32)
    conf_col = column(eye, (cface * elements + celem + 1).astype(jnp.float32))
    conf = dot3(*halves(pad_lanes(get(11), TRACE_PAD)), get(12), get(13))
    conf_out[...] = jnp.where(iota(conf.shape, 1) == TAG_FACE, conf_col, conf)
    send.wait()


def cell_kernel(peers, row_cap, get, y_out, col_out, spread):
    order, crow = get(0), get(1)
    elements = order.shape[1]
    slots = peers * row_cap
    place, slot = row_places(crow, peers, row_cap, elements)
    take = onehot_rows(place, slots)
    order_col = column(take, order.astype(jnp.float32))
    elem_col = column(take, iota((1, elements), 1).astype(jnp.float32) + 1.0)
    lane = iota((slots, 128), 1)
    slot_col = column(take, slot + 1.0)
    col_out[...] = jnp.where(lane == 0, order_col, jnp.where(lane == 1, elem_col, slot_col))
    take = take.astype(jnp.bfloat16)
    spread[...] = jnp.zeros_like(spread)
    for half, part in enumerate(halves(get(2))):
        moved = dot(take, part)
        for v in range(VARS):
            spread[half, v * slots : (v + 1) * slots, :CELL] = moved[:, v * CELL : (v + 1) * CELL]
    order_rows = jnp.concatenate([order_col] * VARS, axis=0)
    high, low = spread[0], spread[1]
    wide_high = jnp.concatenate([jnp.where(order_rows == float(p), high, 0.0).astype(jnp.bfloat16) for p in ORDERS], axis=1)
    wide_low = jnp.concatenate([jnp.where(order_rows == float(p), low, 0.0).astype(jnp.bfloat16) for p in ORDERS], axis=1)
    y_out[...] = dot3(wide_high, wide_low, get(3), get(4))


def face_kernel(peers, row_cap, elements, groups, get, incoming, conf, y, cols, table_high, table_low, out, spread):
    slots, per_group = peers * row_cap, sublanes(row_cap)
    message = incoming[...].reshape(peers * per_group, incoming.shape[2])
    x = jnp.concatenate([*[message[:, g * STEP : (g + 1) * STEP] for g in range(groups)], conf[...]], axis=0)
    code_col = x[:, TAG_FACE : TAG_FACE + 1]
    count = x.shape[0]
    code_row = jnp.sum(jnp.where(iota((count, count), 0) == iota((count, count), 1), code_col, 0.0), axis=0, keepdims=True)
    order_col, elem_col = cols[:, 0:1], cols[:, 1:2]
    wanted = jnp.concatenate([jnp.where(elem_col > 0.0, elem_col + float(f * elements), -1.0) for f in range(FACES)], axis=0)
    gather = (wanted == code_row).astype(jnp.bfloat16)
    high, low = halves(x)
    face_sum = dot(gather, high) + dot(gather, low)
    spread[...] = jnp.zeros_like(spread)
    for f in range(FACES):
        for v in range(VARS):
            spread[v * slots : (v + 1) * slots, f * FACE_PAD : f * FACE_PAD + FLAT] = face_sum[
                f * slots : (f + 1) * slots, v * FLAT : (v + 1) * FLAT
            ]
    order_rows = jnp.concatenate([order_col] * VARS, axis=0)
    z = spread[...]
    wide = jnp.concatenate([jnp.where(order_rows == float(p), z, 0.0) for p in ORDERS], axis=1)
    high, low = halves(wide)
    total = y[...] + dot3(high, low, table_high[...], table_low[...])
    rows = peers * per_group
    for j in range(row_cap // per_group):
        for v in range(VARS):
            part = total[v * slots + j * rows : v * slots + (j + 1) * rows]
            first = j * ROW_STEP + v * ROW
            out[:, :, first : first + ROW] = part.reshape(peers, per_group, ROW)
        tag = cols[j * rows : (j + 1) * rows, 2:3]
        first = j * ROW_STEP + TAG_SLOT
        out[:, :, first : first + 1] = tag.reshape(peers, per_group, 1)


def place_kernel(peers, row_cap, get, arrived, out):
    elements, rows, per_group = out.shape[0], peers * row_cap, sublanes(row_cap)
    message = arrived[...].reshape(peers * per_group, arrived.shape[2])
    parts = [message[:, j * ROW_STEP : (j + 1) * ROW_STEP] for j in range(row_cap // per_group)]
    x = jnp.concatenate([part[:, :TAG_SLOT] for part in parts], axis=0)
    slot_col = jnp.concatenate([part[:, TAG_SLOT:] for part in parts], axis=0)
    slot_row = jnp.sum(jnp.where(iota((rows, rows), 0) == iota((rows, rows), 1), slot_col, 0.0), axis=0, keepdims=True)
    put = (iota((elements, rows), 0).astype(jnp.float32) + 1.0 == slot_row).astype(jnp.bfloat16)
    high, low = halves(x)
    rest = (x - high.astype(jnp.float32) - low.astype(jnp.float32)).astype(jnp.bfloat16)
    out[...] = dot(put, high) + dot(put, low) + dot(put, rest)


def fetched(kernel, n_far, n_pass, n_near, n_out, *refs):
    far, near, outs = refs[:n_far], refs[n_far : n_far + n_near], refs[n_far + n_near : n_far + n_near + n_out]
    rest = refs[n_far + n_near + n_out :]
    n_held = n_far - n_pass
    held, sems, scratch = rest[:n_held], rest[n_held], rest[n_held + 1 :]
    held = (*held, *outs[n_out - n_pass :])
    copies = [pltpu.make_async_copy(src, dst, sems.at[i]) for i, (src, dst) in enumerate(zip(far, held))]
    for copy in copies:
        copy.start()

    def get(i):
        copies[i].wait()
        return held[i][...]

    kernel(get, *near, *outs[: n_out - n_pass], *scratch)
    for copy in copies[n_held:]:
        copy.wait()


def like(a):
    return jax.ShapeDtypeStruct(a.shape, a.dtype)


def call(kernel, outs, far, near=(), scratch=(), hand_on=(), flops=0):
    outs = [*outs, *[like(a) for a in hand_on]]
    out_specs = [pl.BlockSpec(memory_space=getattr(a, "memory_space", None) or pltpu.VMEM) for a in outs]
    sizes = [np.prod(a.shape) * a.dtype.itemsize for a in (*far, *near, *outs)]
    held = [pltpu.VMEM(a.shape, a.dtype) for a in far]
    far = (*far, *hand_on)
    in_specs = [pl.BlockSpec(memory_space=pltpu.HBM)] * len(far) + [pl.BlockSpec(memory_space=pltpu.VMEM)] * len(near)
    return pl.pallas_call(
        functools.partial(fetched, kernel, len(far), len(hand_on), len(near), len(outs)),
        in_specs=in_specs,
        out_specs=out_specs,
        out_shape=outs,
        scratch_shapes=[*held, pltpu.SemaphoreType.DMA((max(1, len(far)),)), *scratch],
        compiler_params=pltpu.CompilerParams(vmem_limit_bytes=48 * 1024 * 1024),
        cost_estimate=pl.CostEstimate(flops=flops, bytes_accessed=int(sum(sizes)), transcendentals=0),
    )(*[pltpu.with_memory_space_constraint(a, pltpu.HBM) for a in far], *near)


def exchange(block):
    return lax.all_to_all(block, ("gy", "gx"), split_axis=0, concat_axis=0, tiled=True)


def from_behind(block, axis, distance):
    devices = range(lax.axis_size(axis))
    route = [((i - distance) % len(devices), i) for i in devices]
    return lax.ppermute(block, axis, route)


def body(
    adjoint,
    order,
    mortar_trace,
    mortar_sub,
    mortar_dest,
    mortar_elem,
    mortar_face,
    conf_trace,
    conf_elem,
    conf_face,
    coarse_row,
):
    elements = adjoint.shape[0]
    count = mortar_trace.shape[0]
    confs = conf_trace.shape[0]
    peers = lax.axis_size("gx") * lax.axis_size("gy")
    cap = max(2, 2 * count // peers)
    row_cap = max(2, elements // peers)
    slots = peers * row_cap
    per_group = sublanes(row_cap)
    groups = -(-cap // per_group)
    lift, conf_lift, cell, face = [tuple(jnp.asarray(t) for t in pair) for pair in basis_tables()]
    f32 = jnp.float32
    line = lambda a: a.reshape(1, -1)
    order, coarse_row = line(order), line(coarse_row)
    message = (peers, per_group, groups * STEP)
    outgoing, conf = call(
        functools.partial(pack_kernel, peers, cap, per_group, elements),
        [pltpu.HBM(message, f32), jax.ShapeDtypeStruct((confs, STEP), f32)],
        (
            line(mortar_dest),
            line(mortar_sub),
            mortar_trace,
            *lift,
            line(mortar_elem),
            line(mortar_face),
            line(conf_face),
            line(conf_elem),
            conf_trace,
            *conf_lift,
        ),
        scratch=[pltpu.VMEM(message, f32), pltpu.SemaphoreType.DMA((1,))],
    )
    incoming = exchange(outgoing)
    conf = from_behind(conf, "gz", 1)
    y, cols, *face = call(
        functools.partial(cell_kernel, peers, row_cap),
        [jax.ShapeDtypeStruct((VARS * slots, ROW), f32), jax.ShapeDtypeStruct((slots, 128), f32)],
        (order, coarse_row, adjoint, *cell),
        scratch=[pltpu.VMEM((2, VARS * slots, CELL_PAD), f32)],
        hand_on=face,
    )
    (rows,) = call(
        functools.partial(face_kernel, peers, row_cap, elements, groups),
        [jax.ShapeDtypeStruct((peers, per_group, row_cap // per_group * ROW_STEP), f32)],
        (),
        (incoming, conf, y, cols, *face),
        scratch=[pltpu.VMEM((VARS * slots, FACES_PAD), f32)],
    )
    (out,) = call(
        functools.partial(place_kernel, peers, row_cap),
        [jax.ShapeDtypeStruct((elements, VARS * ROW), f32)],
        (),
        (exchange(rows),),
    )
    return out


def solution(mesh):
    rows = P(("gx", "gy", "gz"))
    wide = P(("gx", "gy", "gz"), None)
    return jax.shard_map(
        body,
        mesh=mesh,
        in_specs=(wide, rows, wide, rows, wide, rows, rows, wide, rows, rows, rows),
        out_specs=wide,
        check_vma=False,
    )
```

```python
import functools

import jax
import jax.numpy as jnp
import ml_dtypes
import numpy as np
from jax import lax
from jax.experimental import pallas as pl
from jax.experimental.pallas import tpu as pltpu
from jax.sharding import PartitionSpec as P

VARS = 5
NODE = 7
FACE = NODE * NODE
CELL = NODE * FACE
ROW = 216
FACES = 6
ORDERS = (2, 3, 4, 5, 6)
TRACE = VARS * FACE
TRACE_PAD = 256
FLAT = 36
SENT = VARS * FLAT
STEP = 192
TAG_FACE = SENT
ROWS_PAD = 1152
TAG_SLOT = VARS * ROW
CELL_PAD = 384
FACE_PAD = 40
FACES_PAD = 256


def grid_nodes(degree):
    return -np.cos(np.pi * np.arange(degree + 1) / degree)


def lagrange_rows(degree, points):
    anchors = grid_nodes(degree)
    values = np.ones((len(points), degree + 1))
    for k in range(degree + 1):
        for other in range(degree + 1):
            if other != k:
                values[:, k] *= (points - anchors[other]) / (anchors[k] - anchors[other])
    return values


def split_table(table):
    table = np.asarray(table, np.float32)
    high = table.astype(ml_dtypes.bfloat16)
    low = (table - high.astype(np.float32)).astype(ml_dtypes.bfloat16)
    return high, low


@functools.lru_cache(maxsize=None)
def basis_tables():
    top_nodes = grid_nodes(6)
    mortar = [lagrange_rows(6, (top_nodes - 1.0) / 2.0), lagrange_rows(6, (top_nodes + 1.0) / 2.0)]
    flat = lagrange_rows(5, top_nodes)
    lift = np.zeros((5, TRACE_PAD, STEP))
    for sub in range(5):
        both = (mortar[sub // 2] @ flat, mortar[sub % 2] @ flat) if sub < 4 else (flat, flat)
        for v in range(VARS):
            lift[sub, v * FACE : (v + 1) * FACE, v * FLAT : (v + 1) * FLAT] = np.kron(*both)
    cell = np.zeros((len(ORDERS), CELL_PAD, ROW))
    face = np.zeros((len(ORDERS), FACES_PAD, ROW))
    for index, p in enumerate(ORDERS):
        shrink = np.zeros((6, NODE))
        shrink[:p, : p + 1] = lagrange_rows(p - 1, grid_nodes(p)).T
        cell[index, :CELL] = np.einsum("ai,bj,ck->ijkabc", shrink, shrink, shrink).reshape(CELL, ROW)
        lower = np.zeros((6, 6))
        lower[:p] = lagrange_rows(p - 1, grid_nodes(5)).T
        low, high = shrink[:, 0], shrink[:, p]
        for axis, spec in enumerate(("c,ai,bj->ijcab", "c,ai,bj->ijacb", "c,ai,bj->ijabc")):
            for side, edge in enumerate((low, high)):
                first = (2 * axis + side) * FACE_PAD
                face[index, first : first + FLAT] = np.einsum(spec, edge, lower, lower).reshape(FLAT, ROW)
    return (
        split_table(lift[:4].transpose(1, 0, 2).reshape(TRACE_PAD, -1)),
        split_table(lift[4]),
        split_table(cell.reshape(-1, ROW)),
        split_table(face.reshape(-1, ROW)),
    )


def iota(shape, axis):
    return lax.broadcasted_iota(jnp.int32, shape, axis)


def halves(x):
    high = x.astype(jnp.bfloat16)
    low = (x - high.astype(jnp.float32)).astype(jnp.bfloat16)
    return high, low


def dot(a, b):
    return jnp.dot(a, b, preferred_element_type=jnp.float32)


def dot3(high, low, table_high, table_low):
    return dot(high, table_high) + dot(low, table_high) + dot(high, table_low)


def earlier(member):
    count = member.shape[1]
    before = (iota((count, count), 0) < iota((count, count), 1)).astype(jnp.float32)
    return dot(member.astype(jnp.bfloat16), before.astype(jnp.bfloat16))


def device_of(shape):
    size_x, size_y = lax.axis_size("gx"), lax.axis_size("gy")
    rank = iota(shape, 0)
    return rank % size_x * size_y + rank // size_x


def owner_of(crow, peers, elements):
    first = device_of((peers, crow.shape[1])) * elements
    return ((crow >= first) & (crow < first + elements)).astype(jnp.float32)


def row_places(crow, peers, elements, stride):
    member = owner_of(crow, peers, elements)
    rank = earlier(member)
    block = iota(member.shape, 0).astype(jnp.float32)
    place = jnp.sum(member * (block * stride + rank), axis=0, keepdims=True)
    owned = (device_of(member.shape) * elements).astype(jnp.float32)
    slot = crow.astype(jnp.float32) - jnp.sum(member * owned, axis=0, keepdims=True)
    return place, slot


def onehot_rows(place, rows):
    return (iota((rows, place.shape[1]), 0).astype(jnp.float32) == place).astype(jnp.float32)


def column(onehot, values):
    return jnp.sum(onehot * values, axis=1, keepdims=True)


def pad_lanes(x, lanes):
    return jnp.concatenate([x, jnp.zeros((x.shape[0], lanes - x.shape[1]), x.dtype)], axis=1)


def pack_kernel(peers, cap, row_cap, elements, get, out, conf_out, message, sent):
    dest, elem, face, sub = [get(i) for i in range(4)]
    count = dest.shape[1]
    groups, slots = -(-cap // row_cap), peers * row_cap
    member = (device_of((peers, count)) == dest).astype(jnp.float32)
    block = jnp.sum(member * iota(member.shape, 0).astype(jnp.float32), axis=0, keepdims=True)
    rank = jnp.sum(member * earlier(member), axis=0, keepdims=True)
    group = sum([(rank >= float(g * row_cap)).astype(jnp.float32) for g in range(1, groups)], jnp.zeros_like(rank))
    place = group * float(slots - row_cap) + block * float(row_cap) + rank
    put = onehot_rows(place, groups * slots)
    code_col = column(put, (face * elements + elem + 1).astype(jnp.float32))
    eye = (iota((count, count), 0) == iota((count, count), 1)).astype(jnp.float32)
    sub_col = column(eye, sub.astype(jnp.float32))
    lifts = dot3(*halves(pad_lanes(get(4), TRACE_PAD)), get(5), get(6))
    lifted = lifts[:, :STEP]
    for s in range(1, 4):
        lifted = jnp.where(sub_col == float(s), lifts[:, s * STEP : (s + 1) * STEP], lifted)
    lifted_high, lifted_low = halves(lifted)
    put = put.astype(jnp.bfloat16)
    packed = dot(put, lifted_high) + dot(put, lifted_low)
    packed = jnp.where(iota(packed.shape, 1) == TAG_FACE, code_col, packed)
    for g in range(groups):
        message[:, :, g * STEP : (g + 1) * STEP] = packed[g * slots : (g + 1) * slots].reshape(peers, row_cap, STEP)
    send = pltpu.make_async_copy(message, out, sent.at[0])
    send.start()
    cface, celem = get(7), get(8)
    confs = cface.shape[1]
    eye = (iota((confs, confs), 0) == iota((confs, confs), 1)).astype(jnp.float32)
    conf_col = column(eye, (cface * elements + celem + 1).astype(jnp.float32))
    conf = dot3(*halves(pad_lanes(get(9), TRACE_PAD)), get(10), get(11))
    conf_out[...] = jnp.where(iota(conf.shape, 1) == TAG_FACE, conf_col, conf)
    send.wait()


def cell_kernel(peers, row_cap, get, y_out, col_out, spread):
    order, crow = get(0), get(1)
    elements = order.shape[1]
    slots = peers * row_cap
    place, slot = row_places(crow, peers, elements, row_cap)
    take = onehot_rows(place, slots)
    order_col = column(take, order.astype(jnp.float32))
    elem_col = column(take, iota((1, elements), 1).astype(jnp.float32) + 1.0)
    lane = iota((slots, 128), 1)
    slot_col = column(take, slot + 1.0)
    col_out[...] = jnp.where(lane == 0, order_col, jnp.where(lane == 1, elem_col, slot_col))
    take = take.astype(jnp.bfloat16)
    spread[...] = jnp.zeros_like(spread)
    for half, part in enumerate(halves(get(2))):
        moved = dot(take, part)
        for v in range(VARS):
            spread[half, v * slots : (v + 1) * slots, :CELL] = moved[:, v * CELL : (v + 1) * CELL]
    order_rows = jnp.concatenate([order_col] * VARS, axis=0)
    high, low = spread[0], spread[1]
    wide_high = jnp.concatenate([jnp.where(order_rows == float(p), high, 0.0).astype(jnp.bfloat16) for p in ORDERS], axis=1)
    wide_low = jnp.concatenate([jnp.where(order_rows == float(p), low, 0.0).astype(jnp.bfloat16) for p in ORDERS], axis=1)
    y_out[...] = dot3(wide_high, wide_low, get(3), get(4))


def face_kernel(peers, row_cap, elements, groups, get, incoming, conf, y, cols, table_high, table_low, out, spread):
    slots = peers * row_cap
    message = incoming[...].reshape(slots, incoming.shape[2])
    x = jnp.concatenate([*[message[:, g * STEP : (g + 1) * STEP] for g in range(groups)], conf[...]], axis=0)
    code_col = x[:, TAG_FACE : TAG_FACE + 1]
    count = x.shape[0]
    code_row = jnp.sum(jnp.where(iota((count, count), 0) == iota((count, count), 1), code_col, 0.0), axis=0, keepdims=True)
    order_col, elem_col = cols[:, 0:1], cols[:, 1:2]
    wanted = jnp.concatenate([jnp.where(elem_col > 0.0, elem_col + float(f * elements), -1.0) for f in range(FACES)], axis=0)
    gather = (wanted == code_row).astype(jnp.bfloat16)
    high, low = halves(x)
    face_sum = dot(gather, high) + dot(gather, low)
    spread[...] = jnp.zeros_like(spread)
    for f in range(FACES):
        for v in range(VARS):
            spread[v * slots : (v + 1) * slots, f * FACE_PAD : f * FACE_PAD + FLAT] = face_sum[
                f * slots : (f + 1) * slots, v * FLAT : (v + 1) * FLAT
            ]
    order_rows = jnp.concatenate([order_col] * VARS, axis=0)
    masks = [(order_rows == float(p)).astype(jnp.bfloat16) for p in ORDERS]
    high, low = [jnp.concatenate([half * mask for mask in masks], axis=1) for half in halves(spread[...])]
    total = y[...] + dot3(high, low, table_high[...], table_low[...])
    for v in range(VARS):
        out[:, :, v * ROW : (v + 1) * ROW] = total[v * slots : (v + 1) * slots].reshape(peers, row_cap, ROW)
    out[:, :, TAG_SLOT : TAG_SLOT + 1] = cols[:, 2:3].reshape(peers, row_cap, 1)


def place_kernel(peers, row_cap, get, arrived, out):
    elements = out.shape[0]
    rows = peers * row_cap
    message = arrived[...].reshape(rows, arrived.shape[2])
    x, slot_col = message[:, :TAG_SLOT], message[:, TAG_SLOT : TAG_SLOT + 1]
    slot_row = jnp.sum(jnp.where(iota((rows, rows), 0) == iota((rows, rows), 1), slot_col, 0.0), axis=0, keepdims=True)
    put = (iota((elements, rows), 0).astype(jnp.float32) + 1.0 == slot_row).astype(jnp.bfloat16)
    high, low = halves(x)
    out[...] = dot(put, high) + dot(put, low)


def fetched(kernel, n_far, n_pass, n_near, n_out, *refs):
    far, near, outs = refs[:n_far], refs[n_far : n_far + n_near], refs[n_far + n_near : n_far + n_near + n_out]
    rest = refs[n_far + n_near + n_out :]
    n_held = n_far - n_pass
    held, sems, scratch = rest[:n_held], rest[n_held], rest[n_held + 1 :]
    held = (*held, *outs[n_out - n_pass :])
    copies = [pltpu.make_async_copy(src, dst, sems.at[i]) for i, (src, dst) in enumerate(zip(far, held))]
    for copy in copies:
        copy.start()

    def get(i):
        copies[i].wait()
        return held[i][...]

    kernel(get, *near, *outs[: n_out - n_pass], *scratch)
    for copy in copies[n_held:]:
        copy.wait()


def like(a):
    return jax.ShapeDtypeStruct(a.shape, a.dtype)


def call(kernel, outs, far, near=(), scratch=(), hand_on=(), flops=0):
    outs = [*outs, *[like(a) for a in hand_on]]
    out_specs = [pl.BlockSpec(memory_space=getattr(a, "memory_space", None) or pltpu.VMEM) for a in outs]
    sizes = [np.prod(a.shape) * a.dtype.itemsize for a in (*far, *near, *outs)]
    held = [pltpu.VMEM(a.shape, a.dtype) for a in far]
    far = (*far, *hand_on)
    in_specs = [pl.BlockSpec(memory_space=pltpu.HBM)] * len(far) + [pl.BlockSpec(memory_space=pltpu.VMEM)] * len(near)
    return pl.pallas_call(
        functools.partial(fetched, kernel, len(far), len(hand_on), len(near), len(outs)),
        in_specs=in_specs,
        out_specs=out_specs,
        out_shape=outs,
        scratch_shapes=[*held, pltpu.SemaphoreType.DMA((max(1, len(far)),)), *scratch],
        compiler_params=pltpu.CompilerParams(vmem_limit_bytes=48 * 1024 * 1024),
        cost_estimate=pl.CostEstimate(flops=flops, bytes_accessed=int(sum(sizes)), transcendentals=0),
    )(*[pltpu.with_memory_space_constraint(a, pltpu.HBM) for a in far], *near)


def exchange(block):
    return lax.all_to_all(block, ("gy", "gx"), split_axis=0, concat_axis=0, tiled=True)


def from_behind(block, axis, distance):
    devices = range(lax.axis_size(axis))
    route = [((i - distance) % len(devices), i) for i in devices]
    return lax.ppermute(block, axis, route)


def body(
    adjoint,
    order,
    mortar_trace,
    mortar_sub,
    mortar_dest,
    mortar_elem,
    mortar_face,
    conf_trace,
    conf_elem,
    conf_face,
    coarse_row,
):
    elements = adjoint.shape[0]
    count = mortar_trace.shape[0]
    confs = conf_trace.shape[0]
    peers = lax.axis_size("gx") * lax.axis_size("gy")
    cap = max(2, 2 * count // peers)
    row_cap = max(2, elements // peers)
    slots = peers * row_cap
    groups = -(-cap // row_cap)
    lanes = groups * STEP
    lift, conf_lift, cell, face = [tuple(jnp.asarray(t) for t in pair) for pair in basis_tables()]
    f32 = jnp.float32
    line = lambda a: a.reshape(1, -1)
    order, coarse_row = line(order), line(coarse_row)
    message = (peers, row_cap, lanes)
    outgoing, conf = call(
        functools.partial(pack_kernel, peers, cap, row_cap, elements),
        [pltpu.HBM(message, f32), jax.ShapeDtypeStruct((confs, STEP), f32)],
        (
            line(mortar_dest),
            line(mortar_elem),
            line(mortar_face),
            line(mortar_sub),
            mortar_trace,
            *lift,
            line(conf_face),
            line(conf_elem),
            conf_trace,
            *conf_lift,
        ),
        scratch=[pltpu.VMEM(message, f32), pltpu.SemaphoreType.DMA((1,))],
    )
    incoming = exchange(outgoing)
    conf = from_behind(conf, "gz", 1)
    y, cols, *face = call(
        functools.partial(cell_kernel, peers, row_cap),
        [jax.ShapeDtypeStruct((VARS * slots, ROW), f32), jax.ShapeDtypeStruct((slots, 128), f32)],
        (order, coarse_row, adjoint, *cell),
        scratch=[pltpu.VMEM((2, VARS * slots, CELL_PAD), f32)],
        hand_on=face,
    )
    (rows,) = call(
        functools.partial(face_kernel, peers, row_cap, elements, groups),
        [jax.ShapeDtypeStruct((peers, row_cap, ROWS_PAD), f32)],
        (),
        (incoming, conf, y, cols, *face),
        scratch=[pltpu.VMEM((VARS * slots, FACES_PAD), f32)],
    )
    (out,) = call(
        functools.partial(place_kernel, peers, row_cap),
        [jax.ShapeDtypeStruct((elements, VARS * ROW), f32)],
        (),
        (exchange(rows),),
    )
    return out


def solution(mesh):
    rows = P(("gx", "gy", "gz"))
    wide = P(("gx", "gy", "gz"), None)
    return jax.shard_map(
        body,
        mesh=mesh,
        in_specs=(wide, rows, wide, rows, wide, rows, rows, wide, rows, rows, rows),
        out_specs=wide,
        check_vma=False,
    )
```

```python
import functools

import jax
import jax.numpy as jnp
import ml_dtypes
import numpy as np
from jax import lax
from jax.experimental import pallas as pl
from jax.experimental.pallas import tpu as pltpu
from jax.sharding import PartitionSpec as P

VARS = 5
NODE = 7
FACE = NODE * NODE
CELL = NODE * FACE
ROW = 216
FACES = 6
ORDERS = (2, 3, 4, 5, 6)
TRACE = VARS * FACE
TRACE_PAD = 256
FLAT = 36
SENT = VARS * FLAT
STEP = 192
TAG_FACE = SENT
ROWS_PAD = 1152
TAG_SLOT = VARS * ROW
CELL_PAD = 384
FACE_PAD = 40
FACES_PAD = 256


def grid_nodes(degree):
    return -np.cos(np.pi * np.arange(degree + 1) / degree)


def lagrange_rows(degree, points):
    anchors = grid_nodes(degree)
    values = np.ones((len(points), degree + 1))
    for k in range(degree + 1):
        for other in range(degree + 1):
            if other != k:
                values[:, k] *= (points - anchors[other]) / (anchors[k] - anchors[other])
    return values


def split_table(table):
    table = np.asarray(table, np.float32)
    high = table.astype(ml_dtypes.bfloat16)
    low = (table - high.astype(np.float32)).astype(ml_dtypes.bfloat16)
    return high, low


@functools.lru_cache(maxsize=None)
def basis_tables():
    top_nodes = grid_nodes(6)
    mortar = [lagrange_rows(6, (top_nodes - 1.0) / 2.0), lagrange_rows(6, (top_nodes + 1.0) / 2.0)]
    flat = lagrange_rows(5, top_nodes)
    lift = np.zeros((5, TRACE_PAD, STEP))
    for sub in range(5):
        both = (mortar[sub // 2] @ flat, mortar[sub % 2] @ flat) if sub < 4 else (flat, flat)
        for v in range(VARS):
            lift[sub, v * FACE : (v + 1) * FACE, v * FLAT : (v + 1) * FLAT] = np.kron(*both)
    cell = np.zeros((len(ORDERS), CELL_PAD, ROW))
    face = np.zeros((len(ORDERS), FACES_PAD, ROW))
    for index, p in enumerate(ORDERS):
        shrink = np.zeros((6, NODE))
        shrink[:p, : p + 1] = lagrange_rows(p - 1, grid_nodes(p)).T
        cell[index, :CELL] = np.einsum("ai,bj,ck->ijkabc", shrink, shrink, shrink).reshape(CELL, ROW)
        lower = np.zeros((6, 6))
        lower[:p] = lagrange_rows(p - 1, grid_nodes(5)).T
        low, high = shrink[:, 0], shrink[:, p]
        for axis, spec in enumerate(("c,ai,bj->ijcab", "c,ai,bj->ijacb", "c,ai,bj->ijabc")):
            for side, edge in enumerate((low, high)):
                first = (2 * axis + side) * FACE_PAD
                face[index, first : first + FLAT] = np.einsum(spec, edge, lower, lower).reshape(FLAT, ROW)
    return (
        split_table(lift[:2].reshape(-1, STEP)) + split_table(lift[2:4].reshape(-1, STEP)),
        split_table(lift[4]),
        split_table(cell.reshape(-1, ROW)),
        split_table(face.reshape(-1, ROW)),
    )


def iota(shape, axis):
    return lax.broadcasted_iota(jnp.int32, shape, axis)


def halves(x):
    high = x.astype(jnp.bfloat16)
    low = (x - high.astype(jnp.float32)).astype(jnp.bfloat16)
    return high, low


def dot(a, b):
    return jnp.dot(a, b, preferred_element_type=jnp.float32)


def dot3(high, low, table_high, table_low):
    return dot(high, table_high) + dot(low, table_high) + dot(high, table_low)


def earlier(member):
    count = member.shape[1]
    before = (iota((count, count), 0) < iota((count, count), 1)).astype(jnp.float32)
    return dot(member.astype(jnp.bfloat16), before.astype(jnp.bfloat16))


def device_of(shape):
    size_x, size_y = lax.axis_size("gx"), lax.axis_size("gy")
    rank = iota(shape, 0)
    return rank % size_x * size_y + rank // size_x


def owner_of(crow, peers, elements):
    first = device_of((peers, crow.shape[1])) * elements
    return ((crow >= first) & (crow < first + elements)).astype(jnp.float32)


def row_places(crow, peers, elements, stride):
    member = owner_of(crow, peers, elements)
    rank = earlier(member)
    block = iota(member.shape, 0).astype(jnp.float32)
    place = jnp.sum(member * (block * stride + rank), axis=0, keepdims=True)
    owned = (device_of(member.shape) * elements).astype(jnp.float32)
    slot = crow.astype(jnp.float32) - jnp.sum(member * owned, axis=0, keepdims=True)
    return place, slot


def onehot_rows(place, rows):
    return (iota((rows, place.shape[1]), 0).astype(jnp.float32) == place).astype(jnp.float32)


def column(onehot, values):
    return jnp.sum(onehot * values, axis=1, keepdims=True)


def pad_lanes(x, lanes):
    return jnp.concatenate([x, jnp.zeros((x.shape[0], lanes - x.shape[1]), x.dtype)], axis=1)


def pack_kernel(peers, cap, row_cap, elements, get, out, conf_out, message, sent):
    dest, sub = get(0), get(1)
    count = dest.shape[1]
    groups, slots = -(-cap // row_cap), peers * row_cap
    member = (device_of((peers, count)) == dest).astype(jnp.float32)
    block = jnp.sum(member * iota(member.shape, 0).astype(jnp.float32), axis=0, keepdims=True)
    rank = jnp.sum(member * earlier(member), axis=0, keepdims=True)
    group = sum([(rank >= float(g * row_cap)).astype(jnp.float32) for g in range(1, groups)], jnp.zeros_like(rank))
    place = group * float(slots - row_cap) + block * float(row_cap) + rank
    put = onehot_rows(place, groups * slots)
    eye = (iota((count, count), 0) == iota((count, count), 1)).astype(jnp.float32)
    sub_col = column(eye, sub.astype(jnp.float32))
    high, low = halves(pad_lanes(get(2), TRACE_PAD))
    masks = [(sub_col == float(s)).astype(jnp.bfloat16) for s in range(4)]
    lifted = jnp.zeros((count, STEP), jnp.float32)
    for first in (0, 2):
        wide = [jnp.concatenate([half * mask for mask in masks[first : first + 2]], axis=1) for half in (high, low)]
        lifted = lifted + dot3(*wide, get(3 + first), get(4 + first))
    lifted_high, lifted_low = halves(lifted)
    code_col = column(put, (get(8) * elements + get(7) + 1).astype(jnp.float32))
    put = put.astype(jnp.bfloat16)
    packed = dot(put, lifted_high) + dot(put, lifted_low)
    packed = jnp.where(iota(packed.shape, 1) == TAG_FACE, code_col, packed)
    bounds = (0, groups // 2 // 2 * 2, groups)
    sends = []
    for half, (first, last) in enumerate(zip(bounds[:-1], bounds[1:])):
        if first == last:
            continue
        for g in range(first, last):
            message[:, :, g * STEP : (g + 1) * STEP] = packed[g * slots : (g + 1) * slots].reshape(peers, row_cap, STEP)
        lanes = pl.ds(first * STEP, (last - first) * STEP)
        send = pltpu.make_async_copy(message.at[:, :, lanes], out.at[:, :, lanes], sent.at[half])
        send.start()
        sends.append(send)
    cface, celem = get(9), get(10)
    confs = cface.shape[1]
    eye = (iota((confs, confs), 0) == iota((confs, confs), 1)).astype(jnp.float32)
    conf_col = column(eye, (cface * elements + celem + 1).astype(jnp.float32))
    conf = dot3(*halves(pad_lanes(get(11), TRACE_PAD)), get(12), get(13))
    conf_out[...] = jnp.where(iota(conf.shape, 1) == TAG_FACE, conf_col, conf)
    for send in sends:
        send.wait()


def cell_kernel(peers, row_cap, get, y_out, col_out, spread):
    order, crow = get(0), get(1)
    elements = order.shape[1]
    slots = peers * row_cap
    place, slot = row_places(crow, peers, elements, row_cap)
    take = onehot_rows(place, slots)
    order_col = column(take, order.astype(jnp.float32))
    elem_col = column(take, iota((1, elements), 1).astype(jnp.float32) + 1.0)
    lane = iota((slots, 128), 1)
    slot_col = column(take, slot + 1.0)
    col_out[...] = jnp.where(lane == 0, order_col, jnp.where(lane == 1, elem_col, slot_col))
    take = take.astype(jnp.bfloat16)
    spread[...] = jnp.zeros_like(spread)
    for half, part in enumerate(halves(get(2))):
        moved = dot(take, part)
        for v in range(VARS):
            spread[half, v * slots : (v + 1) * slots, :CELL] = moved[:, v * CELL : (v + 1) * CELL]
    order_rows = jnp.concatenate([order_col] * VARS, axis=0)
    high, low = spread[0], spread[1]
    wide_high = jnp.concatenate([jnp.where(order_rows == float(p), high, 0.0).astype(jnp.bfloat16) for p in ORDERS], axis=1)
    wide_low = jnp.concatenate([jnp.where(order_rows == float(p), low, 0.0).astype(jnp.bfloat16) for p in ORDERS], axis=1)
    y_out[...] = dot3(wide_high, wide_low, get(3), get(4))


def face_kernel(peers, row_cap, elements, groups, get, incoming, conf, y, cols, table_high, table_low, out, spread):
    slots = peers * row_cap
    message = incoming[...].reshape(slots, incoming.shape[2])
    x = jnp.concatenate([*[message[:, g * STEP : (g + 1) * STEP] for g in range(groups)], conf[...]], axis=0)
    code_col = x[:, TAG_FACE : TAG_FACE + 1]
    count = x.shape[0]
    code_row = jnp.sum(jnp.where(iota((count, count), 0) == iota((count, count), 1), code_col, 0.0), axis=0, keepdims=True)
    order_col, elem_col = cols[:, 0:1], cols[:, 1:2]
    wanted = jnp.concatenate([jnp.where(elem_col > 0.0, elem_col + float(f * elements), -1.0) for f in range(FACES)], axis=0)
    gather = (wanted == code_row).astype(jnp.bfloat16)
    high, low = halves(x)
    face_sum = dot(gather, high) + dot(gather, low)
    spread[...] = jnp.zeros_like(spread)
    for f in range(FACES):
        for v in range(VARS):
            spread[v * slots : (v + 1) * slots, f * FACE_PAD : f * FACE_PAD + FLAT] = face_sum[
                f * slots : (f + 1) * slots, v * FLAT : (v + 1) * FLAT
            ]
    order_rows = jnp.concatenate([order_col] * VARS, axis=0)
    z = spread[...]
    wide = jnp.concatenate([jnp.where(order_rows == float(p), z, 0.0) for p in ORDERS], axis=1)
    high, low = halves(wide)
    total = y[...] + dot3(high, low, table_high[...], table_low[...])
    for v in range(VARS):
        out[:, :, v * ROW : (v + 1) * ROW] = total[v * slots : (v + 1) * slots].reshape(peers, row_cap, ROW)
    out[:, :, TAG_SLOT : TAG_SLOT + 1] = cols[:, 2:3].reshape(peers, row_cap, 1)


def place_kernel(peers, row_cap, get, arrived, out):
    elements = out.shape[0]
    rows = peers * row_cap
    message = arrived[...].reshape(rows, arrived.shape[2])
    x, slot_col = message[:, :TAG_SLOT], message[:, TAG_SLOT : TAG_SLOT + 1]
    slot_row = jnp.sum(jnp.where(iota((rows, rows), 0) == iota((rows, rows), 1), slot_col, 0.0), axis=0, keepdims=True)
    put = (iota((elements, rows), 0).astype(jnp.float32) + 1.0 == slot_row).astype(jnp.bfloat16)
    high, low = halves(x)
    out[...] = dot(put, high) + dot(put, low)


def fetched(kernel, n_far, n_pass, n_near, n_out, *refs):
    far, near, outs = refs[:n_far], refs[n_far : n_far + n_near], refs[n_far + n_near : n_far + n_near + n_out]
    rest = refs[n_far + n_near + n_out :]
    n_held = n_far - n_pass
    held, sems, scratch = rest[:n_held], rest[n_held], rest[n_held + 1 :]
    held = (*held, *outs[n_out - n_pass :])
    copies = [pltpu.make_async_copy(src, dst, sems.at[i]) for i, (src, dst) in enumerate(zip(far, held))]
    for copy in copies:
        copy.start()

    def get(i):
        copies[i].wait()
        return held[i][...]

    kernel(get, *near, *outs[: n_out - n_pass], *scratch)
    for copy in copies[n_held:]:
        copy.wait()


def like(a):
    return jax.ShapeDtypeStruct(a.shape, a.dtype)


def call(kernel, outs, far, near=(), scratch=(), hand_on=(), flops=0):
    outs = [*outs, *[like(a) for a in hand_on]]
    out_specs = [pl.BlockSpec(memory_space=getattr(a, "memory_space", None) or pltpu.VMEM) for a in outs]
    sizes = [np.prod(a.shape) * a.dtype.itemsize for a in (*far, *near, *outs)]
    held = [pltpu.VMEM(a.shape, a.dtype) for a in far]
    far = (*far, *hand_on)
    in_specs = [pl.BlockSpec(memory_space=pltpu.HBM)] * len(far) + [pl.BlockSpec(memory_space=pltpu.VMEM)] * len(near)
    return pl.pallas_call(
        functools.partial(fetched, kernel, len(far), len(hand_on), len(near), len(outs)),
        in_specs=in_specs,
        out_specs=out_specs,
        out_shape=outs,
        scratch_shapes=[*held, pltpu.SemaphoreType.DMA((max(1, len(far)),)), *scratch],
        compiler_params=pltpu.CompilerParams(vmem_limit_bytes=48 * 1024 * 1024),
        cost_estimate=pl.CostEstimate(flops=flops, bytes_accessed=int(sum(sizes)), transcendentals=0),
    )(*[pltpu.with_memory_space_constraint(a, pltpu.HBM) for a in far], *near)


def exchange(block):
    return lax.all_to_all(block, ("gy", "gx"), split_axis=0, concat_axis=0, tiled=True)


def from_behind(block, axis, distance):
    devices = range(lax.axis_size(axis))
    route = [((i - distance) % len(devices), i) for i in devices]
    return lax.ppermute(block, axis, route)


def body(
    adjoint,
    order,
    mortar_trace,
    mortar_sub,
    mortar_dest,
    mortar_elem,
    mortar_face,
    conf_trace,
    conf_elem,
    conf_face,
    coarse_row,
):
    elements = adjoint.shape[0]
    count = mortar_trace.shape[0]
    confs = conf_trace.shape[0]
    peers = lax.axis_size("gx") * lax.axis_size("gy")
    cap = max(2, 2 * count // peers)
    row_cap = max(2, elements // peers)
    slots = peers * row_cap
    groups = -(-cap // row_cap)
    lanes = groups * STEP
    lift, conf_lift, cell, face = [tuple(jnp.asarray(t) for t in pair) for pair in basis_tables()]
    f32 = jnp.float32
    line = lambda a: a.reshape(1, -1)
    order, coarse_row = line(order), line(coarse_row)
    message = (peers, row_cap, lanes)
    outgoing, conf = call(
        functools.partial(pack_kernel, peers, cap, row_cap, elements),
        [pltpu.HBM(message, f32), jax.ShapeDtypeStruct((confs, STEP), f32)],
        (
            line(mortar_dest),
            line(mortar_sub),
            mortar_trace,
            *lift,
            line(mortar_elem),
            line(mortar_face),
            line(conf_face),
            line(conf_elem),
            conf_trace,
            *conf_lift,
        ),
        scratch=[pltpu.VMEM(message, f32), pltpu.SemaphoreType.DMA((2,))],
    )
    incoming = exchange(outgoing)
    conf = from_behind(conf, "gz", 1)
    y, cols, *face = call(
        functools.partial(cell_kernel, peers, row_cap),
        [jax.ShapeDtypeStruct((VARS * slots, ROW), f32), jax.ShapeDtypeStruct((slots, 128), f32)],
        (order, coarse_row, adjoint, *cell),
        scratch=[pltpu.VMEM((2, VARS * slots, CELL_PAD), f32)],
        hand_on=face,
    )
    (rows,) = call(
        functools.partial(face_kernel, peers, row_cap, elements, groups),
        [jax.ShapeDtypeStruct((peers, row_cap, ROWS_PAD), f32)],
        (),
        (incoming, conf, y, cols, *face),
        scratch=[pltpu.VMEM((VARS * slots, FACES_PAD), f32)],
    )
    (out,) = call(
        functools.partial(place_kernel, peers, row_cap),
        [jax.ShapeDtypeStruct((elements, VARS * ROW), f32)],
        (),
        (exchange(rows),),
    )
    return out


def solution(mesh):
    rows = P(("gx", "gy", "gz"))
    wide = P(("gx", "gy", "gz"), None)
    return jax.shard_map(
        body,
        mesh=mesh,
        in_specs=(wide, rows, wide, rows, wide, rows, rows, wide, rows, rows, rows),
        out_specs=wide,
        check_vma=False,
    )
```

```python
import functools

import jax
import jax.numpy as jnp
import ml_dtypes
import numpy as np
from jax import lax
from jax.experimental import pallas as pl
from jax.experimental.pallas import tpu as pltpu
from jax.sharding import PartitionSpec as P

VARS = 5
NODE = 7
FACE = NODE * NODE
CELL = NODE * FACE
ROW = 216
FACES = 6
ORDERS = (2, 3, 4, 5, 6)
TRACE = VARS * FACE
TRACE_PAD = 256
FLAT = 36
SENT = VARS * FLAT
STEP = 192
TAG_FACE = SENT
ROWS_PAD = 1152
TAG_SLOT = VARS * ROW
CELL_PAD = 384
FACE_PAD = 40
FACES_PAD = 256


def grid_nodes(degree):
    return -np.cos(np.pi * np.arange(degree + 1) / degree)


def lagrange_rows(degree, points):
    anchors = grid_nodes(degree)
    values = np.ones((len(points), degree + 1))
    for k in range(degree + 1):
        for other in range(degree + 1):
            if other != k:
                values[:, k] *= (points - anchors[other]) / (anchors[k] - anchors[other])
    return values


def split_table(table):
    table = np.asarray(table, np.float32)
    high = table.astype(ml_dtypes.bfloat16)
    low = (table - high.astype(np.float32)).astype(ml_dtypes.bfloat16)
    return high, low


@functools.lru_cache(maxsize=None)
def basis_tables():
    top_nodes = grid_nodes(6)
    mortar = [lagrange_rows(6, (top_nodes - 1.0) / 2.0), lagrange_rows(6, (top_nodes + 1.0) / 2.0)]
    flat = lagrange_rows(5, top_nodes)
    lift = np.zeros((5, TRACE_PAD, STEP))
    for sub in range(5):
        both = (mortar[sub // 2] @ flat, mortar[sub % 2] @ flat) if sub < 4 else (flat, flat)
        for v in range(VARS):
            lift[sub, v * FACE : (v + 1) * FACE, v * FLAT : (v + 1) * FLAT] = np.kron(*both)
    cell = np.zeros((len(ORDERS), CELL_PAD, ROW))
    face = np.zeros((len(ORDERS), FACES_PAD, ROW))
    for index, p in enumerate(ORDERS):
        shrink = np.zeros((6, NODE))
        shrink[:p, : p + 1] = lagrange_rows(p - 1, grid_nodes(p)).T
        cell[index, :CELL] = np.einsum("ai,bj,ck->ijkabc", shrink, shrink, shrink).reshape(CELL, ROW)
        lower = np.zeros((6, 6))
        lower[:p] = lagrange_rows(p - 1, grid_nodes(5)).T
        low, high = shrink[:, 0], shrink[:, p]
        for axis, spec in enumerate(("c,ai,bj->ijcab", "c,ai,bj->ijacb", "c,ai,bj->ijabc")):
            for side, edge in enumerate((low, high)):
                first = (2 * axis + side) * FACE_PAD
                face[index, first : first + FLAT] = np.einsum(spec, edge, lower, lower).reshape(FLAT, ROW)
    return (
        split_table(lift[:2].reshape(-1, STEP)) + split_table(lift[2:4].reshape(-1, STEP)),
        split_table(lift[4]),
        split_table(cell.reshape(-1, ROW)),
        split_table(face.reshape(-1, ROW)),
    )


def iota(shape, axis):
    return lax.broadcasted_iota(jnp.int32, shape, axis)


def halves(x):
    high = x.astype(jnp.bfloat16)
    low = (x - high.astype(jnp.float32)).astype(jnp.bfloat16)
    return high, low


def dot(a, b):
    return jnp.dot(a, b, preferred_element_type=jnp.float32)


def dot3(high, low, table_high, table_low):
    return dot(high, table_high) + dot(low, table_high) + dot(high, table_low)


def earlier(member):
    count = member.shape[1]
    before = (iota((count, count), 0) < iota((count, count), 1)).astype(jnp.float32)
    return dot(member.astype(jnp.bfloat16), before.astype(jnp.bfloat16))


def ranked(rank, size_y, where):
    x, y = rank // size_y, rank % size_y
    return x * size_y + where(x % 2 == 0, y, size_y - 1 - y)


def device_of(shape):
    return ranked(iota(shape, 0), lax.axis_size("gy"), jnp.where)


def owner_of(crow, peers, elements):
    first = device_of((peers, crow.shape[1])) * elements
    return ((crow >= first) & (crow < first + elements)).astype(jnp.float32)


def row_places(crow, peers, elements, stride):
    member = owner_of(crow, peers, elements)
    rank = earlier(member)
    block = iota(member.shape, 0).astype(jnp.float32)
    place = jnp.sum(member * (block * stride + rank), axis=0, keepdims=True)
    owned = (device_of(member.shape) * elements).astype(jnp.float32)
    slot = crow.astype(jnp.float32) - jnp.sum(member * owned, axis=0, keepdims=True)
    return place, slot


def onehot_rows(place, rows):
    return (iota((rows, place.shape[1]), 0).astype(jnp.float32) == place).astype(jnp.float32)


def column(onehot, values):
    return jnp.sum(onehot * values, axis=1, keepdims=True)


def pad_lanes(x, lanes):
    return jnp.concatenate([x, jnp.zeros((x.shape[0], lanes - x.shape[1]), x.dtype)], axis=1)


def pack_kernel(peers, cap, row_cap, elements, get, out, conf_out, message, sent):
    dest, sub = get(0), get(1)
    count = dest.shape[1]
    groups, slots = -(-cap // row_cap), peers * row_cap
    member = (device_of((peers, count)) == dest).astype(jnp.float32)
    block = jnp.sum(member * iota(member.shape, 0).astype(jnp.float32), axis=0, keepdims=True)
    rank = jnp.sum(member * earlier(member), axis=0, keepdims=True)
    group = sum([(rank >= float(g * row_cap)).astype(jnp.float32) for g in range(1, groups)], jnp.zeros_like(rank))
    place = group * float(slots - row_cap) + block * float(row_cap) + rank
    put = onehot_rows(place, groups * slots)
    eye = (iota((count, count), 0) == iota((count, count), 1)).astype(jnp.float32)
    sub_col = column(eye, sub.astype(jnp.float32))
    high, low = halves(pad_lanes(get(2), TRACE_PAD))
    masks = [(sub_col == float(s)).astype(jnp.bfloat16) for s in range(4)]
    lifted = jnp.zeros((count, STEP), jnp.float32)
    for first in (0, 2):
        wide = [jnp.concatenate([half * mask for mask in masks[first : first + 2]], axis=1) for half in (high, low)]
        lifted = lifted + dot3(*wide, get(3 + first), get(4 + first))
    lifted_high, lifted_low = halves(lifted)
    code_col = column(put, (get(8) * elements + get(7) + 1).astype(jnp.float32))
    put = put.astype(jnp.bfloat16)
    packed = dot(put, lifted_high) + dot(put, lifted_low)
    packed = jnp.where(iota(packed.shape, 1) == TAG_FACE, code_col, packed)
    bounds = (0, groups // 2 // 2 * 2, groups)
    sends = []
    for half, (first, last) in enumerate(zip(bounds[:-1], bounds[1:])):
        if first == last:
            continue
        for g in range(first, last):
            message[:, :, g * STEP : (g + 1) * STEP] = packed[g * slots : (g + 1) * slots].reshape(peers, row_cap, STEP)
        lanes = pl.ds(first * STEP, (last - first) * STEP)
        send = pltpu.make_async_copy(message.at[:, :, lanes], out.at[:, :, lanes], sent.at[half])
        send.start()
        sends.append(send)
    cface, celem = get(9), get(10)
    confs = cface.shape[1]
    eye = (iota((confs, confs), 0) == iota((confs, confs), 1)).astype(jnp.float32)
    conf_col = column(eye, (cface * elements + celem + 1).astype(jnp.float32))
    conf = dot3(*halves(pad_lanes(get(11), TRACE_PAD)), get(12), get(13))
    conf_out[...] = jnp.where(iota(conf.shape, 1) == TAG_FACE, conf_col, conf)
    for send in sends:
        send.wait()


def cell_kernel(peers, row_cap, get, y_out, col_out, spread):
    order, crow = get(0), get(1)
    elements = order.shape[1]
    slots = peers * row_cap
    place, slot = row_places(crow, peers, elements, row_cap)
    take = onehot_rows(place, slots)
    order_col = column(take, order.astype(jnp.float32))
    elem_col = column(take, iota((1, elements), 1).astype(jnp.float32) + 1.0)
    lane = iota((slots, 128), 1)
    slot_col = column(take, slot + 1.0)
    col_out[...] = jnp.where(lane == 0, order_col, jnp.where(lane == 1, elem_col, slot_col))
    take = take.astype(jnp.bfloat16)
    spread[...] = jnp.zeros_like(spread)
    for half, part in enumerate(halves(get(2))):
        moved = dot(take, part)
        for v in range(VARS):
            spread[half, v * slots : (v + 1) * slots, :CELL] = moved[:, v * CELL : (v + 1) * CELL]
    order_rows = jnp.concatenate([order_col] * VARS, axis=0)
    high, low = spread[0], spread[1]
    wide_high = jnp.concatenate([jnp.where(order_rows == float(p), high, 0.0).astype(jnp.bfloat16) for p in ORDERS], axis=1)
    wide_low = jnp.concatenate([jnp.where(order_rows == float(p), low, 0.0).astype(jnp.bfloat16) for p in ORDERS], axis=1)
    y_out[...] = dot3(wide_high, wide_low, get(3), get(4))


def face_kernel(peers, row_cap, elements, groups, get, incoming, conf, y, cols, table_high, table_low, out, spread):
    slots = peers * row_cap
    message = incoming[...].reshape(slots, incoming.shape[2])
    x = jnp.concatenate([*[message[:, g * STEP : (g + 1) * STEP] for g in range(groups)], conf[...]], axis=0)
    code_col = x[:, TAG_FACE : TAG_FACE + 1]
    count = x.shape[0]
    code_row = jnp.sum(jnp.where(iota((count, count), 0) == iota((count, count), 1), code_col, 0.0), axis=0, keepdims=True)
    order_col, elem_col = cols[:, 0:1], cols[:, 1:2]
    wanted = jnp.concatenate([jnp.where(elem_col > 0.0, elem_col + float(f * elements), -1.0) for f in range(FACES)], axis=0)
    gather = (wanted == code_row).astype(jnp.bfloat16)
    high, low = halves(x)
    face_sum = dot(gather, high) + dot(gather, low)
    spread[...] = jnp.zeros_like(spread)
    for f in range(FACES):
        for v in range(VARS):
            spread[v * slots : (v + 1) * slots, f * FACE_PAD : f * FACE_PAD + FLAT] = face_sum[
                f * slots : (f + 1) * slots, v * FLAT : (v + 1) * FLAT
            ]
    order_rows = jnp.concatenate([order_col] * VARS, axis=0)
    z = spread[...]
    wide = jnp.concatenate([jnp.where(order_rows == float(p), z, 0.0) for p in ORDERS], axis=1)
    high, low = halves(wide)
    total = y[...] + dot3(high, low, table_high[...], table_low[...])
    for v in range(VARS):
        out[:, :, v * ROW : (v + 1) * ROW] = total[v * slots : (v + 1) * slots].reshape(peers, row_cap, ROW)
    out[:, :, TAG_SLOT : TAG_SLOT + 1] = cols[:, 2:3].reshape(peers, row_cap, 1)


def place_kernel(peers, row_cap, get, arrived, out):
    elements = out.shape[0]
    rows = peers * row_cap
    message = arrived[...].reshape(rows, arrived.shape[2])
    x, slot_col = message[:, :TAG_SLOT], message[:, TAG_SLOT : TAG_SLOT + 1]
    slot_row = jnp.sum(jnp.where(iota((rows, rows), 0) == iota((rows, rows), 1), slot_col, 0.0), axis=0, keepdims=True)
    put = (iota((elements, rows), 0).astype(jnp.float32) + 1.0 == slot_row).astype(jnp.bfloat16)
    high, low = halves(x)
    out[...] = dot(put, high) + dot(put, low)


def fetched(kernel, n_far, n_pass, n_near, n_out, *refs):
    far, near, outs = refs[:n_far], refs[n_far : n_far + n_near], refs[n_far + n_near : n_far + n_near + n_out]
    rest = refs[n_far + n_near + n_out :]
    n_held = n_far - n_pass
    held, sems, scratch = rest[:n_held], rest[n_held], rest[n_held + 1 :]
    held = (*held, *outs[n_out - n_pass :])
    copies = [pltpu.make_async_copy(src, dst, sems.at[i]) for i, (src, dst) in enumerate(zip(far, held))]
    for copy in copies:
        copy.start()

    def get(i):
        copies[i].wait()
        return held[i][...]

    kernel(get, *near, *outs[: n_out - n_pass], *scratch)
    for copy in copies[n_held:]:
        copy.wait()


def like(a):
    return jax.ShapeDtypeStruct(a.shape, a.dtype)


def call(kernel, outs, far, near=(), scratch=(), hand_on=(), flops=0):
    outs = [*outs, *[like(a) for a in hand_on]]
    out_specs = [pl.BlockSpec(memory_space=getattr(a, "memory_space", None) or pltpu.VMEM) for a in outs]
    sizes = [np.prod(a.shape) * a.dtype.itemsize for a in (*far, *near, *outs)]
    held = [pltpu.VMEM(a.shape, a.dtype) for a in far]
    far = (*far, *hand_on)
    in_specs = [pl.BlockSpec(memory_space=pltpu.HBM)] * len(far) + [pl.BlockSpec(memory_space=pltpu.VMEM)] * len(near)
    return pl.pallas_call(
        functools.partial(fetched, kernel, len(far), len(hand_on), len(near), len(outs)),
        in_specs=in_specs,
        out_specs=out_specs,
        out_shape=outs,
        scratch_shapes=[*held, pltpu.SemaphoreType.DMA((max(1, len(far)),)), *scratch],
        compiler_params=pltpu.CompilerParams(vmem_limit_bytes=48 * 1024 * 1024),
        cost_estimate=pl.CostEstimate(flops=flops, bytes_accessed=int(sum(sizes)), transcendentals=0),
    )(*[pltpu.with_memory_space_constraint(a, pltpu.HBM) for a in far], *near)


def exchange(block):
    order = ranked(np.arange(block.shape[0]), lax.axis_size("gy"), np.where).tolist()
    return lax.all_to_all(block, ("gx", "gy"), split_axis=0, concat_axis=0, tiled=True, axis_index_groups=[order])


def from_behind(block, axis, distance):
    devices = range(lax.axis_size(axis))
    route = [((i - distance) % len(devices), i) for i in devices]
    return lax.ppermute(block, axis, route)


def body(
    adjoint,
    order,
    mortar_trace,
    mortar_sub,
    mortar_dest,
    mortar_elem,
    mortar_face,
    conf_trace,
    conf_elem,
    conf_face,
    coarse_row,
):
    elements = adjoint.shape[0]
    count = mortar_trace.shape[0]
    confs = conf_trace.shape[0]
    peers = lax.axis_size("gx") * lax.axis_size("gy")
    cap = max(2, 2 * count // peers)
    row_cap = max(2, elements // peers)
    slots = peers * row_cap
    groups = -(-cap // row_cap)
    lanes = groups * STEP
    lift, conf_lift, cell, face = [tuple(jnp.asarray(t) for t in pair) for pair in basis_tables()]
    f32 = jnp.float32
    line = lambda a: a.reshape(1, -1)
    order, coarse_row = line(order), line(coarse_row)
    message = (peers, row_cap, lanes)
    outgoing, conf = call(
        functools.partial(pack_kernel, peers, cap, row_cap, elements),
        [pltpu.HBM(message, f32), jax.ShapeDtypeStruct((confs, STEP), f32)],
        (
            line(mortar_dest),
            line(mortar_sub),
            mortar_trace,
            *lift,
            line(mortar_elem),
            line(mortar_face),
            line(conf_face),
            line(conf_elem),
            conf_trace,
            *conf_lift,
        ),
        scratch=[pltpu.VMEM(message, f32), pltpu.SemaphoreType.DMA((2,))],
    )
    incoming = exchange(outgoing)
    conf = from_behind(conf, "gz", 1)
    y, cols, *face = call(
        functools.partial(cell_kernel, peers, row_cap),
        [jax.ShapeDtypeStruct((VARS * slots, ROW), f32), jax.ShapeDtypeStruct((slots, 128), f32)],
        (order, coarse_row, adjoint, *cell),
        scratch=[pltpu.VMEM((2, VARS * slots, CELL_PAD), f32)],
        hand_on=face,
    )
    (rows,) = call(
        functools.partial(face_kernel, peers, row_cap, elements, groups),
        [jax.ShapeDtypeStruct((peers, row_cap, ROWS_PAD), f32)],
        (),
        (incoming, conf, y, cols, *face),
        scratch=[pltpu.VMEM((VARS * slots, FACES_PAD), f32)],
    )
    (out,) = call(
        functools.partial(place_kernel, peers, row_cap),
        [jax.ShapeDtypeStruct((elements, VARS * ROW), f32)],
        (),
        (exchange(rows),),
    )
    return out


def solution(mesh):
    rows = P(("gx", "gy", "gz"))
    wide = P(("gx", "gy", "gz"), None)
    return jax.shard_map(
        body,
        mesh=mesh,
        in_specs=(wide, rows, wide, rows, wide, rows, rows, wide, rows, rows, rows),
        out_specs=wide,
        check_vma=False,
    )
```

```python
import functools

import jax
import jax.numpy as jnp
import ml_dtypes
import numpy as np
from jax import lax
from jax.experimental import pallas as pl
from jax.experimental.pallas import tpu as pltpu
from jax.sharding import PartitionSpec as P

VARS = 5
NODE = 7
FACE = NODE * NODE
CELL = NODE * FACE
ROW = 216
FACES = 6
ORDERS = (2, 3, 4, 5, 6)
TRACE = VARS * FACE
SUB_STEP = 64
FLAT = 36
SENT = VARS * FLAT
STEP = 192
TAG_FACE = SENT
ROWS_PAD = 1152
TAG_SLOT = VARS * ROW
CELL_PAD = 384
FACE_PAD = 40
FACES_PAD = 256


def grid_nodes(degree):
    return -np.cos(np.pi * np.arange(degree + 1) / degree)


def lagrange_rows(degree, points):
    anchors = grid_nodes(degree)
    values = np.ones((len(points), degree + 1))
    for k in range(degree + 1):
        for other in range(degree + 1):
            if other != k:
                values[:, k] *= (points - anchors[other]) / (anchors[k] - anchors[other])
    return values


def split_table(table):
    table = np.asarray(table, np.float32)
    high = table.astype(ml_dtypes.bfloat16)
    low = (table - high.astype(np.float32)).astype(ml_dtypes.bfloat16)
    return high, low


@functools.lru_cache(maxsize=None)
def basis_tables():
    top_nodes = grid_nodes(6)
    mortar = [lagrange_rows(6, (top_nodes - 1.0) / 2.0), lagrange_rows(6, (top_nodes + 1.0) / 2.0)]
    flat = lagrange_rows(5, top_nodes)
    lift = np.zeros((SUB_STEP, 6 * SUB_STEP))
    for sub in range(5):
        both = (mortar[sub // 2] @ flat, mortar[sub % 2] @ flat) if sub < 4 else (flat, flat)
        lift[:FACE, sub * SUB_STEP : sub * SUB_STEP + FLAT] = np.kron(*both)
    cell = np.zeros((len(ORDERS), CELL_PAD, ROW))
    face = np.zeros((len(ORDERS), FACES_PAD, ROW))
    for index, p in enumerate(ORDERS):
        shrink = np.zeros((6, NODE))
        shrink[:p, : p + 1] = lagrange_rows(p - 1, grid_nodes(p)).T
        cell[index, :CELL] = np.einsum("ai,bj,ck->ijkabc", shrink, shrink, shrink).reshape(CELL, ROW)
        lower = np.zeros((6, 6))
        lower[:p] = lagrange_rows(p - 1, grid_nodes(5)).T
        low, high = shrink[:, 0], shrink[:, p]
        for axis, spec in enumerate(("c,ai,bj->ijcab", "c,ai,bj->ijacb", "c,ai,bj->ijabc")):
            for side, edge in enumerate((low, high)):
                first = (2 * axis + side) * FACE_PAD
                face[index, first : first + FLAT] = np.einsum(spec, edge, lower, lower).reshape(FLAT, ROW)
    return (
        np.concatenate(split_table(lift)),
        split_table(cell.reshape(-1, ROW)),
        split_table(face.reshape(-1, ROW)),
    )


def iota(shape, axis):
    return lax.broadcasted_iota(jnp.int32, shape, axis)


def halves(x):
    high = x.astype(jnp.bfloat16)
    low = (x - high.astype(jnp.float32)).astype(jnp.bfloat16)
    return high, low


def dot(a, b):
    return jnp.dot(a, b, preferred_element_type=jnp.float32)


def dot3(high, low, table_high, table_low):
    return dot(high, table_high) + dot(low, table_high) + dot(high, table_low)


def earlier(member):
    count = member.shape[1]
    before = (iota((count, count), 0) < iota((count, count), 1)).astype(jnp.float32)
    return dot(member.astype(jnp.bfloat16), before.astype(jnp.bfloat16))


def device_of(shape):
    size_x, size_y = lax.axis_size("gx"), lax.axis_size("gy")
    rank = iota(shape, 0)
    return rank % size_x * size_y + rank // size_x


def owner_of(crow, peers, elements):
    first = device_of((peers, crow.shape[1])) * elements
    return ((crow >= first) & (crow < first + elements)).astype(jnp.float32)


def row_places(crow, peers, elements, stride):
    member = owner_of(crow, peers, elements)
    rank = earlier(member)
    block = iota(member.shape, 0).astype(jnp.float32)
    place = jnp.sum(member * (block * stride + rank), axis=0, keepdims=True)
    owned = (device_of(member.shape) * elements).astype(jnp.float32)
    slot = crow.astype(jnp.float32) - jnp.sum(member * owned, axis=0, keepdims=True)
    return place, slot


def onehot_rows(place, rows):
    return (iota((rows, place.shape[1]), 0).astype(jnp.float32) == place).astype(jnp.float32)


def column(onehot, values):
    return jnp.sum(onehot * values, axis=1, keepdims=True)


def pad_lanes(x, lanes):
    return jnp.concatenate([x, jnp.zeros((x.shape[0], lanes - x.shape[1]), x.dtype)], axis=1)


def stacked(trace):
    wide = pad_lanes(trace, TRACE - FACE + SUB_STEP)
    return jnp.concatenate([wide[:, v * FACE : v * FACE + SUB_STEP] for v in range(VARS)], axis=0)


def side_by_side(products):
    count = products.shape[0] // VARS
    parts = [products[v * count : (v + 1) * count, :FLAT] for v in range(VARS)]
    return jnp.concatenate([*parts, jnp.zeros((count, STEP - SENT), jnp.float32)], axis=1)


def pack_kernel(peers, cap, row_cap, elements, get, out, conf_out, message, sent):
    dest, sub = get(0), get(1)
    count = dest.shape[1]
    groups, slots = -(-cap // row_cap), peers * row_cap
    member = (device_of((peers, count)) == dest).astype(jnp.float32)
    block = jnp.sum(member * iota(member.shape, 0).astype(jnp.float32), axis=0, keepdims=True)
    rank = jnp.sum(member * earlier(member), axis=0, keepdims=True)
    group = sum([(rank >= float(g * row_cap)).astype(jnp.float32) for g in range(1, groups)], jnp.zeros_like(rank))
    place = group * float(slots - row_cap) + block * float(row_cap) + rank
    put = onehot_rows(place, groups * slots)
    eye = (iota((count, count), 0) == iota((count, count), 1)).astype(jnp.float32)
    sub_col = column(eye, sub.astype(jnp.float32))
    subs = jnp.concatenate([sub_col] * VARS, axis=0)
    tables = get(3)
    table_high, table_low = tables[:SUB_STEP], tables[SUB_STEP:]
    split = 4 * SUB_STEP
    lifts = dot3(*halves(stacked(get(2))), table_high[:, :split], table_low[:, :split])
    lifts = jnp.where(subs < 2.0, lifts[:, : 2 * SUB_STEP], lifts[:, 2 * SUB_STEP :])
    odd = (subs == 1.0) | (subs == 3.0)
    lifted = side_by_side(jnp.where(odd, lifts[:, SUB_STEP:], lifts[:, :SUB_STEP]))
    lifted_high, lifted_low = halves(lifted)
    code_col = column(put, (get(5) * elements + get(4) + 1).astype(jnp.float32))
    put = put.astype(jnp.bfloat16)
    packed = dot(put, lifted_high) + dot(put, lifted_low)
    packed = jnp.where(iota(packed.shape, 1) == TAG_FACE, code_col, packed)
    bounds = (0, groups // 2 // 2 * 2, groups)
    sends = []
    for half, (first, last) in enumerate(zip(bounds[:-1], bounds[1:])):
        if first == last:
            continue
        for g in range(first, last):
            message[:, :, g * STEP : (g + 1) * STEP] = packed[g * slots : (g + 1) * slots].reshape(peers, row_cap, STEP)
        lanes = pl.ds(first * STEP, (last - first) * STEP)
        send = pltpu.make_async_copy(message.at[:, :, lanes], out.at[:, :, lanes], sent.at[half])
        send.start()
        sends.append(send)
    cface, celem = get(6), get(7)
    confs = cface.shape[1]
    eye = (iota((confs, confs), 0) == iota((confs, confs), 1)).astype(jnp.float32)
    conf_col = column(eye, (cface * elements + celem + 1).astype(jnp.float32))
    conf = side_by_side(dot3(*halves(stacked(get(8))), table_high[:, split:], table_low[:, split:]))
    conf_out[...] = jnp.where(iota(conf.shape, 1) == TAG_FACE, conf_col, conf)
    for send in sends:
        send.wait()


def cell_kernel(peers, row_cap, get, y_out, col_out, spread):
    order, crow = get(0), get(1)
    elements = order.shape[1]
    slots = peers * row_cap
    place, slot = row_places(crow, peers, elements, row_cap)
    take = onehot_rows(place, slots)
    order_col = column(take, order.astype(jnp.float32))
    elem_col = column(take, iota((1, elements), 1).astype(jnp.float32) + 1.0)
    lane = iota((slots, 128), 1)
    slot_col = column(take, slot + 1.0)
    col_out[...] = jnp.where(lane == 0, order_col, jnp.where(lane == 1, elem_col, slot_col))
    take = take.astype(jnp.bfloat16)
    spread[...] = jnp.zeros_like(spread)
    for half, part in enumerate(halves(get(2))):
        moved = dot(take, part)
        for v in range(VARS):
            spread[half, v * slots : (v + 1) * slots, :CELL] = moved[:, v * CELL : (v + 1) * CELL]
    order_rows = jnp.concatenate([order_col] * VARS, axis=0)
    high, low = spread[0], spread[1]
    wide_high = jnp.concatenate([jnp.where(order_rows == float(p), high, 0.0).astype(jnp.bfloat16) for p in ORDERS], axis=1)
    wide_low = jnp.concatenate([jnp.where(order_rows == float(p), low, 0.0).astype(jnp.bfloat16) for p in ORDERS], axis=1)
    y_out[...] = dot3(wide_high, wide_low, get(3), get(4))


def face_kernel(peers, row_cap, elements, groups, get, incoming, conf, y, cols, table_high, table_low, out, spread):
    slots = peers * row_cap
    message = incoming[...].reshape(slots, incoming.shape[2])
    x = jnp.concatenate([*[message[:, g * STEP : (g + 1) * STEP] for g in range(groups)], conf[...]], axis=0)
    code_col = x[:, TAG_FACE : TAG_FACE + 1]
    count = x.shape[0]
    code_row = jnp.sum(jnp.where(iota((count, count), 0) == iota((count, count), 1), code_col, 0.0), axis=0, keepdims=True)
    order_col, elem_col = cols[:, 0:1], cols[:, 1:2]
    wanted = jnp.concatenate([jnp.where(elem_col > 0.0, elem_col + float(f * elements), -1.0) for f in range(FACES)], axis=0)
    gather = (wanted == code_row).astype(jnp.bfloat16)
    high, low = halves(x)
    face_sum = dot(gather, high) + dot(gather, low)
    spread[...] = jnp.zeros_like(spread)
    for f in range(FACES):
        for v in range(VARS):
            spread[v * slots : (v + 1) * slots, f * FACE_PAD : f * FACE_PAD + FLAT] = face_sum[
                f * slots : (f + 1) * slots, v * FLAT : (v + 1) * FLAT
            ]
    order_rows = jnp.concatenate([order_col] * VARS, axis=0)
    z = spread[...]
    wide = jnp.concatenate([jnp.where(order_rows == float(p), z, 0.0) for p in ORDERS], axis=1)
    high, low = halves(wide)
    total = y[...] + dot3(high, low, table_high[...], table_low[...])
    for v in range(VARS):
        out[:, :, v * ROW : (v + 1) * ROW] = total[v * slots : (v + 1) * slots].reshape(peers, row_cap, ROW)
    out[:, :, TAG_SLOT : TAG_SLOT + 1] = cols[:, 2:3].reshape(peers, row_cap, 1)


def place_kernel(peers, row_cap, get, arrived, out):
    elements = out.shape[0]
    rows = peers * row_cap
    message = arrived[...].reshape(rows, arrived.shape[2])
    x, slot_col = message[:, :TAG_SLOT], message[:, TAG_SLOT : TAG_SLOT + 1]
    slot_row = jnp.sum(jnp.where(iota((rows, rows), 0) == iota((rows, rows), 1), slot_col, 0.0), axis=0, keepdims=True)
    put = (iota((elements, rows), 0).astype(jnp.float32) + 1.0 == slot_row).astype(jnp.bfloat16)
    high, low = halves(x)
    out[...] = dot(put, high) + dot(put, low)


def fetched(kernel, n_far, n_pass, n_near, n_out, *refs):
    far, near, outs = refs[:n_far], refs[n_far : n_far + n_near], refs[n_far + n_near : n_far + n_near + n_out]
    rest = refs[n_far + n_near + n_out :]
    n_held = n_far - n_pass
    held, sems, scratch = rest[:n_held], rest[n_held], rest[n_held + 1 :]
    held = (*held, *outs[n_out - n_pass :])
    copies = [pltpu.make_async_copy(src, dst, sems.at[i]) for i, (src, dst) in enumerate(zip(far, held))]
    for copy in copies:
        copy.start()

    def get(i):
        copies[i].wait()
        return held[i][...]

    kernel(get, *near, *outs[: n_out - n_pass], *scratch)
    for copy in copies[n_held:]:
        copy.wait()


def like(a):
    return jax.ShapeDtypeStruct(a.shape, a.dtype)


def call(kernel, outs, far, near=(), scratch=(), hand_on=(), flops=0):
    outs = [*outs, *[like(a) for a in hand_on]]
    out_specs = [pl.BlockSpec(memory_space=getattr(a, "memory_space", None) or pltpu.VMEM) for a in outs]
    sizes = [np.prod(a.shape) * a.dtype.itemsize for a in (*far, *near, *outs)]
    held = [pltpu.VMEM(a.shape, a.dtype) for a in far]
    far = (*far, *hand_on)
    in_specs = [pl.BlockSpec(memory_space=pltpu.HBM)] * len(far) + [pl.BlockSpec(memory_space=pltpu.VMEM)] * len(near)
    return pl.pallas_call(
        functools.partial(fetched, kernel, len(far), len(hand_on), len(near), len(outs)),
        in_specs=in_specs,
        out_specs=out_specs,
        out_shape=outs,
        scratch_shapes=[*held, pltpu.SemaphoreType.DMA((max(1, len(far)),)), *scratch],
        compiler_params=pltpu.CompilerParams(vmem_limit_bytes=48 * 1024 * 1024),
        cost_estimate=pl.CostEstimate(flops=flops, bytes_accessed=int(sum(sizes)), transcendentals=0),
    )(*[pltpu.with_memory_space_constraint(a, pltpu.HBM) for a in far], *near)


def exchange(block):
    return lax.all_to_all(block, ("gy", "gx"), split_axis=0, concat_axis=0, tiled=True)


def from_behind(block, axis, distance):
    devices = range(lax.axis_size(axis))
    route = [((i - distance) % len(devices), i) for i in devices]
    return lax.ppermute(block, axis, route)


def body(
    adjoint,
    order,
    mortar_trace,
    mortar_sub,
    mortar_dest,
    mortar_elem,
    mortar_face,
    conf_trace,
    conf_elem,
    conf_face,
    coarse_row,
):
    elements = adjoint.shape[0]
    count = mortar_trace.shape[0]
    confs = conf_trace.shape[0]
    peers = lax.axis_size("gx") * lax.axis_size("gy")
    cap = max(2, 2 * count // peers)
    row_cap = max(2, elements // peers)
    slots = peers * row_cap
    groups = -(-cap // row_cap)
    lanes = groups * STEP
    lift, cell, face = jax.tree.map(jnp.asarray, basis_tables())
    f32 = jnp.float32
    line = lambda a: a.reshape(1, -1)
    order, coarse_row = line(order), line(coarse_row)
    message = (peers, row_cap, lanes)
    outgoing, conf = call(
        functools.partial(pack_kernel, peers, cap, row_cap, elements),
        [pltpu.HBM(message, f32), jax.ShapeDtypeStruct((confs, STEP), f32)],
        (
            line(mortar_dest),
            line(mortar_sub),
            mortar_trace,
            lift,
            line(mortar_elem),
            line(mortar_face),
            line(conf_face),
            line(conf_elem),
            conf_trace,
        ),
        scratch=[pltpu.VMEM(message, f32), pltpu.SemaphoreType.DMA((2,))],
    )
    incoming = exchange(outgoing)
    conf = from_behind(conf, "gz", 1)
    y, cols, *face = call(
        functools.partial(cell_kernel, peers, row_cap),
        [jax.ShapeDtypeStruct((VARS * slots, ROW), f32), jax.ShapeDtypeStruct((slots, 128), f32)],
        (order, coarse_row, adjoint, *cell),
        scratch=[pltpu.VMEM((2, VARS * slots, CELL_PAD), f32)],
        hand_on=face,
    )
    (rows,) = call(
        functools.partial(face_kernel, peers, row_cap, elements, groups),
        [jax.ShapeDtypeStruct((peers, row_cap, ROWS_PAD), f32)],
        (),
        (incoming, conf, y, cols, *face),
        scratch=[pltpu.VMEM((VARS * slots, FACES_PAD), f32)],
    )
    (out,) = call(
        functools.partial(place_kernel, peers, row_cap),
        [jax.ShapeDtypeStruct((elements, VARS * ROW), f32)],
        (),
        (exchange(rows),),
    )
    return out


def solution(mesh):
    rows = P(("gx", "gy", "gz"))
    wide = P(("gx", "gy", "gz"), None)
    return jax.shard_map(
        body,
        mesh=mesh,
        in_specs=(wide, rows, wide, rows, wide, rows, rows, wide, rows, rows, rows),
        out_specs=wide,
        check_vma=False,
    )
```

```python
import functools

import jax
import jax.numpy as jnp
import ml_dtypes
import numpy as np
from jax import lax
from jax.experimental import pallas as pl
from jax.experimental.pallas import tpu as pltpu
from jax.sharding import PartitionSpec as P

VARS = 5
NODE = 7
FACE = NODE * NODE
CELL = NODE * FACE
ROW = 216
FACES = 6
ORDERS = (2, 3, 4, 5, 6)
TRACE = VARS * FACE
SUB_STEP = 64
FLAT = 36
SENT = VARS * FLAT
STEP = 192
TAG_FACE = SENT
ROWS_PAD = 1152
TAG_SLOT = VARS * ROW
PLACE_SPLIT = 512
CELL_PAD = 384
FACE_PAD = 40
FACES_PAD = 256


def grid_nodes(degree):
    return -np.cos(np.pi * np.arange(degree + 1) / degree)


def lagrange_rows(degree, points):
    anchors = grid_nodes(degree)
    values = np.ones((len(points), degree + 1))
    for k in range(degree + 1):
        for other in range(degree + 1):
            if other != k:
                values[:, k] *= (points - anchors[other]) / (anchors[k] - anchors[other])
    return values


def split_table(table):
    table = np.asarray(table, np.float32)
    high = table.astype(ml_dtypes.bfloat16)
    low = (table - high.astype(np.float32)).astype(ml_dtypes.bfloat16)
    return high, low


@functools.lru_cache(maxsize=None)
def basis_tables():
    top_nodes = grid_nodes(6)
    mortar = [lagrange_rows(6, (top_nodes - 1.0) / 2.0), lagrange_rows(6, (top_nodes + 1.0) / 2.0)]
    flat = lagrange_rows(5, top_nodes)
    lift = np.zeros((SUB_STEP, 6 * SUB_STEP))
    for sub in range(5):
        both = (mortar[sub // 2] @ flat, mortar[sub % 2] @ flat) if sub < 4 else (flat, flat)
        lift[:FACE, sub * SUB_STEP : sub * SUB_STEP + FLAT] = np.kron(*both)
    cell = np.zeros((len(ORDERS), CELL_PAD, ROW))
    face = np.zeros((len(ORDERS), FACES_PAD, ROW))
    for index, p in enumerate(ORDERS):
        shrink = np.zeros((6, NODE))
        shrink[:p, : p + 1] = lagrange_rows(p - 1, grid_nodes(p)).T
        cell[index, :CELL] = np.einsum("ai,bj,ck->ijkabc", shrink, shrink, shrink).reshape(CELL, ROW)
        lower = np.zeros((6, 6))
        lower[:p] = lagrange_rows(p - 1, grid_nodes(5)).T
        low, high = shrink[:, 0], shrink[:, p]
        for axis, spec in enumerate(("c,ai,bj->ijcab", "c,ai,bj->ijacb", "c,ai,bj->ijabc")):
            for side, edge in enumerate((low, high)):
                first = (2 * axis + side) * FACE_PAD
                face[index, first : first + FLAT] = np.einsum(spec, edge, lower, lower).reshape(FLAT, ROW)
    return (
        np.concatenate(split_table(lift)),
        split_table(cell.reshape(-1, ROW)),
        split_table(face.reshape(-1, ROW)),
    )


def iota(shape, axis):
    return lax.broadcasted_iota(jnp.int32, shape, axis)


def halves(x):
    high = x.astype(jnp.bfloat16)
    low = (x - high.astype(jnp.float32)).astype(jnp.bfloat16)
    return high, low


def dot(a, b):
    return jnp.dot(a, b, preferred_element_type=jnp.float32)


def dot3(high, low, table_high, table_low):
    return dot(high, table_high) + dot(low, table_high) + dot(high, table_low)


def earlier(member):
    count = member.shape[1]
    before = (iota((count, count), 0) < iota((count, count), 1)).astype(jnp.float32)
    return dot(member.astype(jnp.bfloat16), before.astype(jnp.bfloat16))


def device_of(shape):
    size_x, size_y = lax.axis_size("gx"), lax.axis_size("gy")
    rank = iota(shape, 0)
    return rank % size_x * size_y + rank // size_x


def owner_of(crow, peers, elements):
    first = device_of((peers, crow.shape[1])) * elements
    return ((crow >= first) & (crow < first + elements)).astype(jnp.float32)


def row_places(crow, peers, elements, stride):
    member = owner_of(crow, peers, elements)
    rank = earlier(member)
    block = iota(member.shape, 0).astype(jnp.float32)
    place = jnp.sum(member * (block * stride + rank), axis=0, keepdims=True)
    owned = (device_of(member.shape) * elements).astype(jnp.float32)
    slot = crow.astype(jnp.float32) - jnp.sum(member * owned, axis=0, keepdims=True)
    return place, slot


def onehot_rows(place, rows):
    return (iota((rows, place.shape[1]), 0).astype(jnp.float32) == place).astype(jnp.float32)


def column(onehot, values):
    return jnp.sum(onehot * values, axis=1, keepdims=True)


def pad_lanes(x, lanes):
    return jnp.concatenate([x, jnp.zeros((x.shape[0], lanes - x.shape[1]), x.dtype)], axis=1)


def stacked(trace):
    wide = pad_lanes(trace, TRACE - FACE + SUB_STEP)
    return jnp.concatenate([wide[:, v * FACE : v * FACE + SUB_STEP] for v in range(VARS)], axis=0)


def side_by_side(products):
    count = products.shape[0] // VARS
    parts = [products[v * count : (v + 1) * count, :FLAT] for v in range(VARS)]
    return jnp.concatenate([*parts, jnp.zeros((count, STEP - SENT), jnp.float32)], axis=1)


def pack_kernel(peers, cap, row_cap, elements, get, out, conf_out, message, sent):
    dest, sub = get(0), get(1)
    count = dest.shape[1]
    groups, slots = -(-cap // row_cap), peers * row_cap
    member = (device_of((peers, count)) == dest).astype(jnp.float32)
    block = jnp.sum(member * iota(member.shape, 0).astype(jnp.float32), axis=0, keepdims=True)
    rank = jnp.sum(member * earlier(member), axis=0, keepdims=True)
    group = sum([(rank >= float(g * row_cap)).astype(jnp.float32) for g in range(1, groups)], jnp.zeros_like(rank))
    place = group * float(slots - row_cap) + block * float(row_cap) + rank
    put = onehot_rows(place, groups * slots)
    eye = (iota((count, count), 0) == iota((count, count), 1)).astype(jnp.float32)
    sub_col = column(eye, sub.astype(jnp.float32))
    subs = jnp.concatenate([sub_col] * VARS, axis=0)
    tables = get(3)
    table_high, table_low = tables[:SUB_STEP], tables[SUB_STEP:]
    split = 4 * SUB_STEP
    lifts = dot3(*halves(stacked(get(2))), table_high[:, :split], table_low[:, :split])
    lifts = jnp.where(subs < 2.0, lifts[:, : 2 * SUB_STEP], lifts[:, 2 * SUB_STEP :])
    odd = (subs == 1.0) | (subs == 3.0)
    lifted = side_by_side(jnp.where(odd, lifts[:, SUB_STEP:], lifts[:, :SUB_STEP]))
    lifted_high, lifted_low = halves(lifted)
    code_col = column(put, (get(5) * elements + get(4) + 1).astype(jnp.float32))
    put = put.astype(jnp.bfloat16)
    packed = dot(put, lifted_high) + dot(put, lifted_low)
    packed = jnp.where(iota(packed.shape, 1) == TAG_FACE, code_col, packed)
    bounds = (0, groups // 2 // 2 * 2, groups)
    sends = []
    for half, (first, last) in enumerate(zip(bounds[:-1], bounds[1:])):
        if first == last:
            continue
        for g in range(first, last):
            message[:, :, g * STEP : (g + 1) * STEP] = packed[g * slots : (g + 1) * slots].reshape(peers, row_cap, STEP)
        lanes = pl.ds(first * STEP, (last - first) * STEP)
        send = pltpu.make_async_copy(message.at[:, :, lanes], out.at[:, :, lanes], sent.at[half])
        send.start()
        sends.append(send)
    cface, celem = get(6), get(7)
    confs = cface.shape[1]
    eye = (iota((confs, confs), 0) == iota((confs, confs), 1)).astype(jnp.float32)
    conf_col = column(eye, (cface * elements + celem + 1).astype(jnp.float32))
    conf = side_by_side(dot3(*halves(stacked(get(8))), table_high[:, split:], table_low[:, split:]))
    conf_out[...] = jnp.where(iota(conf.shape, 1) == TAG_FACE, conf_col, conf)
    for send in sends:
        send.wait()


def cell_kernel(peers, row_cap, get, conf, y_out, col_out, conf_out, spread):
    order, crow = get(0), get(1)
    elements = order.shape[1]
    slots = peers * row_cap
    place, slot = row_places(crow, peers, elements, row_cap)
    take = onehot_rows(place, slots)
    order_col = column(take, order.astype(jnp.float32))
    elem_col = column(take, iota((1, elements), 1).astype(jnp.float32) + 1.0)
    lane = iota((slots, 128), 1)
    slot_col = column(take, slot + 1.0)
    col_out[...] = jnp.where(lane == 0, order_col, jnp.where(lane == 1, elem_col, slot_col))
    take = take.astype(jnp.bfloat16)
    spread[...] = jnp.zeros_like(spread)
    for half, part in enumerate(halves(get(2))):
        moved = dot(take, part)
        for v in range(VARS):
            spread[half, v * slots : (v + 1) * slots, :CELL] = moved[:, v * CELL : (v + 1) * CELL]
    order_rows = jnp.concatenate([order_col] * VARS, axis=0)
    high, low = spread[0], spread[1]
    wide_high = jnp.concatenate([jnp.where(order_rows == float(p), high, 0.0).astype(jnp.bfloat16) for p in ORDERS], axis=1)
    wide_low = jnp.concatenate([jnp.where(order_rows == float(p), low, 0.0).astype(jnp.bfloat16) for p in ORDERS], axis=1)
    conf_out[...] = conf[...]
    y_out[...] = dot3(wide_high, wide_low, get(3), get(4))


def face_kernel(peers, row_cap, elements, groups, get, incoming, conf, y, cols, table_high, table_low, out, spread):
    slots = peers * row_cap
    message = incoming[...].reshape(slots, incoming.shape[2])
    x = jnp.concatenate([*[message[:, g * STEP : (g + 1) * STEP] for g in range(groups)], conf[...]], axis=0)
    code_col = x[:, TAG_FACE : TAG_FACE + 1]
    count = x.shape[0]
    code_row = jnp.sum(jnp.where(iota((count, count), 0) == iota((count, count), 1), code_col, 0.0), axis=0, keepdims=True)
    order_col, elem_col = cols[:, 0:1], cols[:, 1:2]
    wanted = jnp.concatenate([jnp.where(elem_col > 0.0, elem_col + float(f * elements), -1.0) for f in range(FACES)], axis=0)
    gather = (wanted == code_row).astype(jnp.bfloat16)
    high, low = halves(x)
    face_sum = dot(gather, high) + dot(gather, low)
    spread[...] = jnp.zeros_like(spread)
    for f in range(FACES):
        for v in range(VARS):
            spread[v * slots : (v + 1) * slots, f * FACE_PAD : f * FACE_PAD + FLAT] = face_sum[
                f * slots : (f + 1) * slots, v * FLAT : (v + 1) * FLAT
            ]
    order_rows = jnp.concatenate([order_col] * VARS, axis=0)
    z = spread[...]
    wide = jnp.concatenate([jnp.where(order_rows == float(p), z, 0.0) for p in ORDERS], axis=1)
    high, low = halves(wide)
    total = y[...] + dot3(high, low, table_high[...], table_low[...])
    for v in range(VARS):
        out[:, :, v * ROW : (v + 1) * ROW] = total[v * slots : (v + 1) * slots].reshape(peers, row_cap, ROW)
    out[:, :, TAG_SLOT : TAG_SLOT + 1] = cols[:, 2:3].reshape(peers, row_cap, 1)


def place_kernel(peers, row_cap, get, arrived, out, placed, sent):
    elements = out.shape[0]
    rows = peers * row_cap
    message = arrived[...].reshape(rows, arrived.shape[2])
    slot_col = message[:, TAG_SLOT : TAG_SLOT + 1]
    slot_row = jnp.sum(jnp.where(iota((rows, rows), 0) == iota((rows, rows), 1), slot_col, 0.0), axis=0, keepdims=True)
    put = (iota((elements, rows), 0).astype(jnp.float32) + 1.0 == slot_row).astype(jnp.bfloat16)
    sends = []
    for half, (first, last) in enumerate(((0, PLACE_SPLIT), (PLACE_SPLIT, TAG_SLOT))):
        high, low = halves(message[:, first:last])
        placed[:, first:last] = dot(put, high) + dot(put, low)
        lanes = pl.ds(first, last - first)
        send = pltpu.make_async_copy(placed.at[:, lanes], out.at[:, lanes], sent.at[half])
        send.start()
        sends.append(send)
    for send in sends:
        send.wait()


def fetched(kernel, n_far, n_pass, n_near, n_out, *refs):
    far, near, outs = refs[:n_far], refs[n_far : n_far + n_near], refs[n_far + n_near : n_far + n_near + n_out]
    rest = refs[n_far + n_near + n_out :]
    n_held = n_far - n_pass
    held, sems, scratch = rest[:n_held], rest[n_held], rest[n_held + 1 :]
    held = (*held, *outs[n_out - n_pass :])
    copies = [pltpu.make_async_copy(src, dst, sems.at[i]) for i, (src, dst) in enumerate(zip(far, held))]
    for copy in copies:
        copy.start()

    def get(i):
        copies[i].wait()
        return held[i][...]

    kernel(get, *near, *outs[: n_out - n_pass], *scratch)
    for copy in copies[n_held:]:
        copy.wait()


def like(a):
    return jax.ShapeDtypeStruct(a.shape, a.dtype)


def call(kernel, outs, far, near=(), scratch=(), hand_on=(), flops=0):
    outs = [*outs, *[like(a) for a in hand_on]]
    out_specs = [pl.BlockSpec(memory_space=getattr(a, "memory_space", None) or pltpu.VMEM) for a in outs]
    sizes = [np.prod(a.shape) * a.dtype.itemsize for a in (*far, *near, *outs)]
    held = [pltpu.VMEM(a.shape, a.dtype) for a in far]
    far = (*far, *hand_on)
    in_specs = [pl.BlockSpec(memory_space=pltpu.HBM)] * len(far) + [pl.BlockSpec(memory_space=pltpu.VMEM)] * len(near)
    return pl.pallas_call(
        functools.partial(fetched, kernel, len(far), len(hand_on), len(near), len(outs)),
        in_specs=in_specs,
        out_specs=out_specs,
        out_shape=outs,
        scratch_shapes=[*held, pltpu.SemaphoreType.DMA((max(1, len(far)),)), *scratch],
        compiler_params=pltpu.CompilerParams(vmem_limit_bytes=48 * 1024 * 1024),
        cost_estimate=pl.CostEstimate(flops=flops, bytes_accessed=int(sum(sizes)), transcendentals=0),
    )(*[pltpu.with_memory_space_constraint(a, pltpu.HBM) for a in far], *near)


def exchange(block):
    return lax.all_to_all(block, ("gy", "gx"), split_axis=0, concat_axis=0, tiled=True)


def from_behind(block, axis, distance):
    devices = range(lax.axis_size(axis))
    route = [((i - distance) % len(devices), i) for i in devices]
    return lax.ppermute(block, axis, route)


def body(
    adjoint,
    order,
    mortar_trace,
    mortar_sub,
    mortar_dest,
    mortar_elem,
    mortar_face,
    conf_trace,
    conf_elem,
    conf_face,
    coarse_row,
):
    elements = adjoint.shape[0]
    count = mortar_trace.shape[0]
    confs = conf_trace.shape[0]
    peers = lax.axis_size("gx") * lax.axis_size("gy")
    cap = max(2, 2 * count // peers)
    row_cap = max(2, elements // peers)
    slots = peers * row_cap
    groups = -(-cap // row_cap)
    lanes = groups * STEP
    lift, cell, face = jax.tree.map(jnp.asarray, basis_tables())
    f32 = jnp.float32
    line = lambda a: a.reshape(1, -1)
    order, coarse_row = line(order), line(coarse_row)
    message = (peers, row_cap, lanes)
    outgoing, conf = call(
        functools.partial(pack_kernel, peers, cap, row_cap, elements),
        [pltpu.HBM(message, f32), jax.ShapeDtypeStruct((confs, STEP), f32)],
        (
            line(mortar_dest),
            line(mortar_sub),
            mortar_trace,
            lift,
            line(mortar_elem),
            line(mortar_face),
            line(conf_face),
            line(conf_elem),
            conf_trace,
        ),
        scratch=[pltpu.VMEM(message, f32), pltpu.SemaphoreType.DMA((2,))],
    )
    incoming = exchange(outgoing)
    y, cols, conf, *face = call(
        functools.partial(cell_kernel, peers, row_cap),
        [
            jax.ShapeDtypeStruct((VARS * slots, ROW), f32),
            jax.ShapeDtypeStruct((slots, 128), f32),
            jax.ShapeDtypeStruct(conf.shape, f32),
        ],
        (order, coarse_row, adjoint, *cell),
        (conf,),
        scratch=[pltpu.VMEM((2, VARS * slots, CELL_PAD), f32)],
        hand_on=face,
    )
    conf = from_behind(conf, "gz", 1)
    (rows,) = call(
        functools.partial(face_kernel, peers, row_cap, elements, groups),
        [jax.ShapeDtypeStruct((peers, row_cap, ROWS_PAD), f32)],
        (),
        (incoming, conf, y, cols, *face),
        scratch=[pltpu.VMEM((VARS * slots, FACES_PAD), f32)],
    )
    (out,) = call(
        functools.partial(place_kernel, peers, row_cap),
        [pltpu.HBM((elements, VARS * ROW), f32)],
        (),
        (exchange(rows),),
        scratch=[pltpu.VMEM((elements, VARS * ROW), f32), pltpu.SemaphoreType.DMA((2,))],
    )
    return out


def solution(mesh):
    rows = P(("gx", "gy", "gz"))
    wide = P(("gx", "gy", "gz"), None)
    return jax.shard_map(
        body,
        mesh=mesh,
        in_specs=(wide, rows, wide, rows, wide, rows, rows, wide, rows, rows, rows),
        out_specs=wide,
        check_vma=False,
    )
```

```python
import functools

import jax
import jax.numpy as jnp
import ml_dtypes
import numpy as np
from jax import lax
from jax.experimental import pallas as pl
from jax.experimental.pallas import tpu as pltpu
from jax.sharding import PartitionSpec as P

VARS = 5
NODE = 7
FACE = NODE * NODE
CELL = NODE * FACE
ROW = 216
FACES = 6
ORDERS = (2, 3, 4, 5, 6)
TRACE = VARS * FACE
SUB_STEP = 64
FLAT = 36
SENT = VARS * FLAT
STEP = 192
TAG_FACE = SENT
ROWS_PAD = 1152
TAG_SLOT = VARS * ROW
CELL_PAD = 384
FACE_PAD = 40
FACES_PAD = 256


def grid_nodes(degree):
    return -np.cos(np.pi * np.arange(degree + 1) / degree)


def lagrange_rows(degree, points):
    anchors = grid_nodes(degree)
    values = np.ones((len(points), degree + 1))
    for k in range(degree + 1):
        for other in range(degree + 1):
            if other != k:
                values[:, k] *= (points - anchors[other]) / (anchors[k] - anchors[other])
    return values


def split_table(table):
    table = np.asarray(table, np.float32)
    high = table.astype(ml_dtypes.bfloat16)
    low = (table - high.astype(np.float32)).astype(ml_dtypes.bfloat16)
    return high, low


@functools.lru_cache(maxsize=None)
def basis_tables():
    top_nodes = grid_nodes(6)
    mortar = [lagrange_rows(6, (top_nodes - 1.0) / 2.0), lagrange_rows(6, (top_nodes + 1.0) / 2.0)]
    flat = lagrange_rows(5, top_nodes)
    lift = np.zeros((SUB_STEP, 6 * SUB_STEP))
    for sub in range(5):
        both = (mortar[sub // 2] @ flat, mortar[sub % 2] @ flat) if sub < 4 else (flat, flat)
        lift[:FACE, sub * SUB_STEP : sub * SUB_STEP + FLAT] = np.kron(*both)
    cell = np.zeros((len(ORDERS), CELL_PAD, ROW))
    face = np.zeros((len(ORDERS), FACES_PAD, ROW))
    for index, p in enumerate(ORDERS):
        shrink = np.zeros((6, NODE))
        shrink[:p, : p + 1] = lagrange_rows(p - 1, grid_nodes(p)).T
        cell[index, :CELL] = np.einsum("ai,bj,ck->ijkabc", shrink, shrink, shrink).reshape(CELL, ROW)
        lower = np.zeros((6, 6))
        lower[:p] = lagrange_rows(p - 1, grid_nodes(5)).T
        low, high = shrink[:, 0], shrink[:, p]
        for axis, spec in enumerate(("c,ai,bj->ijcab", "c,ai,bj->ijacb", "c,ai,bj->ijabc")):
            for side, edge in enumerate((low, high)):
                first = (2 * axis + side) * FACE_PAD
                face[index, first : first + FLAT] = np.einsum(spec, edge, lower, lower).reshape(FLAT, ROW)
    return (
        np.concatenate(split_table(lift)),
        split_table(cell.reshape(-1, ROW)),
        split_table(face.reshape(-1, ROW)),
    )


def iota(shape, axis):
    return lax.broadcasted_iota(jnp.int32, shape, axis)


def halves(x):
    high = x.astype(jnp.bfloat16)
    low = (x - high.astype(jnp.float32)).astype(jnp.bfloat16)
    return high, low


def dot(a, b):
    return jnp.dot(a, b, preferred_element_type=jnp.float32)


def dot3(high, low, table_high, table_low):
    return dot(high, table_high) + dot(low, table_high) + dot(high, table_low)


def earlier(member):
    count = member.shape[1]
    before = (iota((count, count), 0) < iota((count, count), 1)).astype(jnp.float32)
    return dot(member.astype(jnp.bfloat16), before.astype(jnp.bfloat16))


def device_of(shape):
    size_x, size_y = lax.axis_size("gx"), lax.axis_size("gy")
    rank = iota(shape, 0)
    return rank % size_x * size_y + rank // size_x


def owner_of(crow, peers, elements):
    first = device_of((peers, crow.shape[1])) * elements
    return ((crow >= first) & (crow < first + elements)).astype(jnp.float32)


def row_places(crow, peers, elements, stride):
    member = owner_of(crow, peers, elements)
    rank = earlier(member)
    block = iota(member.shape, 0).astype(jnp.float32)
    place = jnp.sum(member * (block * stride + rank), axis=0, keepdims=True)
    owned = (device_of(member.shape) * elements).astype(jnp.float32)
    slot = crow.astype(jnp.float32) - jnp.sum(member * owned, axis=0, keepdims=True)
    return place, slot


def onehot_rows(place, rows):
    return (iota((rows, place.shape[1]), 0).astype(jnp.float32) == place).astype(jnp.float32)


def column(onehot, values):
    return jnp.sum(onehot * values, axis=1, keepdims=True)


def pad_lanes(x, lanes):
    return jnp.concatenate([x, jnp.zeros((x.shape[0], lanes - x.shape[1]), x.dtype)], axis=1)


def stacked(trace):
    wide = pad_lanes(trace, TRACE - FACE + SUB_STEP)
    return jnp.concatenate([wide[:, v * FACE : v * FACE + SUB_STEP] for v in range(VARS)], axis=0)


def side_by_side(products):
    count = products.shape[0] // VARS
    parts = [products[v * count : (v + 1) * count, :FLAT] for v in range(VARS)]
    return jnp.concatenate([*parts, jnp.zeros((count, STEP - SENT), jnp.float32)], axis=1)


def restrict_cells(take, order_col, adjoint, table_high, table_low, spread):
    slots = take.shape[0]
    take = take.astype(jnp.bfloat16)
    spread[...] = jnp.zeros_like(spread)
    for half, part in enumerate(halves(adjoint)):
        moved = dot(take, part)
        for v in range(VARS):
            spread[half, v * slots : (v + 1) * slots, :CELL] = moved[:, v * CELL : (v + 1) * CELL]
    order_rows = jnp.concatenate([order_col] * VARS, axis=0)
    wide = [
        jnp.concatenate([jnp.where(order_rows == float(p), spread[half], 0.0).astype(jnp.bfloat16) for p in ORDERS], axis=1)
        for half in range(2)
    ]
    return dot3(*wide, table_high, table_low)


def pack_kernel(peers, cap, row_cap, elements, get, out, conf_out, y_out, message, sent, spread):
    dest, sub = get(0), get(1)
    count = dest.shape[1]
    groups, slots = -(-cap // row_cap), peers * row_cap
    member = (device_of((peers, count)) == dest).astype(jnp.float32)
    block = jnp.sum(member * iota(member.shape, 0).astype(jnp.float32), axis=0, keepdims=True)
    rank = jnp.sum(member * earlier(member), axis=0, keepdims=True)
    group = sum([(rank >= float(g * row_cap)).astype(jnp.float32) for g in range(1, groups)], jnp.zeros_like(rank))
    place = group * float(slots - row_cap) + block * float(row_cap) + rank
    put = onehot_rows(place, groups * slots)
    eye = (iota((count, count), 0) == iota((count, count), 1)).astype(jnp.float32)
    sub_col = column(eye, sub.astype(jnp.float32))
    subs = jnp.concatenate([sub_col] * VARS, axis=0)
    tables = get(3)
    table_high, table_low = tables[:SUB_STEP], tables[SUB_STEP:]
    split = 4 * SUB_STEP
    lifts = dot3(*halves(stacked(get(2))), table_high[:, :split], table_low[:, :split])
    lifts = jnp.where(subs < 2.0, lifts[:, : 2 * SUB_STEP], lifts[:, 2 * SUB_STEP :])
    odd = (subs == 1.0) | (subs == 3.0)
    lifted = side_by_side(jnp.where(odd, lifts[:, SUB_STEP:], lifts[:, :SUB_STEP]))
    lifted_high, lifted_low = halves(lifted)
    code_col = column(put, (get(5) * elements + get(4) + 1).astype(jnp.float32))
    put = put.astype(jnp.bfloat16)
    packed = dot(put, lifted_high) + dot(put, lifted_low)
    packed = jnp.where(iota(packed.shape, 1) == TAG_FACE, code_col, packed)
    bounds = (0, groups // 2 // 2 * 2, groups)
    sends = []
    for half, (first, last) in enumerate(zip(bounds[:-1], bounds[1:])):
        if first == last:
            continue
        for g in range(first, last):
            message[:, :, g * STEP : (g + 1) * STEP] = packed[g * slots : (g + 1) * slots].reshape(peers, row_cap, STEP)
        lanes = pl.ds(first * STEP, (last - first) * STEP)
        send = pltpu.make_async_copy(message.at[:, :, lanes], out.at[:, :, lanes], sent.at[half])
        send.start()
        sends.append(send)
    cface, celem = get(6), get(7)
    confs = cface.shape[1]
    eye = (iota((confs, confs), 0) == iota((confs, confs), 1)).astype(jnp.float32)
    conf_col = column(eye, (cface * elements + celem + 1).astype(jnp.float32))
    conf = side_by_side(dot3(*halves(stacked(get(8))), table_high[:, split:], table_low[:, split:]))
    conf_out[...] = jnp.where(iota(conf.shape, 1) == TAG_FACE, conf_col, conf)
    order, crow, adjoint, table_high, table_low = [get(i) for i in range(9, 14)]

    @pl.when(lax.axis_index("gz") % 2 == 0)
    def _():
        take = onehot_rows(row_places(crow, peers, elements, row_cap)[0], slots)
        order_col = column(take, order.astype(jnp.float32))
        y_out[...] = restrict_cells(take, order_col, adjoint, table_high, table_low, spread)

    for send in sends:
        send.wait()


def cell_kernel(peers, row_cap, get, y_early, y_out, col_out, spread):
    order, crow = get(0), get(1)
    elements = order.shape[1]
    slots = peers * row_cap
    place, slot = row_places(crow, peers, elements, row_cap)
    take = onehot_rows(place, slots)
    order_col = column(take, order.astype(jnp.float32))
    elem_col = column(take, iota((1, elements), 1).astype(jnp.float32) + 1.0)
    lane = iota((slots, 128), 1)
    slot_col = column(take, slot + 1.0)
    col_out[...] = jnp.where(lane == 0, order_col, jnp.where(lane == 1, elem_col, slot_col))
    adjoint, table_high, table_low = get(2), get(3), get(4)
    early = lax.axis_index("gz") % 2 == 0

    @pl.when(early)
    def _():
        y_out[...] = y_early[...]

    @pl.when(jnp.logical_not(early))
    def _():
        y_out[...] = restrict_cells(take, order_col, adjoint, table_high, table_low, spread)


def face_kernel(peers, row_cap, elements, groups, get, incoming, conf, y, cols, table_high, table_low, out, spread):
    slots = peers * row_cap
    message = incoming[...].reshape(slots, incoming.shape[2])
    x = jnp.concatenate([*[message[:, g * STEP : (g + 1) * STEP] for g in range(groups)], conf[...]], axis=0)
    code_col = x[:, TAG_FACE : TAG_FACE + 1]
    count = x.shape[0]
    code_row = jnp.sum(jnp.where(iota((count, count), 0) == iota((count, count), 1), code_col, 0.0), axis=0, keepdims=True)
    order_col, elem_col = cols[:, 0:1], cols[:, 1:2]
    wanted = jnp.concatenate([jnp.where(elem_col > 0.0, elem_col + float(f * elements), -1.0) for f in range(FACES)], axis=0)
    gather = (wanted == code_row).astype(jnp.bfloat16)
    high, low = halves(x)
    face_sum = dot(gather, high) + dot(gather, low)
    spread[...] = jnp.zeros_like(spread)
    for f in range(FACES):
        for v in range(VARS):
            spread[v * slots : (v + 1) * slots, f * FACE_PAD : f * FACE_PAD + FLAT] = face_sum[
                f * slots : (f + 1) * slots, v * FLAT : (v + 1) * FLAT
            ]
    order_rows = jnp.concatenate([order_col] * VARS, axis=0)
    z = spread[...]
    wide = jnp.concatenate([jnp.where(order_rows == float(p), z, 0.0) for p in ORDERS], axis=1)
    high, low = halves(wide)
    total = y[...] + dot3(high, low, table_high[...], table_low[...])
    for v in range(VARS):
        out[:, :, v * ROW : (v + 1) * ROW] = total[v * slots : (v + 1) * slots].reshape(peers, row_cap, ROW)
    out[:, :, TAG_SLOT : TAG_SLOT + 1] = cols[:, 2:3].reshape(peers, row_cap, 1)


def place_kernel(peers, row_cap, get, arrived, out):
    elements = out.shape[0]
    rows = peers * row_cap
    message = arrived[...].reshape(rows, arrived.shape[2])
    x, slot_col = message[:, :TAG_SLOT], message[:, TAG_SLOT : TAG_SLOT + 1]
    slot_row = jnp.sum(jnp.where(iota((rows, rows), 0) == iota((rows, rows), 1), slot_col, 0.0), axis=0, keepdims=True)
    put = (iota((elements, rows), 0).astype(jnp.float32) + 1.0 == slot_row).astype(jnp.bfloat16)
    high, low = halves(x)
    out[...] = dot(put, high) + dot(put, low)


def fetched(kernel, n_far, n_pass, n_near, n_out, *refs):
    far, near, outs = refs[:n_far], refs[n_far : n_far + n_near], refs[n_far + n_near : n_far + n_near + n_out]
    rest = refs[n_far + n_near + n_out :]
    n_held = n_far - n_pass
    held, sems, scratch = rest[:n_held], rest[n_held], rest[n_held + 1 :]
    held = (*held, *outs[n_out - n_pass :])
    copies = [pltpu.make_async_copy(src, dst, sems.at[i]) for i, (src, dst) in enumerate(zip(far, held))]
    for copy in copies:
        copy.start()

    def get(i):
        copies[i].wait()
        return held[i][...]

    kernel(get, *near, *outs[: n_out - n_pass], *scratch)
    for copy in copies[n_held:]:
        copy.wait()


def like(a):
    return jax.ShapeDtypeStruct(a.shape, a.dtype)


def call(kernel, outs, far, near=(), scratch=(), hand_on=(), flops=0):
    outs = [*outs, *[like(a) for a in hand_on]]
    out_specs = [pl.BlockSpec(memory_space=getattr(a, "memory_space", None) or pltpu.VMEM) for a in outs]
    sizes = [np.prod(a.shape) * a.dtype.itemsize for a in (*far, *near, *outs)]
    held = [pltpu.VMEM(a.shape, a.dtype) for a in far]
    far = (*far, *hand_on)
    in_specs = [pl.BlockSpec(memory_space=pltpu.HBM)] * len(far) + [pl.BlockSpec(memory_space=pltpu.VMEM)] * len(near)
    return pl.pallas_call(
        functools.partial(fetched, kernel, len(far), len(hand_on), len(near), len(outs)),
        in_specs=in_specs,
        out_specs=out_specs,
        out_shape=outs,
        scratch_shapes=[*held, pltpu.SemaphoreType.DMA((max(1, len(far)),)), *scratch],
        compiler_params=pltpu.CompilerParams(vmem_limit_bytes=48 * 1024 * 1024),
        cost_estimate=pl.CostEstimate(flops=flops, bytes_accessed=int(sum(sizes)), transcendentals=0),
    )(*[pltpu.with_memory_space_constraint(a, pltpu.HBM) for a in far], *near)


def exchange(block):
    return lax.all_to_all(block, ("gy", "gx"), split_axis=0, concat_axis=0, tiled=True)


def from_behind(block, axis, distance):
    devices = range(lax.axis_size(axis))
    route = [((i - distance) % len(devices), i) for i in devices]
    return lax.ppermute(block, axis, route)


def body(
    adjoint,
    order,
    mortar_trace,
    mortar_sub,
    mortar_dest,
    mortar_elem,
    mortar_face,
    conf_trace,
    conf_elem,
    conf_face,
    coarse_row,
):
    elements = adjoint.shape[0]
    count = mortar_trace.shape[0]
    confs = conf_trace.shape[0]
    peers = lax.axis_size("gx") * lax.axis_size("gy")
    cap = max(2, 2 * count // peers)
    row_cap = max(2, elements // peers)
    slots = peers * row_cap
    groups = -(-cap // row_cap)
    lanes = groups * STEP
    lift, cell, face = jax.tree.map(jnp.asarray, basis_tables())
    f32 = jnp.float32
    line = lambda a: a.reshape(1, -1)
    order, coarse_row = line(order), line(coarse_row)
    message = (peers, row_cap, lanes)
    outgoing, conf, y = call(
        functools.partial(pack_kernel, peers, cap, row_cap, elements),
        [
            pltpu.HBM(message, f32),
            jax.ShapeDtypeStruct((confs, STEP), f32),
            jax.ShapeDtypeStruct((VARS * slots, ROW), f32),
        ],
        (
            line(mortar_dest),
            line(mortar_sub),
            mortar_trace,
            lift,
            line(mortar_elem),
            line(mortar_face),
            line(conf_face),
            line(conf_elem),
            conf_trace,
            order,
            coarse_row,
            adjoint,
            *cell,
        ),
        scratch=[
            pltpu.VMEM(message, f32),
            pltpu.SemaphoreType.DMA((2,)),
            pltpu.VMEM((2, VARS * slots, CELL_PAD), f32),
        ],
    )
    incoming = exchange(outgoing)
    conf = from_behind(conf, "gz", 1)
    y, cols, *face = call(
        functools.partial(cell_kernel, peers, row_cap),
        [jax.ShapeDtypeStruct((VARS * slots, ROW), f32), jax.ShapeDtypeStruct((slots, 128), f32)],
        (order, coarse_row, adjoint, *cell),
        (y,),
        scratch=[pltpu.VMEM((2, VARS * slots, CELL_PAD), f32)],
        hand_on=face,
    )
    (rows,) = call(
        functools.partial(face_kernel, peers, row_cap, elements, groups),
        [jax.ShapeDtypeStruct((peers, row_cap, ROWS_PAD), f32)],
        (),
        (incoming, conf, y, cols, *face),
        scratch=[pltpu.VMEM((VARS * slots, FACES_PAD), f32)],
    )
    (out,) = call(
        functools.partial(place_kernel, peers, row_cap),
        [jax.ShapeDtypeStruct((elements, VARS * ROW), f32)],
        (),
        (exchange(rows),),
    )
    return out


def solution(mesh):
    rows = P(("gx", "gy", "gz"))
    wide = P(("gx", "gy", "gz"), None)
    return jax.shard_map(
        body,
        mesh=mesh,
        in_specs=(wide, rows, wide, rows, wide, rows, rows, wide, rows, rows, rows),
        out_specs=wide,
        check_vma=False,
    )
```
